128 devices in a mesh: row: 8 (over z, core), col: 16 (over x, y).
Axes of the slice: x: 4, y: 4, z: 4, core: 2. Of those that a mesh axis runs over, the one named last changes fastest.
Arguments:
- loads: float32 [4, 8, 8, 8, 65536], P(None, None, None, None, ('row', 'col')), may hold values from -5 to 8
- conduct: float32 [8, 8, 8, 65536], P(None, None, None, ('row', 'col')), may hold values from 0.1 to 10
Outputs:
- solution: float32 [4, 8, 8, 8, 65536], P(None, None, None, None, ('row', 'col'))
- residual: float32 [4, 8, 8, 8, 65536], P(None, None, None, None, ('row', 'col'))
- direction: float32 [4, 8, 8, 8, 65536], P(None, None, None, None, ('row', 'col'))
The draws below stay inside these ranges and needn't reach their ends.
All inputs are finite; a program needn't handle non-finite values.
Results may differ from the reference program's by a relative error of at most 0.00009.
Values sent between devices are 32-bit elements; how exact they have to be, the bound alone decides.
A program may use at most 128 MiB of HBM per device.

```python
import math
import jax
import jax.numpy as jnp
import numpy as np
from jax import lax

NODES = 8
BLOCK_X = 2
BLOCK_Y = 2
BLOCK_Z = 128
SOURCES = 4
E_DEV = 512
PEERS = 128
ELEMS = 65536
N_ROW = 8
N_COL = 16


def draw_loads(key, part):
    key = jax.random.fold_in(key, 3)
    shape = (SOURCES, NODES, NODES, NODES, ELEMS)
    owners = jnp.arange(ELEMS, dtype=jnp.int32) // E_DEV
    offset = owners.astype(jnp.float32) / (PEERS - 1)
    rough = jnp.clip(jax.random.normal(key, shape, jnp.float32), -5.0, 5.0)
    values = rough + 3.0 * offset
    return values.astype(jnp.float32)


def block_levels(key, dims, shards, smallest, high):
    level, own = 1.0, jax.random.fold_in(key, 6)
    for axis_at, parts in shards:
        draws = jnp.exp(jax.random.uniform(jax.random.fold_in(own, axis_at), (parts,), jnp.float32, smallest / len(shards), high / len(shards)))
        level = level * jnp.repeat(draws, dims[axis_at] // parts).reshape([-1 if axis == axis_at else 1 for axis in range(len(dims))])
    return level


def setup_inputs(seed: int = 0) -> dict:
    seeds = jax.random.split(jax.random.key(seed), 3)
    loads = draw_loads(jax.random.fold_in(seeds[2], 71), 0)
    conduct = jnp.clip(jnp.exp(math.log(10.0) - 4.6051702 * jax.random.uniform(seeds[1], (NODES, NODES, NODES, ELEMS), jnp.float32) ** block_levels(seeds[1], (NODES, NODES, NODES, ELEMS), ((3, 128),), -0.2, 0.2)), 0.1, 10.0)
    return dict(loads=loads, conduct=conduct)


SCREENING = 0.5
GLL_INNER = [-0.8717401485096066, -0.5917001814331423, -0.2092992179024789, 0.2092992179024789, 0.5917001814331423, 0.8717401485096066]


def gll_tables(dtype):
    degree = NODES - 1
    points = np.array([-1.0] + GLL_INNER + [1.0])
    previous = points * 0.0 + 1.0
    current = points * 1.0
    for order in range(1, degree):
        following = ((2 * order + 1) * points * current - order * previous) / (order + 1)
        previous = current
        current = following
    values = current
    weights = 2.0 / (degree * (degree + 1) * values ** 2)
    spread = points[:, None] - points[None, :]
    index_ids = np.arange(NODES)
    same = index_ids[:, None] == index_ids[None, :]
    safe_spread = np.where(same, 1.0, spread)
    deriv = np.where(same, 0.0, values[:, None] / (values[None, :] * safe_spread))
    corner = degree * (degree + 1) / 4.0
    ends = np.where(index_ids == 0, -corner, np.where(index_ids == degree, corner, 0.0))
    deriv = deriv + np.where(same, ends[None, :], 0.0)
    return jnp.asarray(deriv, dtype), jnp.asarray(weights, dtype)


def stiffness(field, flux, deriv):
    highest = lax.Precision.HIGHEST
    grad_x = jnp.einsum('ai,sijke->sajke', deriv, field, precision=highest) * flux
    result = jnp.einsum('ai,sajke->sijke', deriv, grad_x, precision=highest)
    grad_y = jnp.einsum('bj,sijke->sibke', deriv, field, precision=highest) * flux
    result = result + jnp.einsum('bj,sibke->sijke', deriv, grad_y, precision=highest)
    grad_z = jnp.einsum('ck,sijke->sijce', deriv, field, precision=highest) * flux
    result = result + jnp.einsum('ck,sijce->sijke', deriv, grad_z, precision=highest)
    return result + SCREENING * flux * field


def diagonal_part(flux, deriv):
    highest = lax.Precision.HIGHEST
    square = deriv * deriv
    result = jnp.einsum('ai,ajke->ijke', square, flux, precision=highest)
    result = result + jnp.einsum('bj,ibke->ijke', square, flux, precision=highest)
    result = result + jnp.einsum('ck,ijce->ijke', square, flux, precision=highest)
    return result + SCREENING * flux


def local_sum(field, size_x, size_y, size_z):
    length = field.shape[-1]
    element = jnp.arange(length, dtype=jnp.int32)
    coord_x = element // (size_y * size_z)
    coord_y = (element // size_z) % size_y
    coord_z = element % size_z
    for node_axis, stride, follows, upper_end in ((1, size_y * size_z, coord_x, size_x), (2, size_z, coord_y, size_y), (3, 1, coord_z, size_z)):
        has_next = follows < upper_end - 1
        has_prev = follows > 0
        low_face = lax.slice_in_dim(field, 0, 1, axis=node_axis)
        high_face = lax.slice_in_dim(field, NODES - 1, NODES, axis=node_axis)
        middle = lax.slice_in_dim(field, 1, NODES - 1, axis=node_axis)
        zero_pad = jnp.zeros(low_face.shape[:-1] + (stride,), field.dtype)
        next_face = jnp.concatenate([low_face[..., stride:], zero_pad], -1)
        summed = high_face + jnp.where(has_next, next_face, jnp.zeros_like(next_face))
        behind = jnp.concatenate([zero_pad, summed[..., :-stride]], -1)
        low_face = jnp.where(has_prev, behind, low_face)
        high_face = jnp.where(has_next, summed, high_face)
        field = jnp.concatenate([low_face, middle, high_face], node_axis)
    return field


def to_global(field):
    channels = field.shape[0]
    shaped = field.reshape(channels, NODES, NODES, NODES, N_ROW, N_COL, BLOCK_X, BLOCK_Y, BLOCK_Z)
    shaped = jnp.transpose(shaped, (0, 1, 2, 3, 4, 6, 5, 7, 8))
    return shaped.reshape(channels, NODES, NODES, NODES, -1)


def to_parts(field):
    channels = field.shape[0]
    shaped = field.reshape(channels, NODES, NODES, NODES, N_ROW, BLOCK_X, N_COL, BLOCK_Y, BLOCK_Z)
    shaped = jnp.transpose(shaped, (0, 1, 2, 3, 4, 6, 5, 7, 8))
    return shaped.reshape(channels, NODES, NODES, NODES, -1)


def shared_sum(field):
    def one_channel(single):
        whole = to_global(single[None])
        summed = local_sum(whole, N_ROW * BLOCK_X, N_COL * BLOCK_Y, BLOCK_Z)
        return to_parts(summed)[0]
    return lax.map(one_channel, field)


def reference(loads, conduct):
    dtype = loads.dtype
    deriv, weights = gll_tables(dtype)
    cube = weights[:, None, None] * weights[None, :, None] * weights[None, None, :]
    flux = conduct * cube[..., None]
    diag_k = diagonal_part(flux, deriv)
    ones_field = jnp.ones((1, NODES, NODES, NODES, ELEMS), dtype)
    stacked = shared_sum(jnp.concatenate([loads, diag_k[None], ones_field], 0)).reshape(SOURCES + 2, -1)
    rhs = stacked[:SOURCES]
    diag_a = stacked[SOURCES]
    inverse_mult = 1.0 / stacked[SOURCES + 1]
    first_z = rhs / diag_a
    rz_first = jnp.sum(inverse_mult * rhs * first_z, axis=1)
    shape = (SOURCES, NODES, NODES, NODES, ELEMS)
    applied = lax.map(lambda single: stiffness(single[None], flux, deriv)[0], first_z.reshape(shape))
    image = shared_sum(applied).reshape(SOURCES, -1)
    curvature = jnp.sum(inverse_mult * first_z * image, axis=1)
    alpha = rz_first / curvature
    solution = alpha[:, None] * first_z
    residual = rhs - alpha[:, None] * image
    second_z = residual / diag_a
    rz_second = jnp.sum(inverse_mult * residual * second_z, axis=1)
    direction = second_z + (rz_second / rz_first)[:, None] * first_z
    return solution.reshape(shape), residual.reshape(shape), direction.reshape(shape)
```

```python
import functools

import jax
import jax.numpy as jnp
import numpy as np
from jax import lax
from jax.experimental import pallas as pl
from jax.experimental.pallas import tpu as pltpu
from jax.sharding import PartitionSpec as P

NODES = 8
SOURCES = 4
LANES = 128
N_ROW = 8
N_COL = 16
SCREENING = 0.5
GLL_INNER = [
    -0.8717401485096066,
    -0.5917001814331423,
    -0.2092992179024789,
    0.2092992179024789,
    0.5917001814331423,
    0.8717401485096066,
]
MESH = pl.DeviceIdType.MESH
FIELD = (2, 2, NODES, NODES, NODES, LANES)
ROWS = 4 * NODES**3


def gll_tables():
    degree = NODES - 1
    points = np.array([-1.0] + GLL_INNER + [1.0])
    previous = points * 0.0 + 1.0
    current = points * 1.0
    for order in range(1, degree):
        following = ((2 * order + 1) * points * current - order * previous) / (order + 1)
        previous = current
        current = following
    weights = 2.0 / (degree * (degree + 1) * current**2)
    spread = points[:, None] - points[None, :]
    index_ids = np.arange(NODES)
    same = index_ids[:, None] == index_ids[None, :]
    safe_spread = np.where(same, 1.0, spread)
    deriv = np.where(same, 0.0, current[:, None] / (current[None, :] * safe_spread))
    corner = degree * (degree + 1) / 4.0
    ends = np.where(index_ids == 0, -corner, np.where(index_ids == degree, corner, 0.0))
    deriv = deriv + np.where(same, ends[None, :], 0.0)
    return deriv, weights


DERIV, WEIGHTS = gll_tables()
SQUARE = DERIV * DERIV
HALF = NODES // 2


def halves(table):
    mirrored = table[:HALF, ::-1][:, :HALF]
    direct = table[:HALF, :HALF]
    plus = (direct + mirrored) / 2.0
    minus = (direct - mirrored) / 2.0
    return plus.tolist(), minus.tolist()


D_PLUS, D_MINUS = halves(DERIV)
Q_PLUS, Q_MINUS = halves(SQUARE)


def fold(values):
    plus = [values[i] + values[7 - i] for i in range(HALF)]
    minus = [values[i] - values[7 - i] for i in range(HALF)]
    return plus, minus


def combine(table, values, transposed):
    out = []
    for a in range(HALF):
        total = None
        for i in range(HALF):
            factor = table[i][a] if transposed else table[a][i]
            term = values[i] * factor
            total = term if total is None else total + term
        out.append(total)
    return out


def unfold(base, turn):
    low = [base[a] + turn[a] for a in range(HALF)]
    high = [base[a] - turn[a] for a in range(HALF)]
    return low + high[::-1]


def derive(values):
    plus, minus = fold(values)
    return unfold(combine(D_MINUS, minus, False), combine(D_PLUS, plus, False))


def derive_back(values):
    plus, minus = fold(values)
    return unfold(combine(D_PLUS, minus, True), combine(D_MINUS, plus, True))


def square_back(values):
    plus, minus = fold(values)
    return unfold(combine(Q_PLUS, plus, True), combine(Q_MINUS, minus, True))


def tile_rows(base):
    return pl.ds(pl.multiple_of(base, 8), 8)


def strided(base):
    return pl.ds(base, 8, stride=8)


def line_x(n):
    base = (n // 8) * 512 + (n % 8) * 8
    return [tile_rows(base + 64 * i) for i in range(NODES)]


def line_y(n):
    return [tile_rows(n * 64 + 8 * j) for j in range(NODES)]


def line_z(n):
    base = pl.multiple_of(n * 64, 64)
    return [strided(base + k) for k in range(NODES)]


def lane_ids():
    return lax.broadcasted_iota(jnp.int32, (8, LANES), 1)


def sum_z(first, last):
    lane = lane_ids()
    total = last + jnp.where(lane < LANES - 1, pltpu.roll(first, LANES - 1, 1), 0.0)
    return jnp.where(lane > 0, pltpu.roll(total, 1, 1), first), total


def solve_kernel(
    loads,
    conduct,
    rhs,
    image,
    inverse,
    scalars,
    flux,
    z0,
    weighted,
    from_x,
    from_y,
    from_edge,
    sums,
    part,
    gather_row,
    gather_col,
    in_sem,
    send_sem,
    recv_sem,
    sum_send,
    sum_recv,
):
    row = lax.axis_index("row")
    col = lax.axis_index("col")
    for ex in range(2):
        for ey in range(2):
            lanes = pl.ds((ex * 2 + ey) * LANES, LANES)
            pltpu.make_async_copy(
                conduct.at[:, :, :, lanes], flux.at[ex, ey], in_sem.at[SOURCES]
            ).start()
    for s in range(SOURCES):
        for ex in range(2):
            for ey in range(2):
                lanes = pl.ds((ex * 2 + ey) * LANES, LANES)
                pltpu.make_async_copy(
                    loads.at[s, :, :, :, lanes], rhs.at[s, ex, ey], in_sem.at[s]
                ).start()

    has_up, has_down = row < N_ROW - 1, row > 0
    has_right, has_left = col < N_COL - 1, col > 0
    ways = [
        (1, 0, has_up),
        (-1, 0, has_down),
        (0, 1, has_right),
        (0, -1, has_left),
        (1, 1, has_up & has_right),
        (1, -1, has_up & has_left),
        (-1, 1, has_down & has_right),
        (-1, -1, has_down & has_left),
    ]
    barrier = pltpu.get_barrier_semaphore()
    for step in range(1, N_ROW):
        pl.semaphore_signal(
            barrier, 1, device_id=(lax.rem(row + step, N_ROW), col), device_id_type=MESH
        )
    for step in range(1, N_COL):
        pl.semaphore_signal(
            barrier, 1, device_id=(row, lax.rem(col + step, N_COL)), device_id_type=MESH
        )
    corners = 0
    for dr, dc, there in ways[4:]:

        @pl.when(there)
        def _():
            pl.semaphore_signal(barrier, 1, device_id=(row + dr, col + dc), device_id_type=MESH)

        corners = corners + there.astype(jnp.int32)

    def transfers(q, ref):
        pieces = [
            (ref.at[1, :, 7], from_x.at[q, 0]),
            (ref.at[0, :, 0], from_x.at[q, 1]),
            (ref.at[:, 1, :, 7], from_y.at[q, 0]),
            (ref.at[:, 0, :, 0], from_y.at[q, 1]),
            (ref.at[1, 1, 7, 7], from_edge.at[q, 0]),
            (ref.at[1, 0, 7, 0], from_edge.at[q, 1]),
            (ref.at[0, 1, 0, 7], from_edge.at[q, 2]),
            (ref.at[0, 0, 0, 0], from_edge.at[q, 3]),
        ]
        return [
            pltpu.make_async_remote_copy(
                src,
                dst,
                send_sem.at[q, n],
                recv_sem.at[q, n],
                device_id=(row + ways[n][0], col + ways[n][1]),
                device_id_type=MESH,
            )
            for n, (src, dst) in enumerate(pieces)
        ]

    order = (2, 3, 0, 1, 4, 5, 6, 7)

    def send(q, ref):
        copies = transfers(q, ref)
        for n in order:

            @pl.when(ways[n][2])
            def _():
                copies[n].start()

    def finish(q, ref):
        copies = transfers(q, ref)
        for n in order:

            @pl.when(ways[n][2])
            def _():
                copies[n].wait_send()

        for n in order:

            @pl.when(ways[n ^ 1 if n < 4 else 11 - n][2])
            def _():
                copies[n].wait_recv()

    def clear(ref, there, pick):
        @pl.when(jnp.logical_not(there))
        def _():
            def body(q, carry):
                target = pick(ref, q)
                target[...] = jnp.zeros_like(target)
                return carry

            lax.fori_loop(0, 9, body, 0)

    clear(from_x, has_down, lambda ref, q: ref.at[q, 0])
    clear(from_x, has_up, lambda ref, q: ref.at[q, 1])
    clear(from_y, has_left, lambda ref, q: ref.at[q, 0])
    clear(from_y, has_right, lambda ref, q: ref.at[q, 1])
    clear(from_edge, has_down & has_left, lambda ref, q: ref.at[q, 0])
    clear(from_edge, has_down & has_right, lambda ref, q: ref.at[q, 1])
    clear(from_edge, has_up & has_left, lambda ref, q: ref.at[q, 2])
    clear(from_edge, has_up & has_right, lambda ref, q: ref.at[q, 3])
    sums[...] = jnp.zeros_like(sums)

    def assemble(q, ref):
        def along_x(j, carry):
            for ey in range(2):
                ref[0, ey, 0, j] = ref[0, ey, 0, j] + from_x[q, 0, ey, j]
                ref[1, ey, 7, j] = ref[1, ey, 7, j] + from_x[q, 1, ey, j]
                both = ref[0, ey, 7, j] + ref[1, ey, 0, j]
                ref[0, ey, 7, j] = both
                ref[1, ey, 0, j] = both
            return carry

        lax.fori_loop(0, NODES, along_x, 0, unroll=4)
        for side in range(2):
            from_y[q, side, 0, 0] = from_y[q, side, 0, 0] + from_edge[q, side]
            from_y[q, side, 1, 7] = from_y[q, side, 1, 7] + from_edge[q, 2 + side]
            both = from_y[q, side, 0, 7] + from_y[q, side, 1, 0]
            from_y[q, side, 0, 7] = both
            from_y[q, side, 1, 0] = both

        def along_y(i, carry):
            for ex in range(2):
                ref[ex, 0, i, 0] = ref[ex, 0, i, 0] + from_y[q, 0, ex, i]
                ref[ex, 1, i, 7] = ref[ex, 1, i, 7] + from_y[q, 1, ex, i]
                both = ref[ex, 0, i, 7] + ref[ex, 1, i, 0]
                ref[ex, 0, i, 7] = both
                ref[ex, 1, i, 0] = both
            return carry

        lax.fori_loop(0, NODES, along_y, 0, unroll=4)

    def along_z(flat):
        def body(n, carry):
            base = pl.multiple_of(n * 64, 64)
            first, last = sum_z(flat[strided(base), :], flat[strided(base + 7), :])
            flat[strided(base), :] = first
            flat[strided(base + 7), :] = last
            return carry

        lax.fori_loop(0, 32, body, 0, unroll=8)

    flux2 = flux.reshape(ROWS, LANES)
    inverse2 = inverse.reshape(ROWS, LANES)
    weighted2 = weighted.reshape(ROWS, LANES)
    z02 = z0.reshape(ROWS, LANES)

    pltpu.make_async_copy(flux, flux, in_sem.at[SOURCES]).wait()
    node = lax.broadcasted_iota(jnp.int32, (8, LANES), 0)
    weight_z = jnp.full((8, LANES), WEIGHTS[3], jnp.float32)
    for k in (0, 1, 2):
        ends = (node == k) | (node == 7 - k)
        weight_z = jnp.where(ends, jnp.float32(WEIGHTS[k]), weight_z)

    def weigh(t, carry):
        for i in range(NODES):
            for j in range(NODES):
                at = tile_rows(t * 512 + i * 64 + j * 8)
                flux2[at, :] = flux2[at, :] * (weight_z * float(WEIGHTS[i] * WEIGHTS[j]))
        return carry

    lax.fori_loop(0, 4, weigh, 0)

    def diag_x(n, carry):
        at = line_x(n)
        values = [flux2[a, :] for a in at]
        for a, v, r in zip(at, values, square_back(values)):
            inverse2[a, :] = r + SCREENING * v
        return carry

    def diag_y(n, carry):
        at = line_y(n)
        result = square_back([flux2[a, :] for a in at])
        for a, r in zip(at, result):
            inverse2[a, :] = inverse2[a, :] + r
        return carry

    def diag_z(n, carry):
        at = line_z(n)
        result = square_back([flux2[a, :] for a in at])
        for a, r in zip(at, result):
            inverse2[a, :] = inverse2[a, :] + r
        return carry

    lax.fori_loop(0, 32, diag_x, 0, unroll=2)
    lax.fori_loop(0, 32, diag_y, 0, unroll=2)
    lax.fori_loop(0, 32, diag_z, 0, unroll=2)

    pl.semaphore_wait(barrier, N_ROW - 1 + N_COL - 1 + corners)

    def arrive(s):
        pltpu.make_async_copy(rhs.at[s], rhs.at[s], in_sem.at[s]).wait()
        send(s, rhs.at[s])

    arrive(0)
    send(SOURCES, inverse)
    arrive(1)
    finish(SOURCES, inverse)
    assemble(SOURCES, inverse)
    along_z(inverse2)

    lane = lane_ids()
    twice_z = ((node == 0) & (lane > 0)) | ((node == 7) & (lane < LANES - 1))
    share_z = jnp.where(twice_z, jnp.float32(0.5), jnp.float32(1.0))

    def invert(n, carry):
        for j in range(NODES):
            at = tile_rows(n * 64 + 8 * j)
            value = 1.0 / inverse2[at, :]
            inverse2[at, :] = value
            weighted2[at, :] = value * share_z
        return carry

    lax.fori_loop(0, 32, invert, 0)
    shares = [
        (has_down, 0, 0),
        (None, 0, 7),
        (None, 1, 0),
        (has_up, 1, 7),
    ]
    for there, ex, i in shares:
        share = 0.5 if there is None else jnp.where(there, 0.5, 1.0).astype(jnp.float32)
        for ey in range(2):
            weighted[ex, ey, i] = weighted[ex, ey, i] * share
    shares = [
        (has_left, 0, 0),
        (None, 0, 7),
        (None, 1, 0),
        (has_right, 1, 7),
    ]
    for there, ey, j in shares:
        share = 0.5 if there is None else jnp.where(there, 0.5, 1.0).astype(jnp.float32)
        for ex in range(2):
            weighted[ex, ey, :, j] = weighted[ex, ey, :, j] * share

    zero = jnp.zeros((8, LANES), jnp.float32)

    def put_sum(at, value):
        sums[pl.ds(at, 1), :] = jnp.sum(value, axis=0, keepdims=True)

    def settle(s):
        finish(SOURCES + 1 + s, image.at[s])
        assemble(SOURCES + 1 + s, image.at[s])
        flat = image.at[s].reshape(ROWS, LANES)

        def body(n, carry):
            for j in range(NODES):
                at = tile_rows(n * 64 + 8 * j)
                value = flat[at, :]
                carry = carry + value * value * weighted2[at, :]
            return carry

        put_sum(8 + s, lax.fori_loop(0, 32, body, zero))

    def source(s, carry):
        finish(s, rhs.at[s])
        assemble(s, rhs.at[s])
        right = rhs.at[s].reshape(ROWS, LANES)
        flat = image.at[s].reshape(ROWS, LANES)
        along_z(right)

        def scale(n, carry):
            for j in range(NODES):
                at = tile_rows(n * 64 + 8 * j)
                value = right[at, :]
                z02[at, :] = value * inverse2[at, :]
                carry = carry + value * value * weighted2[at, :]
            return carry

        put_sum(s, lax.fori_loop(0, 32, scale, zero))

        def stiff(at):
            values = [z02[a, :] for a in at]
            weight = [flux2[a, :] for a in at]
            slopes = [g * w for g, w in zip(derive(values), weight)]
            return values, weight, derive_back(slopes)

        def stiff_x(n, carry):
            at = line_x(n)
            values, weight, result = stiff(at)
            for a, v, w, r in zip(at, values, weight, result):
                flat[a, :] = r + SCREENING * w * v
            return carry

        def stiff_y(n, carry):
            at = line_y(n)
            _, _, result = stiff(at)
            for a, r in zip(at, result):
                flat[a, :] = flat[a, :] + r
            return carry

        def stiff_z(n, carry):
            at = line_z(n)
            values, _, result = stiff(at)
            result = [flat[a, :] + r for a, r in zip(at, result)]
            for v, r in zip(values, result):
                carry = carry + v * r
            result[0], result[7] = sum_z(result[0], result[7])
            for a, r in zip(at, result):
                flat[a, :] = r
            return carry

        lax.fori_loop(0, 32, stiff_x, 0, unroll=2)
        lax.fori_loop(0, 32, stiff_y, 0, unroll=2)
        put_sum(4 + s, lax.fori_loop(0, 32, stiff_z, zero, unroll=2))
        send(SOURCES + 1 + s, image.at[s])

        @pl.when(s < SOURCES - 2)
        def _():
            arrive(s + 2)

        @pl.when(s > 0)
        def _():
            settle(s - 1)

        return carry

    lax.fori_loop(0, SOURCES, source, 0)
    settle(SOURCES - 1)

    def gather(stage, slots, mine, count, at, target):
        slots[at] = mine[...]
        copies = [
            pltpu.make_async_remote_copy(
                mine,
                slots.at[at],
                sum_send.at[stage],
                sum_recv.at[stage],
                device_id=target(lax.rem(at + step, count)),
                device_id_type=MESH,
            )
            for step in range(1, count)
        ]
        for copy in copies:
            copy.start()
        others = slots.at[pl.ds(0, count - 1)]
        pltpu.make_async_copy(others, others, sum_recv.at[stage]).wait()
        pltpu.make_async_copy(others, others, sum_send.at[stage]).wait()
        total = slots[0]
        for n in range(1, count):
            total = total + slots[n]
        return total

    part[...] = gather(0, gather_row, sums, N_ROW, row, lambda r: (r, col))
    total = gather(1, gather_col, part, N_COL, col, lambda c: (row, c))
    total = jnp.sum(total, axis=1, keepdims=True)
    rz_first, curvature, square = total[0:4], total[4:8], total[8:12]
    alpha = rz_first / curvature
    rz_second = alpha * alpha * square - rz_first
    beta = rz_second / rz_first
    scalars[0:4, :] = jnp.broadcast_to(alpha, (4, LANES))
    scalars[4:8, :] = jnp.broadcast_to(beta, (4, LANES))


def update_kernel(rhs, image, inverse, scalars, solution_out, residual_out, direction_out):
    s = pl.program_id(0)
    i = pl.program_id(1)
    alpha = jnp.broadcast_to(scalars[pl.ds(s, 1), :], (8, LANES))
    beta = jnp.broadcast_to(scalars[pl.ds(s + 4, 1), :], (8, LANES))
    for ex in range(2):
        for ey in range(2):
            lanes = pl.ds((ex * 2 + ey) * LANES, LANES)
            for j in range(NODES):
                right = rhs[s, ex, ey, i, j]
                inv = inverse[ex, ey, i, j]
                rest = right - alpha * image[s, ex, ey, i, j]
                solution_out[0, 0, j, :, lanes] = alpha * (right * inv)
                residual_out[0, 0, j, :, lanes] = rest
                direction_out[0, 0, j, :, lanes] = (rest + beta * right) * inv


def per_device(loads, conduct):
    f32 = jnp.float32
    vmem = pltpu.VMEM
    whole = pl.BlockSpec(memory_space=vmem)
    many = (SOURCES,) + FIELD
    rhs, image, inverse, scalars = pl.pallas_call(
        solve_kernel,
        out_shape=[vmem(many, f32), vmem(many, f32), vmem(FIELD, f32), vmem((8, LANES), f32)],
        in_specs=[pl.BlockSpec(memory_space=pl.ANY)] * 2,
        out_specs=[whole] * 4,
        scratch_shapes=[
            vmem(FIELD, f32),
            vmem(FIELD, f32),
            vmem(FIELD, f32),
            vmem((9, 2, 2, NODES, NODES, LANES), f32),
            vmem((9, 2, 2, NODES, NODES, LANES), f32),
            vmem((9, 4, NODES, LANES), f32),
            vmem((16, LANES), f32),
            vmem((16, LANES), f32),
            vmem((N_ROW, 16, LANES), f32),
            vmem((N_COL, 16, LANES), f32),
            pltpu.SemaphoreType.DMA((SOURCES + 1,)),
            pltpu.SemaphoreType.DMA((9, 8)),
            pltpu.SemaphoreType.DMA((9, 8)),
            pltpu.SemaphoreType.DMA((2,)),
            pltpu.SemaphoreType.DMA((2,)),
        ],
        compiler_params=pltpu.CompilerParams(
            collective_id=0, has_side_effects=True, vmem_limit_bytes=40 * 1024 * 1024
        ),
    )(loads, conduct)
    shape = (SOURCES, NODES, NODES, NODES, 4 * LANES)
    block = pl.BlockSpec((1, 1, NODES, NODES, 4 * LANES), lambda s, i: (s, i, 0, 0, 0))
    return pl.pallas_call(
        update_kernel,
        grid=(SOURCES, NODES),
        out_shape=[jax.ShapeDtypeStruct(shape, f32)] * 3,
        in_specs=[whole] * 4,
        out_specs=[block] * 3,
        compiler_params=pltpu.CompilerParams(vmem_limit_bytes=16 * 1024 * 1024),
    )(*[pltpu.with_memory_space_constraint(x, vmem) for x in (rhs, image, inverse, scalars)])


def solution(mesh):
    in_specs = (P(None, None, None, None, ("row", "col")), P(None, None, None, ("row", "col")))
    out = P(None, None, None, None, ("row", "col"))
    return jax.shard_map(
        per_device, mesh=mesh, in_specs=in_specs, out_specs=(out, out, out), check_vma=False
    )
```

```python
import functools

import jax
import jax.numpy as jnp
import numpy as np
from jax import lax
from jax.experimental import pallas as pl
from jax.experimental.pallas import tpu as pltpu
from jax.sharding import PartitionSpec as P

NODES = 8
SOURCES = 4
LANES = 128
N_ROW = 8
N_COL = 16
SCREENING = 0.5
GLL_INNER = [
    -0.8717401485096066,
    -0.5917001814331423,
    -0.2092992179024789,
    0.2092992179024789,
    0.5917001814331423,
    0.8717401485096066,
]
MESH = pl.DeviceIdType.MESH
FIELD = (2, 2, NODES, NODES, NODES, LANES)
ROWS = 4 * NODES**3


def gll_tables():
    degree = NODES - 1
    points = np.array([-1.0] + GLL_INNER + [1.0])
    previous = points * 0.0 + 1.0
    current = points * 1.0
    for order in range(1, degree):
        following = ((2 * order + 1) * points * current - order * previous) / (order + 1)
        previous = current
        current = following
    weights = 2.0 / (degree * (degree + 1) * current**2)
    spread = points[:, None] - points[None, :]
    index_ids = np.arange(NODES)
    same = index_ids[:, None] == index_ids[None, :]
    safe_spread = np.where(same, 1.0, spread)
    deriv = np.where(same, 0.0, current[:, None] / (current[None, :] * safe_spread))
    corner = degree * (degree + 1) / 4.0
    ends = np.where(index_ids == 0, -corner, np.where(index_ids == degree, corner, 0.0))
    deriv = deriv + np.where(same, ends[None, :], 0.0)
    return deriv, weights


DERIV, WEIGHTS = gll_tables()
SQUARE = DERIV * DERIV
HALF = NODES // 2


def halves(table):
    mirrored = table[:HALF, ::-1][:, :HALF]
    direct = table[:HALF, :HALF]
    plus = (direct + mirrored) / 2.0
    minus = (direct - mirrored) / 2.0
    return plus.tolist(), minus.tolist()


D_PLUS, D_MINUS = halves(DERIV * np.sqrt(2.0))
Q_PLUS, Q_MINUS = halves(SQUARE * 2.0)


def fold(values):
    plus = [values[i] + values[7 - i] for i in range(HALF)]
    minus = [values[i] - values[7 - i] for i in range(HALF)]
    return plus, minus


def combine(table, values, transposed):
    out = []
    for a in range(HALF):
        total = None
        for i in range(HALF):
            factor = table[i][a] if transposed else table[a][i]
            term = values[i] * factor
            total = term if total is None else total + term
        out.append(total)
    return out


def unfold(base, turn):
    low = [base[a] + turn[a] for a in range(HALF)]
    high = [base[a] - turn[a] for a in range(HALF)]
    return low + high[::-1]


def derive(values):
    plus, minus = fold(values)
    return unfold(combine(D_MINUS, minus, False), combine(D_PLUS, plus, False))


def derive_back(values):
    plus, minus = fold(values)
    return unfold(combine(D_PLUS, minus, True), combine(D_MINUS, plus, True))


def square_back(values):
    plus, minus = fold(values)
    return unfold(combine(Q_PLUS, plus, True), combine(Q_MINUS, minus, True))


def tile_rows(base):
    return pl.ds(pl.multiple_of(base, 8), 8)


def strided(base):
    return pl.ds(base, 8, stride=8)


def line_x(n):
    base = (n // 8) * 512 + (n % 8) * 8
    return [tile_rows(base + 64 * i) for i in range(NODES)]


def line_y(n):
    return [tile_rows(n * 64 + 8 * j) for j in range(NODES)]


def line_z(n):
    base = pl.multiple_of(n * 64, 64)
    return [strided(base + k) for k in range(NODES)]


def lane_ids():
    return lax.broadcasted_iota(jnp.int32, (8, LANES), 1)


def sum_z(first, last):
    lane = lane_ids()
    total = last + jnp.where(lane < LANES - 1, pltpu.roll(first, LANES - 1, 1), 0.0)
    return jnp.where(lane > 0, pltpu.roll(total, 1, 1), first), total


def solve_kernel(
    loads,
    conduct,
    rhs,
    image,
    inverse,
    scalars,
    flux,
    flux_z,
    part_z,
    z0,
    weighted,
    from_x,
    from_y,
    from_edge,
    sums,
    part,
    gather_row,
    gather_col,
    in_sem,
    send_sem,
    recv_sem,
    sum_send,
    sum_recv,
):
    row = lax.axis_index("row")
    col = lax.axis_index("col")
    for ex in range(2):
        for ey in range(2):
            lanes = pl.ds((ex * 2 + ey) * LANES, LANES)
            pltpu.make_async_copy(
                conduct.at[:, :, :, lanes], flux.at[ex, ey], in_sem.at[SOURCES]
            ).start()
    for s in range(SOURCES):
        for ex in range(2):
            for ey in range(2):
                lanes = pl.ds((ex * 2 + ey) * LANES, LANES)
                pltpu.make_async_copy(
                    loads.at[s, :, :, :, lanes], rhs.at[s, ex, ey], in_sem.at[s]
                ).start()

    has_up, has_down = row < N_ROW - 1, row > 0
    has_right, has_left = col < N_COL - 1, col > 0
    ways = [
        (1, 0, has_up),
        (-1, 0, has_down),
        (0, 1, has_right),
        (0, -1, has_left),
        (1, 1, has_up & has_right),
        (1, -1, has_up & has_left),
        (-1, 1, has_down & has_right),
        (-1, -1, has_down & has_left),
    ]
    barrier = pltpu.get_barrier_semaphore()
    for step in range(1, N_ROW):
        pl.semaphore_signal(
            barrier, 1, device_id=(lax.rem(row + step, N_ROW), col), device_id_type=MESH
        )
    for step in range(1, N_COL):
        pl.semaphore_signal(
            barrier, 1, device_id=(row, lax.rem(col + step, N_COL)), device_id_type=MESH
        )
    corners = 0
    for dr, dc, there in ways[4:]:

        @pl.when(there)
        def _():
            pl.semaphore_signal(barrier, 1, device_id=(row + dr, col + dc), device_id_type=MESH)

        corners = corners + there.astype(jnp.int32)

    def transfers(q, ref):
        pieces = [
            (ref.at[1, :, 7], from_x.at[q, 0]),
            (ref.at[0, :, 0], from_x.at[q, 1]),
            (ref.at[:, 1, :, 7], from_y.at[q, 0]),
            (ref.at[:, 0, :, 0], from_y.at[q, 1]),
            (ref.at[1, 1, 7, 7], from_edge.at[q, 0]),
            (ref.at[1, 0, 7, 0], from_edge.at[q, 1]),
            (ref.at[0, 1, 0, 7], from_edge.at[q, 2]),
            (ref.at[0, 0, 0, 0], from_edge.at[q, 3]),
        ]
        return [
            pltpu.make_async_remote_copy(
                src,
                dst,
                send_sem.at[q, n],
                recv_sem.at[q, n],
                device_id=(row + ways[n][0], col + ways[n][1]),
                device_id_type=MESH,
            )
            for n, (src, dst) in enumerate(pieces)
        ]

    order = (2, 3, 0, 1, 4, 5, 6, 7)

    def send(q, ref):
        copies = transfers(q, ref)
        for n in order:

            @pl.when(ways[n][2])
            def _():
                copies[n].start()

    def finish(q, ref):
        copies = transfers(q, ref)
        for n in order:

            @pl.when(ways[n][2])
            def _():
                copies[n].wait_send()

        for n in order:

            @pl.when(ways[n ^ 1 if n < 4 else 11 - n][2])
            def _():
                copies[n].wait_recv()

    def clear(ref, there, pick):
        @pl.when(jnp.logical_not(there))
        def _():
            def body(q, carry):
                target = pick(ref, q)
                target[...] = jnp.zeros_like(target)
                return carry

            lax.fori_loop(0, 9, body, 0)

    clear(from_x, has_down, lambda ref, q: ref.at[q, 0])
    clear(from_x, has_up, lambda ref, q: ref.at[q, 1])
    clear(from_y, has_left, lambda ref, q: ref.at[q, 0])
    clear(from_y, has_right, lambda ref, q: ref.at[q, 1])
    clear(from_edge, has_down & has_left, lambda ref, q: ref.at[q, 0])
    clear(from_edge, has_down & has_right, lambda ref, q: ref.at[q, 1])
    clear(from_edge, has_up & has_left, lambda ref, q: ref.at[q, 2])
    clear(from_edge, has_up & has_right, lambda ref, q: ref.at[q, 3])
    sums[...] = jnp.zeros_like(sums)

    def assemble(q, ref):
        def along_x(j, carry):
            for ey in range(2):
                ref[0, ey, 0, j] = ref[0, ey, 0, j] + from_x[q, 0, ey, j]
                ref[1, ey, 7, j] = ref[1, ey, 7, j] + from_x[q, 1, ey, j]
                both = ref[0, ey, 7, j] + ref[1, ey, 0, j]
                ref[0, ey, 7, j] = both
                ref[1, ey, 0, j] = both
            return carry

        lax.fori_loop(0, NODES, along_x, 0, unroll=4)
        for side in range(2):
            from_y[q, side, 0, 0] = from_y[q, side, 0, 0] + from_edge[q, side]
            from_y[q, side, 1, 7] = from_y[q, side, 1, 7] + from_edge[q, 2 + side]
            both = from_y[q, side, 0, 7] + from_y[q, side, 1, 0]
            from_y[q, side, 0, 7] = both
            from_y[q, side, 1, 0] = both

        def along_y(i, carry):
            for ex in range(2):
                ref[ex, 0, i, 0] = ref[ex, 0, i, 0] + from_y[q, 0, ex, i]
                ref[ex, 1, i, 7] = ref[ex, 1, i, 7] + from_y[q, 1, ex, i]
                both = ref[ex, 0, i, 7] + ref[ex, 1, i, 0]
                ref[ex, 0, i, 7] = both
                ref[ex, 1, i, 0] = both
            return carry

        lax.fori_loop(0, NODES, along_y, 0, unroll=4)

    def along_z(flat):
        def body(n, carry):
            base = pl.multiple_of(n * 64, 64)
            first, last = sum_z(flat[strided(base), :], flat[strided(base + 7), :])
            flat[strided(base), :] = first
            flat[strided(base + 7), :] = last
            return carry

        lax.fori_loop(0, 32, body, 0, unroll=8)

    flux2 = flux.reshape(ROWS, LANES)
    inverse2 = inverse.reshape(ROWS, LANES)
    weighted2 = weighted.reshape(ROWS, LANES)
    z02 = z0.reshape(ROWS, LANES)

    pltpu.make_async_copy(flux, flux, in_sem.at[SOURCES]).wait()
    node = lax.broadcasted_iota(jnp.int32, (8, LANES), 0)
    weight_z = jnp.full((8, LANES), WEIGHTS[3], jnp.float32)
    for k in (0, 1, 2):
        ends = (node == k) | (node == 7 - k)
        weight_z = jnp.where(ends, jnp.float32(WEIGHTS[k]), weight_z)

    def weigh(t, carry):
        for i in range(NODES):
            for j in range(NODES):
                at = tile_rows(t * 512 + i * 64 + j * 8)
                flux2[at, :] = flux2[at, :] * (weight_z * float(SCREENING * WEIGHTS[i] * WEIGHTS[j]))
        return carry

    lax.fori_loop(0, 4, weigh, 0)

    def diag_x(n, carry):
        at = line_x(n)
        values = [flux2[a, :] for a in at]
        for a, v, r in zip(at, values, square_back(values)):
            inverse2[a, :] = r + v
        return carry

    def diag_y(n, carry):
        at = line_y(n)
        result = square_back([flux2[a, :] for a in at])
        for a, r in zip(at, result):
            inverse2[a, :] = inverse2[a, :] + r
        return carry

    def diag_z(n, carry):
        at = line_z(n)
        values = [flux2[a, :] for a in at]
        before = [inverse2[a, :] for a in at]
        for a, v in zip(line_y(n), values):
            flux_z[a, :] = v
        for a, b, r in zip(at, before, square_back(values)):
            inverse2[a, :] = b + r
        return carry

    lax.fori_loop(0, 32, diag_x, 0, unroll=2)
    lax.fori_loop(0, 32, diag_y, 0, unroll=2)
    lax.fori_loop(0, 32, diag_z, 0, unroll=2)

    pl.semaphore_wait(barrier, N_ROW - 1 + N_COL - 1 + corners)

    def arrive(s):
        pltpu.make_async_copy(rhs.at[s], rhs.at[s], in_sem.at[s]).wait()
        send(s, rhs.at[s])

    arrive(0)
    send(SOURCES, inverse)
    for s in range(1, SOURCES):
        arrive(s)
    finish(SOURCES, inverse)
    assemble(SOURCES, inverse)
    along_z(inverse2)

    lane = lane_ids()
    twice_z = ((node == 0) & (lane > 0)) | ((node == 7) & (lane < LANES - 1))
    share_z = jnp.where(twice_z, jnp.float32(0.5), jnp.float32(1.0))

    def invert(n, carry):
        for j in range(NODES):
            at = tile_rows(n * 64 + 8 * j)
            value = 1.0 / inverse2[at, :]
            inverse2[at, :] = value
            weighted2[at, :] = value * share_z
        return carry

    lax.fori_loop(0, 32, invert, 0)
    shares = [
        (has_down, 0, 0),
        (None, 0, 7),
        (None, 1, 0),
        (has_up, 1, 7),
    ]
    for there, ex, i in shares:
        share = 0.5 if there is None else jnp.where(there, 0.5, 1.0).astype(jnp.float32)
        for ey in range(2):
            weighted[ex, ey, i] = weighted[ex, ey, i] * share
    shares = [
        (has_left, 0, 0),
        (None, 0, 7),
        (None, 1, 0),
        (has_right, 1, 7),
    ]
    for there, ey, j in shares:
        share = 0.5 if there is None else jnp.where(there, 0.5, 1.0).astype(jnp.float32)
        for ex in range(2):
            weighted[ex, ey, :, j] = weighted[ex, ey, :, j] * share

    zero = jnp.zeros((8, LANES), jnp.float32)

    def put_sum(at, value):
        sums[pl.ds(at, 1), :] = jnp.sum(value, axis=0, keepdims=True)

    def settle(s):
        finish(SOURCES + 1 + s, image.at[s])
        assemble(SOURCES + 1 + s, image.at[s])
        flat = image.at[s].reshape(ROWS, LANES)
        along_z(flat)

        def body(n, carry):
            for j in range(NODES):
                at = tile_rows(n * 64 + 8 * j)
                value = flat[at, :]
                carry = carry + value * value * weighted2[at, :]
            return carry

        put_sum(8 + s, lax.fori_loop(0, 32, body, zero))

    def source(s, carry):
        finish(s, rhs.at[s])
        assemble(s, rhs.at[s])
        right = rhs.at[s].reshape(ROWS, LANES)
        flat = image.at[s].reshape(ROWS, LANES)
        along_z(right)

        def scale(n, carry):
            for j in range(NODES):
                at = tile_rows(n * 64 + 8 * j)
                value = right[at, :]
                z02[at, :] = value * inverse2[at, :]
                carry = carry + value * value * weighted2[at, :]
            return carry

        put_sum(s, lax.fori_loop(0, 32, scale, zero))

        def stiff(at, weight):
            values = [z02[a, :] for a in at]
            slopes = [g * w for g, w in zip(derive(values), weight)]
            return values, derive_back(slopes)

        def stiff_x(n, carry):
            at = line_x(n)
            weight = [flux2[a, :] for a in at]
            values, result = stiff(at, weight)
            for a, v, w, r in zip(at, values, weight, result):
                flat[a, :] = r + w * v
            return carry

        def stiff_yz(n, carry):
            at = line_y(n)
            strips = line_z(n)
            before = [flat[a, :] for a in at]
            _, result_y = stiff(at, [flux2[a, :] for a in at])
            _, result_z = stiff(strips, [flux_z[a, :] for a in at])
            for a, r in zip(strips, result_z):
                part_z[a, :] = r
            for a, b, r in zip(at, before, result_y):
                flat[a, :] = b + r
            return carry

        def add_z(n, carry):
            for a in line_y(n):
                total = flat[a, :] + part_z[a, :]
                flat[a, :] = total
                carry = carry + z02[a, :] * total
            return carry

        lax.fori_loop(0, 32, stiff_x, 0, unroll=4)
        lax.fori_loop(0, 32, stiff_yz, 0, unroll=2)
        put_sum(4 + s, lax.fori_loop(0, 32, add_z, zero, unroll=2))
        send(SOURCES + 1 + s, image.at[s])

        @pl.when(s > 1)
        def _():
            settle(s - 2)

        return carry

    lax.fori_loop(0, SOURCES, source, 0)
    settle(SOURCES - 2)
    settle(SOURCES - 1)

    def gather(stage, slots, mine, count, at, target):
        slots[at] = mine[...]
        copies = [
            pltpu.make_async_remote_copy(
                mine,
                slots.at[at],
                sum_send.at[stage],
                sum_recv.at[stage],
                device_id=target(lax.rem(at + step, count)),
                device_id_type=MESH,
            )
            for step in range(1, count)
        ]
        for copy in copies:
            copy.start()
        others = slots.at[pl.ds(0, count - 1)]
        pltpu.make_async_copy(others, others, sum_recv.at[stage]).wait()
        pltpu.make_async_copy(others, others, sum_send.at[stage]).wait()
        total = slots[0]
        for n in range(1, count):
            total = total + slots[n]
        return total

    total = jnp.sum(sums[...], axis=1, keepdims=True)
    node16 = lax.broadcasted_iota(jnp.int32, (16, LANES), 0)
    lane16 = lax.broadcasted_iota(jnp.int32, (16, LANES), 1)
    packed = jnp.where(node16 == lane16, jnp.broadcast_to(total, (16, LANES)), 0.0)
    part[0:1, :] = jnp.sum(packed, axis=0, keepdims=True)
    part[1:2, :] = gather(0, gather_row, part.at[0:1], N_ROW, row, lambda r: (r, col))
    total = gather(1, gather_col, part.at[1:2], N_COL, col, lambda c: (row, c))
    total = jnp.broadcast_to(total, (16, LANES))
    total = jnp.sum(jnp.where(node16 == lane16, total, 0.0), axis=1, keepdims=True)
    rz_first, curvature, square = total[0:4], total[4:8], total[8:12]
    alpha = rz_first / curvature
    rz_second = alpha * alpha * square - rz_first
    beta = rz_second / rz_first
    scalars[0:4, :] = jnp.broadcast_to(alpha, (4, LANES))
    scalars[4:8, :] = jnp.broadcast_to(beta, (4, LANES))


SLOTS = 8


def update_kernel(rhs, image, inverse, scalars, first, second, third, staging, sem):
    outputs = (first, second, third)

    def copies(n):
        return [
            pltpu.make_async_copy(
                staging.at[n % SLOTS, q], outputs[q].at[n // NODES, n % NODES], sem.at[n % SLOTS, q]
            )
            for q in range(3)
        ]

    def step(n, carry):
        s, i, slot = n // NODES, n % NODES, n % SLOTS

        @pl.when(n >= SLOTS)
        def _():
            for copy in copies(n - SLOTS):
                copy.wait()

        alpha = jnp.broadcast_to(scalars[pl.ds(s, 1), :], (8, LANES))
        beta = jnp.broadcast_to(scalars[pl.ds(s + 4, 1), :], (8, LANES))
        for ex in range(2):
            for ey in range(2):
                lanes = pl.ds((ex * 2 + ey) * LANES, LANES)
                for j in range(NODES):
                    right = rhs[s, ex, ey, i, j]
                    inv = inverse[ex, ey, i, j]
                    rest = right - alpha * image[s, ex, ey, i, j]
                    staging[slot, 0, j, :, lanes] = alpha * (right * inv)
                    staging[slot, 1, j, :, lanes] = rest
                    staging[slot, 2, j, :, lanes] = (rest + beta * right) * inv
        for copy in copies(n):
            copy.start()
        return carry

    steps = SOURCES * NODES
    lax.fori_loop(0, steps, step, 0)
    for n in range(steps - SLOTS, steps):
        for copy in copies(n):
            copy.wait()


def per_device(loads, conduct):
    f32 = jnp.float32
    vmem = pltpu.VMEM
    whole = pl.BlockSpec(memory_space=vmem)
    many = (SOURCES,) + FIELD
    rhs, image, inverse, scalars = pl.pallas_call(
        solve_kernel,
        out_shape=[vmem(many, f32), vmem(many, f32), vmem(FIELD, f32), vmem((8, LANES), f32)],
        in_specs=[pl.BlockSpec(memory_space=pl.ANY)] * 2,
        out_specs=[whole] * 4,
        scratch_shapes=[
            vmem(FIELD, f32),
            vmem((ROWS, LANES), f32),
            vmem((ROWS, LANES), f32),
            vmem(FIELD, f32),
            vmem(FIELD, f32),
            vmem((9, 2, 2, NODES, NODES, LANES), f32),
            vmem((9, 2, 2, NODES, NODES, LANES), f32),
            vmem((9, 4, NODES, LANES), f32),
            vmem((16, LANES), f32),
            vmem((8, LANES), f32),
            vmem((N_ROW, 1, LANES), f32),
            vmem((N_COL, 1, LANES), f32),
            pltpu.SemaphoreType.DMA((SOURCES + 1,)),
            pltpu.SemaphoreType.DMA((9, 8)),
            pltpu.SemaphoreType.DMA((9, 8)),
            pltpu.SemaphoreType.DMA((2,)),
            pltpu.SemaphoreType.DMA((2,)),
        ],
        compiler_params=pltpu.CompilerParams(
            collective_id=0, has_side_effects=True, vmem_limit_bytes=40 * 1024 * 1024
        ),
    )(*[pltpu.with_memory_space_constraint(x, pltpu.HBM) for x in (loads, conduct)])
    shape = (SOURCES, NODES, NODES, NODES, 4 * LANES)
    return pl.pallas_call(
        update_kernel,
        out_shape=[jax.ShapeDtypeStruct(shape, f32)] * 3,
        in_specs=[whole] * 4,
        out_specs=[pl.BlockSpec(memory_space=pl.ANY)] * 3,
        scratch_shapes=[
            vmem((SLOTS, 3, NODES, NODES, 4 * LANES), f32),
            pltpu.SemaphoreType.DMA((SLOTS, 3)),
        ],
        compiler_params=pltpu.CompilerParams(vmem_limit_bytes=16 * 1024 * 1024),
    )(*[pltpu.with_memory_space_constraint(x, vmem) for x in (rhs, image, inverse, scalars)])


def solution(mesh):
    in_specs = (P(None, None, None, None, ("row", "col")), P(None, None, None, ("row", "col")))
    out = P(None, None, None, None, ("row", "col"))
    return jax.shard_map(
        per_device, mesh=mesh, in_specs=in_specs, out_specs=(out, out, out), check_vma=False
    )
```

```python
import functools

import jax
import jax.numpy as jnp
import numpy as np
from jax import lax
from jax.experimental import pallas as pl
from jax.experimental.pallas import tpu as pltpu
from jax.sharding import PartitionSpec as P

NODES = 8
SOURCES = 4
LANES = 128
N_ROW = 8
N_COL = 16
SCREENING = 0.5
GLL_INNER = [
    -0.8717401485096066,
    -0.5917001814331423,
    -0.2092992179024789,
    0.2092992179024789,
    0.5917001814331423,
    0.8717401485096066,
]
MESH = pl.DeviceIdType.MESH
FIELD = (2, 2, NODES, NODES, NODES, LANES)


def gll_tables():
    degree = NODES - 1
    points = np.array([-1.0] + GLL_INNER + [1.0])
    previous = points * 0.0 + 1.0
    current = points * 1.0
    for order in range(1, degree):
        following = ((2 * order + 1) * points * current - order * previous) / (order + 1)
        previous = current
        current = following
    weights = 2.0 / (degree * (degree + 1) * current**2)
    spread = points[:, None] - points[None, :]
    index_ids = np.arange(NODES)
    same = index_ids[:, None] == index_ids[None, :]
    safe_spread = np.where(same, 1.0, spread)
    deriv = np.where(same, 0.0, current[:, None] / (current[None, :] * safe_spread))
    corner = degree * (degree + 1) / 4.0
    ends = np.where(index_ids == 0, -corner, np.where(index_ids == degree, corner, 0.0))
    deriv = deriv + np.where(same, ends[None, :], 0.0)
    return deriv, weights


DERIV, WEIGHTS = gll_tables()
SQUARE = DERIV * DERIV
HALF = NODES // 2


def halves(table):
    mirrored = table[:HALF, ::-1][:, :HALF]
    direct = table[:HALF, :HALF]
    plus = (direct + mirrored) / 2.0
    minus = (direct - mirrored) / 2.0
    return plus.tolist(), minus.tolist()


D_PLUS, D_MINUS = halves(DERIV * np.sqrt(2.0))
Q_PLUS, Q_MINUS = halves(SQUARE * 2.0)


def fold(values):
    plus = [values[i] + values[7 - i] for i in range(HALF)]
    minus = [values[i] - values[7 - i] for i in range(HALF)]
    return plus, minus


def combine(table, values, transposed):
    out = []
    for a in range(HALF):
        total = None
        for i in range(HALF):
            factor = table[i][a] if transposed else table[a][i]
            term = values[i] * factor
            total = term if total is None else total + term
        out.append(total)
    return out


def unfold(base, turn):
    low = [base[a] + turn[a] for a in range(HALF)]
    high = [base[a] - turn[a] for a in range(HALF)]
    return low + high[::-1]


def derive(values):
    plus, minus = fold(values)
    return unfold(combine(D_MINUS, minus, False), combine(D_PLUS, plus, False))


def derive_back(values):
    plus, minus = fold(values)
    return unfold(combine(D_PLUS, minus, True), combine(D_MINUS, plus, True))


def square_back(values):
    plus, minus = fold(values)
    return unfold(combine(Q_PLUS, plus, True), combine(Q_MINUS, minus, True))


def tree_sum(terms):
    while len(terms) > 1:
        terms = [a + b for a, b in zip(terms[::2], terms[1::2])]
    return terms[0]


def lines_x(t):
    return [[(t, i, j) for i in range(NODES)] for j in range(NODES)]


def lines_y(g):
    return [[(g, u, j) for j in range(NODES)] for u in range(4)]


def lines_z(g):
    return [[(g, u, pl.ds(k, 8, stride=8)) for k in range(NODES)] for u in range(4)]


def views(ref):
    along_x = ref.reshape(4, NODES, NODES, NODES, LANES)
    along_y = ref.reshape(8, 4, NODES, NODES, LANES)
    along_z = ref.reshape(8, 4, NODES * NODES, LANES)
    return along_x, along_y, along_z


def read(ref, line):
    return [ref[at] for at in line]


def write(ref, line, values):
    for at, value in zip(line, values):
        ref[at] = value


def sum_z(first, last):
    lane = lax.broadcasted_iota(jnp.int32, (8, LANES), 1)
    after = jnp.where(lane < LANES - 1, pltpu.roll(first, LANES - 1, 1), 0.0)
    before = jnp.where(lane > 0, pltpu.roll(last, 1, 1), 0.0)
    return first + before, last + after


def assemble_inside(ref):
    for ey in range(2):
        for j in range(NODES):
            both = ref[0, ey, 7, j] + ref[1, ey, 0, j]
            ref[0, ey, 7, j] = both
            ref[1, ey, 0, j] = both
    for ex in range(2):
        for i in range(NODES):
            both = ref[ex, 0, i, 7] + ref[ex, 1, i, 0]
            ref[ex, 0, i, 7] = both
            ref[ex, 1, i, 0] = both
    strips = views(ref)[2]

    def along_z(g, carry):
        lines = [line for u in range(4) for line in lines_z(g * 4 + u)]
        ends = [(strips[line[0]], strips[line[7]]) for line in lines]
        ends = [sum_z(first, last) for first, last in ends]
        for line, (first, last) in zip(lines, ends):
            strips[line[0]] = first
            strips[line[7]] = last
        return carry

    lax.fori_loop(0, 2, along_z, 0)


DIAG = SOURCES
IMAGE = SOURCES + 1
FIELDS = 2 * SOURCES + 1


def solve_kernel(
    loads,
    conduct,
    fields,
    scalars,
    flux,
    flux_z,
    part_z,
    z0,
    weighted,
    from_x,
    from_y,
    from_edge,
    sums,
    part,
    gather_row,
    gather_col,
    in_sem,
    send_sem,
    recv_sem,
    sum_send,
    sum_recv,
):
    row = lax.axis_index("row")
    col = lax.axis_index("col")
    for ex in range(2):
        for ey in range(2):
            lanes = pl.ds((ex * 2 + ey) * LANES, LANES)
            pltpu.make_async_copy(
                conduct.at[:, :, :, lanes], flux.at[ex, ey], in_sem.at[SOURCES]
            ).start()
    for s in range(SOURCES):
        for ex in range(2):
            for ey in range(2):
                lanes = pl.ds((ex * 2 + ey) * LANES, LANES)
                pltpu.make_async_copy(
                    loads.at[s, :, :, :, lanes], fields.at[s, ex, ey], in_sem.at[s]
                ).start()

    has_up, has_down = row < N_ROW - 1, row > 0
    has_right, has_left = col < N_COL - 1, col > 0
    ways = [
        (1, 0, has_up),
        (-1, 0, has_down),
        (0, 1, has_right),
        (0, -1, has_left),
        (1, 1, has_up & has_right),
        (1, -1, has_up & has_left),
        (-1, 1, has_down & has_right),
        (-1, -1, has_down & has_left),
    ]
    barrier = pltpu.get_barrier_semaphore()
    corners = 0
    for dr, dc, there in ways[4:]:

        @pl.when(there)
        def _():
            pl.semaphore_signal(barrier, 1, device_id=(row + dr, col + dc), device_id_type=MESH)

        corners = corners + there.astype(jnp.int32)
    for step in range(1, N_COL):
        pl.semaphore_signal(
            barrier, 1, device_id=(row, lax.rem(col + step, N_COL)), device_id_type=MESH
        )
    for step in range(1, N_ROW):
        pl.semaphore_signal(
            barrier, 1, device_id=(lax.rem(row + step, N_ROW), col), device_id_type=MESH
        )

    def transfers(q):
        ref = fields.at[q]
        pieces = [
            (ref.at[1, :, 7], from_x.at[q, 0]),
            (ref.at[0, :, 0], from_x.at[q, 1]),
            (ref.at[:, 1, :, 7], from_y.at[q, 0]),
            (ref.at[:, 0, :, 0], from_y.at[q, 1]),
            (ref.at[1, 1, 7, 7], from_edge.at[q, 0]),
            (ref.at[1, 0, 7, 0], from_edge.at[q, 1]),
            (ref.at[0, 1, 0, 7], from_edge.at[q, 2]),
            (ref.at[0, 0, 0, 0], from_edge.at[q, 3]),
        ]
        return [
            pltpu.make_async_remote_copy(
                src,
                dst,
                send_sem.at[q, n],
                recv_sem.at[q, n],
                device_id=(row + ways[n][0], col + ways[n][1]),
                device_id_type=MESH,
            )
            for n, (src, dst) in enumerate(pieces)
        ]

    order = (2, 3, 4, 5, 6, 7, 0, 1)

    def send(q):
        copies = transfers(q)
        for n in order:

            @pl.when(ways[n][2])
            def _():
                copies[n].start()

    def collect(q):
        copies = transfers(q)
        for n in order:

            @pl.when(ways[n][2])
            def _():
                copies[n].wait_send()

        for n in order:

            @pl.when(ways[n ^ 1 if n < 4 else 11 - n][2])
            def _():
                copies[n].wait_recv()

        ref = fields.at[q]
        for ey in range(2):
            for j in range(NODES):
                ref[0, ey, 0, j] = ref[0, ey, 0, j] + from_x[q, 0, ey, j]
                ref[1, ey, 7, j] = ref[1, ey, 7, j] + from_x[q, 1, ey, j]
        for ex in range(2):
            for i in range(NODES):
                ref[ex, 0, i, 0] = ref[ex, 0, i, 0] + from_y[q, 0, ex, i]
                ref[ex, 1, i, 7] = ref[ex, 1, i, 7] + from_y[q, 1, ex, i]
        for corner in range(4):
            ex, ey = corner // 2, corner % 2
            at = (ex, ey, 7 * ex, 7 * ey)
            ref[at] = ref[at] + from_edge[q, corner]

    def clear(ref, there, pick):
        @pl.when(jnp.logical_not(there))
        def _():
            def body(q, carry):
                target = pick(ref, q)
                target[...] = jnp.zeros_like(target)
                return carry

            lax.fori_loop(0, FIELDS, body, 0)

    clear(from_x, has_down, lambda ref, q: ref.at[q, 0])
    clear(from_x, has_up, lambda ref, q: ref.at[q, 1])
    clear(from_y, has_left, lambda ref, q: ref.at[q, 0])
    clear(from_y, has_right, lambda ref, q: ref.at[q, 1])
    clear(from_edge, has_down & has_left, lambda ref, q: ref.at[q, 0])
    clear(from_edge, has_down & has_right, lambda ref, q: ref.at[q, 1])
    clear(from_edge, has_up & has_left, lambda ref, q: ref.at[q, 2])
    clear(from_edge, has_up & has_right, lambda ref, q: ref.at[q, 3])
    sums[...] = jnp.zeros_like(sums)

    flux_v = views(flux)
    flux_zv = views(flux_z)
    part_v = views(part_z)
    z0_v = views(z0)
    weighted_v = views(weighted)
    diag_v = views(fields.at[DIAG])

    pltpu.make_async_copy(flux, flux, in_sem.at[SOURCES]).wait()
    node = lax.broadcasted_iota(jnp.int32, (8, LANES), 0)
    lane = lax.broadcasted_iota(jnp.int32, (8, LANES), 1)
    weight_z = jnp.full((8, LANES), WEIGHTS[3], jnp.float32)
    for k in (0, 1, 2):
        ends = (node == k) | (node == 7 - k)
        weight_z = jnp.where(ends, jnp.float32(WEIGHTS[k]), weight_z)

    def diag_x(t, carry):
        for j, line in enumerate(lines_x(t)):
            values = [
                v * (weight_z * float(SCREENING * WEIGHTS[i] * WEIGHTS[j]))
                for i, v in enumerate(read(flux_v[0], line))
            ]
            write(flux_v[0], line, values)
            write(diag_v[0], line, [r + v for r, v in zip(square_back(values), values)])
        return carry

    def diag_yz(g, carry):
        for line, strip in zip(lines_y(g), lines_z(g)):
            before = read(diag_v[1], line)
            result_y = square_back(read(flux_v[1], line))
            values = read(flux_v[2], strip)
            write(flux_zv[1], line, values)
            write(part_v[2], strip, square_back(values))
            write(diag_v[1], line, [b + r for b, r in zip(before, result_y)])
        return carry

    def diag_sum(g, carry):
        for line in lines_y(g):
            both = zip(read(diag_v[1], line), read(part_v[1], line))
            write(diag_v[1], line, [b + r for b, r in both])
        return carry

    lax.fori_loop(0, 4, diag_x, 0)
    lax.fori_loop(0, 8, diag_yz, 0)
    lax.fori_loop(0, 8, diag_sum, 0)

    def prepare(n, carry):
        q = lax.rem(n + DIAG, DIAG + 1)

        @pl.when(n > 0)
        def _():
            pltpu.make_async_copy(fields.at[q], fields.at[q], in_sem.at[q]).wait()

        assemble_inside(fields.at[q])
        return carry

    lax.fori_loop(0, DIAG + 1, prepare, 0)
    pl.semaphore_wait(barrier, N_ROW - 1 + N_COL - 1 + corners)

    def send_first(n, carry):
        send(lax.rem(n + DIAG, DIAG + 1))
        return carry

    lax.fori_loop(0, DIAG + 1, send_first, 0)

    twice_z = ((node == 0) & (lane > 0)) | ((node == 7) & (lane < LANES - 1))
    share_z = jnp.where(twice_z, jnp.float32(0.5), jnp.float32(1.0))
    zero = jnp.zeros((8, LANES), jnp.float32)

    def put_sum(at, value):
        sums[pl.ds(at, 1), :] = jnp.sum(value, axis=0, keepdims=True)

    def invert_all():
        def invert(g, carry):
            for line in lines_y(g):
                values = [1.0 / v for v in read(diag_v[1], line)]
                write(diag_v[1], line, values)
                write(weighted_v[1], line, [v * share_z for v in values])
            return carry

        lax.fori_loop(0, 8, invert, 0)

        def part_of(there):
            return 0.5 if there is None else jnp.where(there, 0.5, 1.0).astype(jnp.float32)

        for there, ex, i in [(has_down, 0, 0), (None, 0, 7), (None, 1, 0), (has_up, 1, 7)]:
            for ey in range(2):
                weighted[ex, ey, i] = weighted[ex, ey, i] * part_of(there)
        for there, ey, j in [(has_left, 0, 0), (None, 0, 7), (None, 1, 0), (has_right, 1, 7)]:
            for ex in range(2):
                weighted[ex, ey, :, j] = weighted[ex, ey, :, j] * part_of(there)

    def apply(s):
        right_v = views(fields.at[s])
        image_v = views(fields.at[IMAGE + s])

        def scale(g, carry):
            terms = []
            for line in lines_y(g):
                values = read(right_v[1], line)
                write(z0_v[1], line, [v * d for v, d in zip(values, read(diag_v[1], line))])
                terms += [v * v * d for v, d in zip(values, read(weighted_v[1], line))]
            return carry + tree_sum(terms)

        put_sum(s, lax.fori_loop(0, 8, scale, zero))

        def stiff(values, weight):
            return derive_back([g * w for g, w in zip(derive(values), weight)])

        def stiff_x(t, carry):
            for line in lines_x(t):
                values, weight = read(z0_v[0], line), read(flux_v[0], line)
                result = stiff(values, weight)
                write(image_v[0], line, [r + w * v for r, w, v in zip(result, weight, values)])
            return carry

        def stiff_yz(g, carry):
            pairs = list(zip(lines_y(g), lines_z(g)))
            results = [stiff(read(z0_v[2], strip), read(flux_zv[1], line)) for line, strip in pairs]
            for (line, strip), result in zip(pairs, results):
                write(part_v[2], strip, result)
            for line, _ in pairs:
                before = read(image_v[1], line)
                result = stiff(read(z0_v[1], line), read(flux_v[1], line))
                write(image_v[1], line, [b + r for b, r in zip(before, result)])
            return carry

        def add_z(g, carry):
            terms = []
            for line in lines_y(g):
                both = zip(read(image_v[1], line), read(part_v[1], line))
                total = [a + b for a, b in both]
                write(image_v[1], line, total)
                terms += [v * r for v, r in zip(read(z0_v[1], line), total)]
            return carry + tree_sum(terms)

        lax.fori_loop(0, 4, stiff_x, 0)
        lax.fori_loop(0, 8, stiff_yz, 0)
        put_sum(SOURCES + s, lax.fori_loop(0, 8, add_z, zero))
        assemble_inside(fields.at[IMAGE + s])
        send(IMAGE + s)

    def settle(s):
        image_v = views(fields.at[IMAGE + s])

        def square(g, carry):
            terms = []
            for line in lines_y(g):
                both = zip(read(image_v[1], line), read(weighted_v[1], line))
                terms += [v * v * w for v, w in both]
            return carry + tree_sum(terms)

        put_sum(2 * SOURCES + s, lax.fori_loop(0, 8, square, zero))

    def advance(n, carry):
        q = jnp.where(n == 0, DIAG, jnp.where(n <= SOURCES, n - 1, n))
        collect(q)
        pl.when(n == 0)(invert_all)
        pl.when((n > 0) & (n <= SOURCES))(lambda: apply(n - 1))
        pl.when(n > SOURCES)(lambda: settle(n - IMAGE))
        return carry

    lax.fori_loop(0, FIELDS, advance, 0)

    def gather(stage, slots, mine, count, at, target):
        slots[at] = mine[...]
        copies = [
            pltpu.make_async_remote_copy(
                mine,
                slots.at[at],
                sum_send.at[stage],
                sum_recv.at[stage],
                device_id=target(lax.rem(at + step, count)),
                device_id_type=MESH,
            )
            for step in range(1, count)
        ]
        for copy in copies:
            copy.start()
        others = slots.at[pl.ds(0, count - 1)]
        pltpu.make_async_copy(others, others, sum_recv.at[stage]).wait()
        pltpu.make_async_copy(others, others, sum_send.at[stage]).wait()
        total = slots[0]
        for n in range(1, count):
            total = total + slots[n]
        return total

    total = jnp.sum(sums[...], axis=1, keepdims=True)
    node16 = lax.broadcasted_iota(jnp.int32, (16, LANES), 0)
    lane16 = lax.broadcasted_iota(jnp.int32, (16, LANES), 1)
    packed = jnp.where(node16 == lane16, jnp.broadcast_to(total, (16, LANES)), 0.0)
    part[0:1, :] = jnp.sum(packed, axis=0, keepdims=True)
    part[1:2, :] = gather(0, gather_row, part.at[0:1], N_ROW, row, lambda r: (r, col))
    total = gather(1, gather_col, part.at[1:2], N_COL, col, lambda c: (row, c))
    total = jnp.broadcast_to(total, (16, LANES))
    total = jnp.sum(jnp.where(node16 == lane16, total, 0.0), axis=1, keepdims=True)
    rz_first, curvature, square = total[0:4], total[4:8], total[8:12]
    alpha = rz_first / curvature
    rz_second = alpha * alpha * square - rz_first
    beta = rz_second / rz_first
    scalars[0:4, :] = jnp.broadcast_to(alpha, (4, LANES))
    scalars[4:8, :] = jnp.broadcast_to(beta, (4, LANES))


SLOTS = 8


def update_kernel(fields, scalars, first, second, third, staging, sem):
    outputs = (first, second, third)

    def copies(n):
        return [
            pltpu.make_async_copy(
                staging.at[n % SLOTS, q], outputs[q].at[n // NODES, n % NODES], sem.at[n % SLOTS, q]
            )
            for q in range(3)
        ]

    def step(n, carry):
        s, i, slot = n // NODES, n % NODES, n % SLOTS

        @pl.when(n >= SLOTS)
        def _():
            for copy in copies(n - SLOTS):
                copy.wait()

        alpha = jnp.broadcast_to(scalars[pl.ds(s, 1), :], (8, LANES))
        beta = jnp.broadcast_to(scalars[pl.ds(s + 4, 1), :], (8, LANES))
        for ex in range(2):
            for ey in range(2):
                lanes = pl.ds((ex * 2 + ey) * LANES, LANES)
                for j in range(NODES):
                    right = fields[s, ex, ey, i, j]
                    inv = fields[DIAG, ex, ey, i, j]
                    rest = right - alpha * fields[IMAGE + s, ex, ey, i, j]
                    staging[slot, 0, j, :, lanes] = alpha * (right * inv)
                    staging[slot, 1, j, :, lanes] = rest
                    staging[slot, 2, j, :, lanes] = (rest + beta * right) * inv
        for copy in copies(n):
            copy.start()
        return carry

    steps = SOURCES * NODES
    lax.fori_loop(0, steps, step, 0)
    for n in range(steps - SLOTS, steps):
        for copy in copies(n):
            copy.wait()


def per_device(loads, conduct):
    f32 = jnp.float32
    vmem = pltpu.VMEM
    whole = pl.BlockSpec(memory_space=vmem)
    fields, scalars = pl.pallas_call(
        solve_kernel,
        out_shape=[vmem((FIELDS,) + FIELD, f32), vmem((8, LANES), f32)],
        in_specs=[pl.BlockSpec(memory_space=pl.ANY)] * 2,
        out_specs=[whole] * 2,
        scratch_shapes=[
            vmem(FIELD, f32),
            vmem(FIELD, f32),
            vmem(FIELD, f32),
            vmem(FIELD, f32),
            vmem(FIELD, f32),
            vmem((9, 2, 2, NODES, NODES, LANES), f32),
            vmem((9, 2, 2, NODES, NODES, LANES), f32),
            vmem((9, 4, NODES, LANES), f32),
            vmem((16, LANES), f32),
            vmem((8, LANES), f32),
            vmem((N_ROW, 1, LANES), f32),
            vmem((N_COL, 1, LANES), f32),
            pltpu.SemaphoreType.DMA((SOURCES + 1,)),
            pltpu.SemaphoreType.DMA((9, 8)),
            pltpu.SemaphoreType.DMA((9, 8)),
            pltpu.SemaphoreType.DMA((2,)),
            pltpu.SemaphoreType.DMA((2,)),
        ],
        compiler_params=pltpu.CompilerParams(
            collective_id=0, has_side_effects=True, vmem_limit_bytes=40 * 1024 * 1024
        ),
    )(*[pltpu.with_memory_space_constraint(x, pltpu.HBM) for x in (loads, conduct)])
    shape = (SOURCES, NODES, NODES, NODES, 4 * LANES)
    return pl.pallas_call(
        update_kernel,
        out_shape=[jax.ShapeDtypeStruct(shape, f32)] * 3,
        in_specs=[whole] * 2,
        out_specs=[pl.BlockSpec(memory_space=pl.ANY)] * 3,
        scratch_shapes=[
            vmem((SLOTS, 3, NODES, NODES, 4 * LANES), f32),
            pltpu.SemaphoreType.DMA((SLOTS, 3)),
        ],
        compiler_params=pltpu.CompilerParams(vmem_limit_bytes=16 * 1024 * 1024),
    )(*[pltpu.with_memory_space_constraint(x, vmem) for x in (fields, scalars)])


def solution(mesh):
    in_specs = (P(None, None, None, None, ("row", "col")), P(None, None, None, ("row", "col")))
    out = P(None, None, None, None, ("row", "col"))
    return jax.shard_map(
        per_device, mesh=mesh, in_specs=in_specs, out_specs=(out, out, out), check_vma=False
    )
```

```python
import functools

import jax
import jax.numpy as jnp
import numpy as np
from jax import lax
from jax.experimental import pallas as pl
from jax.experimental.pallas import tpu as pltpu
from jax.sharding import PartitionSpec as P

NODES = 8
SOURCES = 4
LANES = 128
N_ROW = 8
N_COL = 16
SCREENING = 0.5
GLL_INNER = [
    -0.8717401485096066,
    -0.5917001814331423,
    -0.2092992179024789,
    0.2092992179024789,
    0.5917001814331423,
    0.8717401485096066,
]
MESH = pl.DeviceIdType.MESH
FIELD = (2, 2, NODES, NODES, NODES, LANES)


def gll_tables():
    degree = NODES - 1
    points = np.array([-1.0] + GLL_INNER + [1.0])
    previous = points * 0.0 + 1.0
    current = points * 1.0
    for order in range(1, degree):
        following = ((2 * order + 1) * points * current - order * previous) / (order + 1)
        previous = current
        current = following
    weights = 2.0 / (degree * (degree + 1) * current**2)
    spread = points[:, None] - points[None, :]
    index_ids = np.arange(NODES)
    same = index_ids[:, None] == index_ids[None, :]
    safe_spread = np.where(same, 1.0, spread)
    deriv = np.where(same, 0.0, current[:, None] / (current[None, :] * safe_spread))
    corner = degree * (degree + 1) / 4.0
    ends = np.where(index_ids == 0, -corner, np.where(index_ids == degree, corner, 0.0))
    deriv = deriv + np.where(same, ends[None, :], 0.0)
    return deriv, weights


DERIV, WEIGHTS = gll_tables()
SQUARE = DERIV * DERIV
HALF = NODES // 2


def halves(table):
    mirrored = table[:HALF, ::-1][:, :HALF]
    direct = table[:HALF, :HALF]
    plus = (direct + mirrored) / 2.0
    minus = (direct - mirrored) / 2.0
    return plus.tolist(), minus.tolist()


SLOPE = DERIV * np.sqrt(2.0)
D_PLUS, D_MINUS = halves(SLOPE)
Q_PLUS, Q_MINUS = halves(SQUARE * 2.0)


def fold(values):
    plus = [values[i] + values[7 - i] for i in range(HALF)]
    minus = [values[i] - values[7 - i] for i in range(HALF)]
    return plus, minus


def combine(table, values, transposed):
    out = []
    for a in range(HALF):
        total = None
        for i in range(HALF):
            factor = table[i][a] if transposed else table[a][i]
            term = values[i] * factor
            total = term if total is None else total + term
        out.append(total)
    return out


def unfold(base, turn):
    low = [base[a] + turn[a] for a in range(HALF)]
    high = [base[a] - turn[a] for a in range(HALF)]
    return low + high[::-1]


def derive(values):
    plus, minus = fold(values)
    return unfold(combine(D_MINUS, minus, False), combine(D_PLUS, plus, False))


def derive_back(values):
    plus, minus = fold(values)
    return unfold(combine(D_PLUS, minus, True), combine(D_MINUS, plus, True))


def square_back(values):
    plus, minus = fold(values)
    return unfold(combine(Q_PLUS, plus, True), combine(Q_MINUS, minus, True))


def tree_sum(terms):
    while len(terms) > 1:
        terms = [a + b for a, b in zip(terms[::2], terms[1::2])]
    return terms[0]


def lines_x(t):
    return [[(t, i, j) for i in range(NODES)] for j in range(NODES)]


def lines_y(g):
    return [[(g, u, j) for j in range(NODES)] for u in range(4)]


def lines_z(g):
    return [[(g, u, pl.ds(k, 8, stride=8)) for k in range(NODES)] for u in range(4)]


def views(ref):
    along_x = ref.reshape(4, NODES, NODES, NODES, LANES)
    along_y = ref.reshape(8, 4, NODES, NODES, LANES)
    along_z = ref.reshape(8, 4, NODES * NODES, LANES)
    return along_x, along_y, along_z


def read(ref, line):
    return [ref[at] for at in line]


def write(ref, line, values):
    for at, value in zip(line, values):
        ref[at] = value


def sum_z(first, last):
    lane = lax.broadcasted_iota(jnp.int32, (8, LANES), 1)
    after = jnp.where(lane < LANES - 1, pltpu.roll(first, LANES - 1, 1), 0.0)
    before = jnp.where(lane > 0, pltpu.roll(last, 1, 1), 0.0)
    return first + before, last + after


def assemble_inside(ref):
    for ey in range(2):
        for j in range(NODES):
            both = ref[0, ey, 7, j] + ref[1, ey, 0, j]
            ref[0, ey, 7, j] = both
            ref[1, ey, 0, j] = both
    for ex in range(2):
        for i in range(NODES):
            both = ref[ex, 0, i, 7] + ref[ex, 1, i, 0]
            ref[ex, 0, i, 7] = both
            ref[ex, 1, i, 0] = both
    strips = views(ref)[2]

    def along_z(g, carry):
        lines = [line for u in range(4) for line in lines_z(g * 4 + u)]
        ends = [(strips[line[0]], strips[line[7]]) for line in lines]
        ends = [sum_z(first, last) for first, last in ends]
        for line, (first, last) in zip(lines, ends):
            strips[line[0]] = first
            strips[line[7]] = last
        return carry

    lax.fori_loop(0, 2, along_z, 0)


DIAG = SOURCES
IMAGE = SOURCES + 1
FIELDS = 2 * SOURCES + 1


def solve_kernel(
    loads,
    conduct,
    fields,
    inverse,
    scalars,
    flux,
    flux_z,
    part_z,
    z0,
    z_face,
    coef_x,
    coef_y,
    weighted,
    from_x,
    from_y,
    from_edge,
    sums,
    part,
    gather_row,
    gather_col,
    in_sem,
    send_sem,
    recv_sem,
    sum_send,
    sum_recv,
):
    row = lax.axis_index("row")
    col = lax.axis_index("col")
    for ex in range(2):
        for ey in range(2):
            lanes = pl.ds((ex * 2 + ey) * LANES, LANES)
            pltpu.make_async_copy(
                conduct.at[:, :, :, lanes], flux.at[ex, ey], in_sem.at[SOURCES]
            ).start()
    for s in range(SOURCES):
        for ex in range(2):
            for ey in range(2):
                lanes = pl.ds((ex * 2 + ey) * LANES, LANES)
                pltpu.make_async_copy(
                    loads.at[s, :, :, :, lanes], fields.at[s, ex, ey], in_sem.at[s]
                ).start()

    has_up, has_down = row < N_ROW - 1, row > 0
    has_right, has_left = col < N_COL - 1, col > 0
    ways = [
        (1, 0, has_up),
        (-1, 0, has_down),
        (0, 1, has_right),
        (0, -1, has_left),
        (1, 1, has_up & has_right),
        (1, -1, has_up & has_left),
        (-1, 1, has_down & has_right),
        (-1, -1, has_down & has_left),
    ]
    barrier = pltpu.get_barrier_semaphore()
    corners = 0
    for dr, dc, there in ways[4:]:

        @pl.when(there)
        def _():
            pl.semaphore_signal(barrier, 1, device_id=(row + dr, col + dc), device_id_type=MESH)

        corners = corners + there.astype(jnp.int32)
    for step in range(1, N_COL):
        pl.semaphore_signal(
            barrier, 1, device_id=(row, lax.rem(col + step, N_COL)), device_id_type=MESH
        )
    for step in range(1, N_ROW):
        pl.semaphore_signal(
            barrier, 1, device_id=(lax.rem(row + step, N_ROW), col), device_id_type=MESH
        )

    def transfers(q):
        ref = fields.at[q]
        rest = pl.ds(1, NODES - 1)
        pieces = [
            (2, ref.at[0, 1, :, 7], from_y.at[q, 0, 0]),
            (2, ref.at[1, 1, rest, 7], from_y.at[q, 0, 1, rest]),
            (3, ref.at[0, 0, :, 0], from_y.at[q, 1, 0]),
            (3, ref.at[1, 0, rest, 0], from_y.at[q, 1, 1, rest]),
            (4, ref.at[1, 1, 7, 7], from_edge.at[q, 0]),
            (5, ref.at[1, 0, 7, 0], from_edge.at[q, 1]),
            (6, ref.at[0, 1, 0, 7], from_edge.at[q, 2]),
            (7, ref.at[0, 0, 0, 0], from_edge.at[q, 3]),
            (0, ref.at[1, :, 7], from_x.at[q, 0]),
            (1, ref.at[0, :, 0], from_x.at[q, 1]),
        ]
        return [
            (
                way,
                pltpu.make_async_remote_copy(
                    src,
                    dst,
                    send_sem.at[q, n],
                    recv_sem.at[q, n],
                    device_id=(row + ways[way][0], col + ways[way][1]),
                    device_id_type=MESH,
                ),
            )
            for n, (way, src, dst) in enumerate(pieces)
        ]

    def send(q):
        for way, copy in transfers(q):
            pl.when(ways[way][2])(copy.start)

    def collect(q):
        copies = transfers(q)
        for way, copy in copies:
            pl.when(ways[way][2])(copy.wait_send)
        for way, copy in copies:
            pl.when(ways[way ^ 1 if way < 4 else 11 - way][2])(copy.wait_recv)
        ref = fields.at[q]
        for ey in range(2):
            for j in range(NODES):
                ref[0, ey, 0, j] = ref[0, ey, 0, j] + from_x[q, 0, ey, j]
                ref[1, ey, 7, j] = ref[1, ey, 7, j] + from_x[q, 1, ey, j]
        for ex in range(2):
            for i in range(NODES):
                at = (0, 7) if (ex, i) == (1, 0) else (ex, i)
                ref[ex, 0, i, 0] = ref[ex, 0, i, 0] + from_y[(q, 0) + at]
                ref[ex, 1, i, 7] = ref[ex, 1, i, 7] + from_y[(q, 1) + at]
        for corner in range(4):
            ex, ey = corner // 2, corner % 2
            at = (ex, ey, 7 * ex, 7 * ey)
            ref[at] = ref[at] + from_edge[q, corner]

    def clear(ref, there, pick):
        @pl.when(jnp.logical_not(there))
        def _():
            def body(q, carry):
                target = pick(ref, q)
                target[...] = jnp.zeros_like(target)
                return carry

            lax.fori_loop(0, FIELDS, body, 0)

    clear(from_x, has_down, lambda ref, q: ref.at[q, 0])
    clear(from_x, has_up, lambda ref, q: ref.at[q, 1])
    clear(from_y, has_left, lambda ref, q: ref.at[q, 0])
    clear(from_y, has_right, lambda ref, q: ref.at[q, 1])
    clear(from_edge, has_down & has_left, lambda ref, q: ref.at[q, 0])
    clear(from_edge, has_down & has_right, lambda ref, q: ref.at[q, 1])
    clear(from_edge, has_up & has_left, lambda ref, q: ref.at[q, 2])
    clear(from_edge, has_up & has_right, lambda ref, q: ref.at[q, 3])
    sums[...] = jnp.zeros_like(sums)

    flux_v = views(flux)
    flux_zv = views(flux_z)
    part_v = views(part_z)
    z0_v = views(z0)
    weighted_v = views(weighted)
    inverse_v = views(inverse)
    diag_v = views(fields.at[DIAG])

    pltpu.make_async_copy(flux, flux, in_sem.at[SOURCES]).wait()
    node = lax.broadcasted_iota(jnp.int32, (8, LANES), 0)
    lane = lax.broadcasted_iota(jnp.int32, (8, LANES), 1)
    weight_z = jnp.full((8, LANES), WEIGHTS[3], jnp.float32)
    for k in (0, 1, 2):
        ends = (node == k) | (node == 7 - k)
        weight_z = jnp.where(ends, jnp.float32(WEIGHTS[k]), weight_z)

    def diag_x(t, carry):
        for j, line in enumerate(lines_x(t)):
            values = [
                v * (weight_z * float(SCREENING * WEIGHTS[i] * WEIGHTS[j]))
                for i, v in enumerate(read(flux_v[0], line))
            ]
            write(flux_v[0], line, values)
            write(diag_v[0], line, [r + v for r, v in zip(square_back(values), values)])
        return carry

    def diag_yz(g, carry):
        for line, strip in zip(lines_y(g), lines_z(g)):
            before = read(diag_v[1], line)
            result_y = square_back(read(flux_v[1], line))
            values = read(flux_v[2], strip)
            write(flux_zv[1], line, values)
            write(part_v[2], strip, square_back(values))
            write(diag_v[1], line, [b + r for b, r in zip(before, result_y)])
        return carry

    def diag_sum(g, carry):
        for line in lines_y(g):
            both = zip(read(diag_v[1], line), read(part_v[1], line))
            write(diag_v[1], line, [b + r for b, r in both])
        return carry

    lax.fori_loop(0, 4, diag_x, 0)
    lax.fori_loop(0, 8, diag_yz, 0)
    lax.fori_loop(0, 8, diag_sum, 0)

    def prepare(n, carry):
        q = lax.rem(n + DIAG, DIAG + 1)

        @pl.when(n > 0)
        def _():
            pltpu.make_async_copy(fields.at[q], fields.at[q], in_sem.at[q]).wait()

        assemble_inside(fields.at[q])
        return carry

    lax.fori_loop(0, DIAG + 1, prepare, 0)

    def invert(g, carry):
        for line in lines_y(g):
            write(inverse_v[1], line, [1.0 / v for v in read(diag_v[1], line)])
        return carry

    lax.fori_loop(0, 8, invert, 0)

    def stiff(values, weight):
        return derive_back([g * w for g, w in zip(derive(values), weight)])

    def own_part(s):
        right_v = views(fields.at[s])
        image_v = views(fields.at[IMAGE + s])

        def scale(g, carry):
            for line in lines_y(g):
                both = zip(read(right_v[1], line), read(inverse_v[1], line))
                write(z0_v[1], line, [v * d for v, d in both])
            return carry

        lax.fori_loop(0, 8, scale, 0)
        empty = jnp.zeros((8, LANES), jnp.float32)
        for ex in range(2):
            for ey in range(2):
                for n in range(NODES):
                    z0[ex, ey, 7 * ex, n] = empty
                    z0[ex, ey, n, 7 * ey] = empty

        def stiff_x(t, carry):
            for line in lines_x(t):
                values, weight = read(z0_v[0], line), read(flux_v[0], line)
                result = stiff(values, weight)
                write(image_v[0], line, [r + w * v for r, w, v in zip(result, weight, values)])
            return carry

        def stiff_yz(g, carry):
            for line, strip in zip(lines_y(g), lines_z(g)):
                before = read(image_v[1], line)
                result_y = stiff(read(z0_v[1], line), read(flux_v[1], line))
                result_z = stiff(read(z0_v[2], strip), read(flux_zv[1], line))
                write(part_v[2], strip, result_z)
                write(image_v[1], line, [b + r for b, r in zip(before, result_y)])
            return carry

        def add_z(g, carry):
            for line in lines_y(g):
                both = zip(read(image_v[1], line), read(part_v[1], line))
                write(image_v[1], line, [a + b for a, b in both])
            return carry

        lax.fori_loop(0, 4, stiff_x, 0)
        lax.fori_loop(0, 8, stiff_yz, 0)
        lax.fori_loop(0, 8, add_z, 0)

    def send_first(n, carry):
        send(lax.rem(n + DIAG, DIAG + 1))
        return carry

    def begin(s, carry):
        @pl.when(s == 1)
        def _():
            pl.semaphore_wait(barrier, N_ROW - 1 + N_COL - 1 + corners)
            lax.fori_loop(0, DIAG + 1, send_first, 0)

        own_part(s)
        return carry

    lax.fori_loop(0, SOURCES, begin, 0)

    for side in range(2):
        end = 7 * side

        def lean(other, carry):
            for n in range(NODES):
                weight = [flux[side, other, a, n] for a in range(NODES)]
                result = derive_back([w * float(SLOPE[a, end]) for a, w in enumerate(weight)])
                result[end] = result[end] + weight[end]
                for i in range(NODES):
                    coef_x[side, other, i, n] = result[i]
                weight = [flux[other, side, n, b] for b in range(NODES)]
                result = derive_back([w * float(SLOPE[b, end]) for b, w in enumerate(weight)])
                for j in range(NODES):
                    coef_y[other, side, n, j] = result[j]
            return carry

        lax.fori_loop(0, 2, lean, 0)

    collect(DIAG)
    for ex in range(2):
        for ey in range(2):
            for n in range(NODES):
                for at in ((ex, ey, 7 * ex, n), (ex, ey, n, 7 * ey)):
                    inverse[at] = 1.0 / fields[(DIAG,) + at]

    face_v = views(z_face)[0]
    face_strip = z_face.reshape(4, NODES, NODES * NODES, LANES)
    face_flat = z_face.reshape(4, NODES**3, LANES)
    flux_flat = flux.reshape(4, NODES**3, LANES)
    coef_xv = views(coef_x)[0]
    coef_yv = views(coef_y)[0]

    def correct(s, carry):
        collect(s)
        for ex in range(2):
            for ey in range(2):
                for n in range(NODES):
                    for at in ((ex, ey, 7 * ex, n), (ex, ey, n, 7 * ey)):
                        z_face[at] = fields[(s,) + at] * inverse[at]
        target = fields.at[IMAGE + s]
        image_v = views(target)[0]
        image_strip = target.reshape(4, NODES, NODES * NODES, LANES)
        image_flat = target.reshape(4, NODES**3, LANES)

        def faces(t, carry):
            i0 = 7 * (t // 2)
            j0 = 7 * lax.rem(t, 2)
            nodes = range(NODES)
            values = [face_v[t, i, j0] for i in nodes]
            weight = [flux_v[0][t, i, j0] for i in nodes]
            result = stiff(values, weight)
            result = [r + w * v for r, w, v in zip(result, weight, values)]
            result_y = stiff([face_v[t, i0, j] for j in nodes], [flux_v[0][t, i0, j] for j in nodes])
            strips = [(t, i0, pl.ds(k, 8, stride=8)) for k in nodes]
            result_z = stiff(read(face_strip, strips), [flux_zv[0][t, i0, k] for k in nodes])
            columns = [(t, pl.ds(j0 * 8 + k, 8, stride=64)) for k in nodes]
            values = [jnp.where(node == i0, 0.0, v) for v in read(face_flat, columns)]
            result_c = stiff(values, read(flux_flat, columns))
            for at, r in zip(strips, result_z):
                image_strip[at] = image_strip[at] + r
            for at, r in zip(columns, result_c):
                image_flat[at] = image_flat[at] + r
            for i, r in zip(nodes, result):
                image_v[t, i, j0] = image_v[t, i, j0] + r
            for j, r in zip(nodes, result_y):
                image_v[t, i0, j] = image_v[t, i0, j] + r
            ends_x = [jnp.where(j0 == j, 0.0, face_v[t, i0, j]) for j in nodes]
            ends_y = [jnp.where(i0 == i, 0.0, face_v[t, i, j0]) for i in nodes]
            for i in nodes:
                for j in nodes:
                    more = coef_xv[t, i, j] * ends_x[j] + coef_yv[t, i, j] * ends_y[i]
                    image_v[t, i, j] = image_v[t, i, j] + more
            return carry

        lax.fori_loop(0, 4, faces, 0)
        assemble_inside(target)
        send(IMAGE + s)
        return carry

    lax.fori_loop(0, SOURCES, correct, 0)

    twice_z = ((node == 0) & (lane > 0)) | ((node == 7) & (lane < LANES - 1))
    share_z = jnp.where(twice_z, jnp.float32(0.5), jnp.float32(1.0))

    def share(g, carry):
        for line in lines_y(g):
            write(weighted_v[1], line, [v * share_z for v in read(inverse_v[1], line)])
        return carry

    lax.fori_loop(0, 8, share, 0)

    def part_of(there):
        return 0.5 if there is None else jnp.where(there, 0.5, 1.0).astype(jnp.float32)

    for there, ex, i in [(has_down, 0, 0), (None, 0, 7), (None, 1, 0), (has_up, 1, 7)]:
        for ey in range(2):
            weighted[ex, ey, i] = weighted[ex, ey, i] * part_of(there)
    for there, ey, j in [(has_left, 0, 0), (None, 0, 7), (None, 1, 0), (has_right, 1, 7)]:
        for ex in range(2):
            weighted[ex, ey, :, j] = weighted[ex, ey, :, j] * part_of(there)

    zero = jnp.zeros((8, LANES), jnp.float32)

    def settle(s, carry):
        collect(IMAGE + s)
        right_v = views(fields.at[s])[1]
        image_v = views(fields.at[IMAGE + s])[1]

        def products(g, carry):
            terms = [[], [], []]
            for line in lines_y(g):
                for at in line:
                    r, v, w = right_v[at], image_v[at], weighted_v[1][at]
                    rw = r * w
                    terms[0].append(r * rw)
                    terms[1].append(v * rw)
                    terms[2].append(v * (v * w))
            return tuple(c + tree_sum(t) for c, t in zip(carry, terms))

        totals = lax.fori_loop(0, 8, products, (zero, zero, zero))
        for n, total in enumerate(totals):
            sums[pl.ds(n * SOURCES + s, 1), :] = jnp.sum(total, axis=0, keepdims=True)
        return carry

    lax.fori_loop(0, SOURCES, settle, 0)

    def gather(stage, slots, mine, count, at, target):
        slots[at] = mine[...]
        copies = [
            pltpu.make_async_remote_copy(
                mine,
                slots.at[at],
                sum_send.at[stage],
                sum_recv.at[stage],
                device_id=target(lax.rem(at + step, count)),
                device_id_type=MESH,
            )
            for step in range(1, count)
        ]
        for copy in copies:
            copy.start()
        others = slots.at[pl.ds(0, count - 1)]
        pltpu.make_async_copy(others, others, sum_recv.at[stage]).wait()
        pltpu.make_async_copy(others, others, sum_send.at[stage]).wait()
        total = slots[0]
        for n in range(1, count):
            total = total + slots[n]
        return total

    total = jnp.sum(sums[...], axis=1, keepdims=True)
    node16 = lax.broadcasted_iota(jnp.int32, (16, LANES), 0)
    lane16 = lax.broadcasted_iota(jnp.int32, (16, LANES), 1)
    packed = jnp.where(node16 == lane16, jnp.broadcast_to(total, (16, LANES)), 0.0)
    part[0:1, :] = jnp.sum(packed, axis=0, keepdims=True)
    part[1:2, :] = gather(0, gather_row, part.at[0:1], N_ROW, row, lambda r: (r, col))
    total = gather(1, gather_col, part.at[1:2], N_COL, col, lambda c: (row, c))
    total = jnp.broadcast_to(total, (16, LANES))
    total = jnp.sum(jnp.where(node16 == lane16, total, 0.0), axis=1, keepdims=True)
    rz_first, curvature, square = total[0:4], total[4:8], total[8:12]
    alpha = rz_first / curvature
    rz_second = alpha * alpha * square - rz_first
    beta = rz_second / rz_first
    scalars[0:4, :] = jnp.broadcast_to(alpha, (4, LANES))
    scalars[4:8, :] = jnp.broadcast_to(beta, (4, LANES))


SLOTS = 8


def update_kernel(fields, inverse, scalars, first, second, third, staging, sem):
    outputs = (first, second, third)

    def copies(n):
        return [
            pltpu.make_async_copy(
                staging.at[n % SLOTS, q], outputs[q].at[n // NODES, n % NODES], sem.at[n % SLOTS, q]
            )
            for q in range(3)
        ]

    def step(n, carry):
        s, i, slot = n // NODES, n % NODES, n % SLOTS

        @pl.when(n >= SLOTS)
        def _():
            for copy in copies(n - SLOTS):
                copy.wait()

        alpha = jnp.broadcast_to(scalars[pl.ds(s, 1), :], (8, LANES))
        beta = jnp.broadcast_to(scalars[pl.ds(s + 4, 1), :], (8, LANES))
        for ex in range(2):
            for ey in range(2):
                lanes = pl.ds((ex * 2 + ey) * LANES, LANES)
                for j in range(NODES):
                    right = fields[s, ex, ey, i, j]
                    inv = inverse[ex, ey, i, j]
                    rest = right - alpha * fields[IMAGE + s, ex, ey, i, j]
                    staging[slot, 0, j, :, lanes] = alpha * (right * inv)
                    staging[slot, 1, j, :, lanes] = rest
                    staging[slot, 2, j, :, lanes] = (rest + beta * right) * inv
        for copy in copies(n):
            copy.start()
        return carry

    steps = SOURCES * NODES
    lax.fori_loop(0, steps, step, 0)
    for n in range(steps - SLOTS, steps):
        for copy in copies(n):
            copy.wait()


def per_device(loads, conduct):
    f32 = jnp.float32
    vmem = pltpu.VMEM
    whole = pl.BlockSpec(memory_space=vmem)
    results = pl.pallas_call(
        solve_kernel,
        out_shape=[vmem((FIELDS,) + FIELD, f32), vmem(FIELD, f32), vmem((8, LANES), f32)],
        in_specs=[pl.BlockSpec(memory_space=pl.ANY)] * 2,
        out_specs=[whole] * 3,
        scratch_shapes=[vmem(FIELD, f32)] * 8
        + [
            vmem((FIELDS, 2, 2, NODES, NODES, LANES), f32),
            vmem((FIELDS, 2, 2, NODES, NODES, LANES), f32),
            vmem((FIELDS, 4, NODES, LANES), f32),
            vmem((16, LANES), f32),
            vmem((8, LANES), f32),
            vmem((N_ROW, 1, LANES), f32),
            vmem((N_COL, 1, LANES), f32),
            pltpu.SemaphoreType.DMA((SOURCES + 1,)),
            pltpu.SemaphoreType.DMA((FIELDS, 10)),
            pltpu.SemaphoreType.DMA((FIELDS, 10)),
            pltpu.SemaphoreType.DMA((2,)),
            pltpu.SemaphoreType.DMA((2,)),
        ],
        compiler_params=pltpu.CompilerParams(
            collective_id=0, has_side_effects=True, vmem_limit_bytes=40 * 1024 * 1024
        ),
    )(*[pltpu.with_memory_space_constraint(x, pltpu.HBM) for x in (loads, conduct)])
    shape = (SOURCES, NODES, NODES, NODES, 4 * LANES)
    return pl.pallas_call(
        update_kernel,
        out_shape=[jax.ShapeDtypeStruct(shape, f32)] * 3,
        in_specs=[whole] * 3,
        out_specs=[pl.BlockSpec(memory_space=pl.ANY)] * 3,
        scratch_shapes=[
            vmem((SLOTS, 3, NODES, NODES, 4 * LANES), f32),
            pltpu.SemaphoreType.DMA((SLOTS, 3)),
        ],
        compiler_params=pltpu.CompilerParams(vmem_limit_bytes=16 * 1024 * 1024),
    )(*[pltpu.with_memory_space_constraint(x, vmem) for x in results])


def solution(mesh):
    in_specs = (P(None, None, None, None, ("row", "col")), P(None, None, None, ("row", "col")))
    out = P(None, None, None, None, ("row", "col"))
    return jax.shard_map(
        per_device, mesh=mesh, in_specs=in_specs, out_specs=(out, out, out), check_vma=False
    )
```

```python
import functools

import jax
import jax.numpy as jnp
import numpy as np
from jax import lax
from jax.experimental import pallas as pl
from jax.experimental.pallas import tpu as pltpu
from jax.sharding import PartitionSpec as P

NODES = 8
SOURCES = 4
LANES = 128
N_ROW = 8
N_COL = 16
SCREENING = 0.5
GLL_INNER = [
    -0.8717401485096066,
    -0.5917001814331423,
    -0.2092992179024789,
    0.2092992179024789,
    0.5917001814331423,
    0.8717401485096066,
]
MESH = pl.DeviceIdType.MESH
FIELD = (2, 2, NODES, NODES, NODES, LANES)


def gll_tables():
    degree = NODES - 1
    points = np.array([-1.0] + GLL_INNER + [1.0])
    previous = points * 0.0 + 1.0
    current = points * 1.0
    for order in range(1, degree):
        following = ((2 * order + 1) * points * current - order * previous) / (order + 1)
        previous = current
        current = following
    weights = 2.0 / (degree * (degree + 1) * current**2)
    spread = points[:, None] - points[None, :]
    index_ids = np.arange(NODES)
    same = index_ids[:, None] == index_ids[None, :]
    safe_spread = np.where(same, 1.0, spread)
    deriv = np.where(same, 0.0, current[:, None] / (current[None, :] * safe_spread))
    corner = degree * (degree + 1) / 4.0
    ends = np.where(index_ids == 0, -corner, np.where(index_ids == degree, corner, 0.0))
    deriv = deriv + np.where(same, ends[None, :], 0.0)
    return deriv, weights


DERIV, WEIGHTS = gll_tables()
SQUARE = DERIV * DERIV
HALF = NODES // 2


def halves(table):
    mirrored = table[:HALF, ::-1][:, :HALF]
    direct = table[:HALF, :HALF]
    plus = (direct + mirrored) / 2.0
    minus = (direct - mirrored) / 2.0
    return plus.tolist(), minus.tolist()


SLOPE = DERIV * np.sqrt(2.0)
D_PLUS, D_MINUS = halves(SLOPE)
Q_PLUS, Q_MINUS = halves(SQUARE * 2.0)


def fold(values):
    plus = [values[i] + values[7 - i] for i in range(HALF)]
    minus = [values[i] - values[7 - i] for i in range(HALF)]
    return plus, minus


def combine(table, values, transposed):
    out = []
    for a in range(HALF):
        total = None
        for i in range(HALF):
            factor = table[i][a] if transposed else table[a][i]
            term = values[i] * factor
            total = term if total is None else total + term
        out.append(total)
    return out


def unfold(base, turn):
    low = [base[a] + turn[a] for a in range(HALF)]
    high = [base[a] - turn[a] for a in range(HALF)]
    return low + high[::-1]


def derive(values):
    plus, minus = fold(values)
    return unfold(combine(D_MINUS, minus, False), combine(D_PLUS, plus, False))


def derive_back(values):
    plus, minus = fold(values)
    return unfold(combine(D_PLUS, minus, True), combine(D_MINUS, plus, True))


def square_back(values):
    plus, minus = fold(values)
    return unfold(combine(Q_PLUS, plus, True), combine(Q_MINUS, minus, True))


def tree_sum(terms):
    while len(terms) > 1:
        terms = [a + b for a, b in zip(terms[::2], terms[1::2])]
    return terms[0]


def lines_x(t):
    return [[(t, i, j) for i in range(NODES)] for j in range(NODES)]


def lines_y(g):
    return [[(g, u, j) for j in range(NODES)] for u in range(4)]


def lines_z(g):
    return [[(g, u, pl.ds(k, 8, stride=8)) for k in range(NODES)] for u in range(4)]


def views(ref):
    along_x = ref.reshape(4, NODES, NODES, NODES, LANES)
    along_y = ref.reshape(8, 4, NODES, NODES, LANES)
    along_z = ref.reshape(8, 4, NODES * NODES, LANES)
    return along_x, along_y, along_z


def read(ref, line):
    return [ref[at] for at in line]


def write(ref, line, values):
    for at, value in zip(line, values):
        ref[at] = value


def sum_z(first, last):
    lane = lax.broadcasted_iota(jnp.int32, (8, LANES), 1)
    after = jnp.where(lane < LANES - 1, pltpu.roll(first, LANES - 1, 1), 0.0)
    before = jnp.where(lane > 0, pltpu.roll(last, 1, 1), 0.0)
    return first + before, last + after


def assemble_inside(ref):
    for ey in range(2):
        for j in range(NODES):
            both = ref[0, ey, 7, j] + ref[1, ey, 0, j]
            ref[0, ey, 7, j] = both
            ref[1, ey, 0, j] = both
    for ex in range(2):
        for i in range(NODES):
            both = ref[ex, 0, i, 7] + ref[ex, 1, i, 0]
            ref[ex, 0, i, 7] = both
            ref[ex, 1, i, 0] = both
    strips = views(ref)[2]

    def along_z(g, carry):
        lines = [line for u in range(4) for line in lines_z(g * 4 + u)]
        ends = [(strips[line[0]], strips[line[7]]) for line in lines]
        ends = [sum_z(first, last) for first, last in ends]
        for line, (first, last) in zip(lines, ends):
            strips[line[0]] = first
            strips[line[7]] = last
        return carry

    lax.fori_loop(0, 2, along_z, 0)


DIAG = SOURCES
IMAGE = SOURCES + 1
FIELDS = 2 * SOURCES + 1


def solve_kernel(
    loads,
    conduct,
    fields,
    inverse,
    scalars,
    flux,
    flux_z,
    part_z,
    z0,
    z_face,
    coef_x,
    coef_y,
    weighted,
    from_x,
    from_y,
    from_edge,
    sums,
    part,
    gather_row,
    gather_col,
    in_sem,
    send_sem,
    recv_sem,
    sum_send,
    sum_recv,
):
    row = lax.axis_index("row")
    col = lax.axis_index("col")
    for ex in range(2):
        for ey in range(2):
            lanes = pl.ds((ex * 2 + ey) * LANES, LANES)
            pltpu.make_async_copy(
                conduct.at[:, :, :, lanes], flux.at[ex, ey], in_sem.at[SOURCES]
            ).start()
    for s in range(SOURCES):
        for ex in range(2):
            for ey in range(2):
                lanes = pl.ds((ex * 2 + ey) * LANES, LANES)
                pltpu.make_async_copy(
                    loads.at[s, :, :, :, lanes], fields.at[s, ex, ey], in_sem.at[s]
                ).start()

    has_up, has_down = row < N_ROW - 1, row > 0
    has_right, has_left = col < N_COL - 1, col > 0
    ways = [
        (1, 0, has_up),
        (-1, 0, has_down),
        (0, 1, has_right),
        (0, -1, has_left),
        (1, 1, has_up & has_right),
        (1, -1, has_up & has_left),
        (-1, 1, has_down & has_right),
        (-1, -1, has_down & has_left),
    ]
    sides_x = has_up.astype(jnp.int32) + has_down.astype(jnp.int32)
    sides_y = has_right.astype(jnp.int32) + has_left.astype(jnp.int32)
    barrier = pltpu.get_barrier_semaphore()
    corners = 0
    for dr, dc, there in ways[4:]:

        @pl.when(there)
        def _():
            pl.semaphore_signal(barrier, 1, device_id=(row + dr, col + dc), device_id_type=MESH)

        corners = corners + there.astype(jnp.int32)
    for step in range(1, N_COL):
        pl.semaphore_signal(
            barrier, 1, device_id=(row, lax.rem(col + step, N_COL)), device_id_type=MESH
        )
    for step in range(1, N_ROW):
        pl.semaphore_signal(
            barrier, 1, device_id=(lax.rem(row + step, N_ROW), col), device_id_type=MESH
        )

    def transfers(q):
        ref = fields.at[q]
        rest = pl.ds(1, NODES - 1)
        pieces = [
            (2, ref.at[0, 1, :, 7], from_y.at[q, 0, 0]),
            (2, ref.at[1, 1, rest, 7], from_y.at[q, 0, 1, rest]),
            (3, ref.at[0, 0, :, 0], from_y.at[q, 1, 0]),
            (3, ref.at[1, 0, rest, 0], from_y.at[q, 1, 1, rest]),
            (4, ref.at[1, 1, 7, 7], from_edge.at[q, 0]),
            (5, ref.at[1, 0, 7, 0], from_edge.at[q, 1]),
            (6, ref.at[0, 1, 0, 7], from_edge.at[q, 2]),
            (7, ref.at[0, 0, 0, 0], from_edge.at[q, 3]),
            (0, ref.at[1, :, 7], from_x.at[q, 0]),
            (1, ref.at[0, :, 0], from_x.at[q, 1]),
        ]
        return [
            (
                way,
                pltpu.make_async_remote_copy(
                    src,
                    dst,
                    send_sem.at[q],
                    recv_sem.at[q],
                    device_id=(row + ways[way][0], col + ways[way][1]),
                    device_id_type=MESH,
                ),
            )
            for way, src, dst in pieces
        ]

    def send(q):
        for way, copy in transfers(q):
            pl.when(ways[way][2])(copy.start)

    def collect(q):
        ref = fields.at[q]
        tiles = ref.reshape(4 * NODES * NODES, NODES, LANES)
        for across in (1, 2):
            for along in (1, 2):

                @pl.when((sides_x == across) & (sides_y == along))
                def _():
                    size = tiles.at[pl.ds(0, 16 * across + 15 * along + across * along)]
                    pltpu.make_async_copy(size, size, send_sem.at[q]).wait()
                    pltpu.make_async_copy(size, size, recv_sem.at[q]).wait()

        for ey in range(2):
            for j in range(NODES):
                ref[0, ey, 0, j] = ref[0, ey, 0, j] + from_x[q, 0, ey, j]
                ref[1, ey, 7, j] = ref[1, ey, 7, j] + from_x[q, 1, ey, j]
        for ex in range(2):
            for i in range(NODES):
                at = (0, 7) if (ex, i) == (1, 0) else (ex, i)
                ref[ex, 0, i, 0] = ref[ex, 0, i, 0] + from_y[(q, 0) + at]
                ref[ex, 1, i, 7] = ref[ex, 1, i, 7] + from_y[(q, 1) + at]
        for corner in range(4):
            ex, ey = corner // 2, corner % 2
            at = (ex, ey, 7 * ex, 7 * ey)
            ref[at] = ref[at] + from_edge[q, corner]

    def clear(ref, there, pick):
        @pl.when(jnp.logical_not(there))
        def _():
            def body(q, carry):
                target = pick(ref, q)
                target[...] = jnp.zeros_like(target)
                return carry

            lax.fori_loop(0, FIELDS, body, 0)

    clear(from_x, has_down, lambda ref, q: ref.at[q, 0])
    clear(from_x, has_up, lambda ref, q: ref.at[q, 1])
    clear(from_y, has_left, lambda ref, q: ref.at[q, 0])
    clear(from_y, has_right, lambda ref, q: ref.at[q, 1])
    clear(from_edge, has_down & has_left, lambda ref, q: ref.at[q, 0])
    clear(from_edge, has_down & has_right, lambda ref, q: ref.at[q, 1])
    clear(from_edge, has_up & has_left, lambda ref, q: ref.at[q, 2])
    clear(from_edge, has_up & has_right, lambda ref, q: ref.at[q, 3])
    sums[...] = jnp.zeros_like(sums)

    flux_v = views(flux)
    flux_zv = views(flux_z)
    part_v = views(part_z)
    z0_v = views(z0)
    weighted_v = views(weighted)
    inverse_v = views(inverse)
    diag_v = views(fields.at[DIAG])

    pltpu.make_async_copy(flux, flux, in_sem.at[SOURCES]).wait()
    node = lax.broadcasted_iota(jnp.int32, (8, LANES), 0)
    lane = lax.broadcasted_iota(jnp.int32, (8, LANES), 1)
    weight_z = jnp.full((8, LANES), WEIGHTS[3], jnp.float32)
    for k in (0, 1, 2):
        ends = (node == k) | (node == 7 - k)
        weight_z = jnp.where(ends, jnp.float32(WEIGHTS[k]), weight_z)

    def diag_x(t, carry):
        for j, line in enumerate(lines_x(t)):
            values = [
                v * (weight_z * float(SCREENING * WEIGHTS[i] * WEIGHTS[j]))
                for i, v in enumerate(read(flux_v[0], line))
            ]
            write(flux_v[0], line, values)
            write(diag_v[0], line, [r + v for r, v in zip(square_back(values), values)])
        return carry

    def diag_yz(g, carry):
        for line, strip in zip(lines_y(g), lines_z(g)):
            before = read(diag_v[1], line)
            result_y = square_back(read(flux_v[1], line))
            values = read(flux_v[2], strip)
            write(flux_zv[1], line, values)
            write(part_v[2], strip, square_back(values))
            write(diag_v[1], line, [b + r for b, r in zip(before, result_y)])
        return carry

    def diag_sum(g, carry):
        for line in lines_y(g):
            both = zip(read(diag_v[1], line), read(part_v[1], line))
            write(diag_v[1], line, [b + r for b, r in both])
        return carry

    lax.fori_loop(0, 4, diag_x, 0)
    lax.fori_loop(0, 8, diag_yz, 0)
    lax.fori_loop(0, 8, diag_sum, 0)

    def prepare(n, carry):
        q = lax.rem(n + DIAG, DIAG + 1)

        @pl.when(n > 0)
        def _():
            pltpu.make_async_copy(fields.at[q], fields.at[q], in_sem.at[q]).wait()

        assemble_inside(fields.at[q])
        return carry

    lax.fori_loop(0, DIAG + 1, prepare, 0)

    def invert(g, carry):
        for line in lines_y(g):
            write(inverse_v[1], line, [1.0 / v for v in read(diag_v[1], line)])
        return carry

    z0_strip = z0.reshape(4, NODES, NODES * NODES, LANES)
    part_strip = part_z.reshape(4, NODES, NODES * NODES, LANES)

    def stiff(values, weight):
        return derive_back([g * w for g, w in zip(derive(values), weight)])

    def own_part(s):
        right_v = views(fields.at[s])
        image_v = views(fields.at[IMAGE + s])

        def scale(g, carry):
            for line in lines_y(g):
                both = zip(read(right_v[1], line), read(inverse_v[1], line))
                write(z0_v[1], line, [v * d for v, d in both])
            return carry

        lax.fori_loop(0, 8, scale, 0)
        empty = jnp.zeros((8, LANES), jnp.float32)
        for ex in range(2):
            for ey in range(2):
                for n in range(NODES):
                    z0[ex, ey, 7 * ex, n] = empty
                    z0[ex, ey, n, 7 * ey] = empty

        def stiff_z(t, carry):
            planes = pl.ds(1 - t // 2, NODES - 1)
            values, weight = z0_strip.at[t, planes], flux_zv[0].at[t, planes]
            result = part_strip.at[t, planes]
            for u in range(NODES - 1):
                strips = [(u, pl.ds(k, 8, stride=8)) for k in range(NODES)]
                out = stiff(read(values, strips), [weight[u, k] for k in range(NODES)])
                write(result, strips, out)
            return carry

        def stiff_x(t, carry):
            end = lax.rem(t, 2)
            lines = pl.ds(1 - end, NODES - 1)
            values, weight = z0_v[0].at[t, :, lines], flux_v[0].at[t, :, lines]
            result = image_v[0].at[t, :, lines]
            for n in range(NODES - 1):
                line = [(i, n) for i in range(NODES)]
                v, w = read(values, line), read(weight, line)
                out = stiff(v, w)
                write(result, line, [r + b * a for r, b, a in zip(out, w, v)])
            for i in range(NODES):
                image_v[0][t, i, 7 * end] = empty
            return carry

        def stiff_y(t, carry):
            planes = pl.ds(1 - t // 2, NODES - 1)
            values, weight = z0_v[0].at[t, planes], flux_v[0].at[t, planes]
            result, other = image_v[0].at[t, planes], part_v[0].at[t, planes]
            for u in range(NODES - 1):
                line = [(u, j) for j in range(NODES)]
                out = stiff(read(values, line), read(weight, line))
                before = zip(read(result, line), read(other, line), out)
                write(result, line, [a + b + r for a, b, r in before])
            return carry

        lax.fori_loop(0, 4, stiff_z, 0)
        lax.fori_loop(0, 4, stiff_x, 0)
        lax.fori_loop(0, 4, stiff_y, 0)

    def send_first(n, carry):
        send(lax.rem(n + DIAG, DIAG + 1))
        return carry

    pl.semaphore_wait(barrier, N_ROW - 1 + N_COL - 1 + corners)
    lax.fori_loop(0, DIAG + 1, send_first, 0)
    lax.fori_loop(0, 8, invert, 0)

    def begin(s, carry):
        own_part(s)
        return carry

    lax.fori_loop(0, SOURCES, begin, 0)

    for side in range(2):
        end = 7 * side

        def lean(other, carry):
            for n in range(NODES):
                weight = [flux[side, other, a, n] for a in range(NODES)]
                result = derive_back([w * float(SLOPE[a, end]) for a, w in enumerate(weight)])
                result[end] = result[end] + weight[end]
                for i in range(NODES):
                    coef_x[side, other, i, n] = result[i]
                weight = [flux[other, side, n, b] for b in range(NODES)]
                result = derive_back([w * float(SLOPE[b, end]) for b, w in enumerate(weight)])
                for j in range(NODES):
                    coef_y[other, side, n, j] = result[j]
            return carry

        lax.fori_loop(0, 2, lean, 0)

    collect(DIAG)
    for ex in range(2):
        for ey in range(2):
            for n in range(NODES):
                for at in ((ex, ey, 7 * ex, n), (ex, ey, n, 7 * ey)):
                    inverse[at] = 1.0 / fields[(DIAG,) + at]

    face_v = views(z_face)[0]
    face_strip = z_face.reshape(4, NODES, NODES * NODES, LANES)
    face_flat = z_face.reshape(4, NODES**3, LANES)
    flux_flat = flux.reshape(4, NODES**3, LANES)
    coef_xv = views(coef_x)[0]
    coef_yv = views(coef_y)[0]

    def correct(s, carry):
        collect(s)
        for ex in range(2):
            for ey in range(2):
                for n in range(NODES):
                    for at in ((ex, ey, 7 * ex, n), (ex, ey, n, 7 * ey)):
                        z_face[at] = fields[(s,) + at] * inverse[at]
        target = fields.at[IMAGE + s]
        image_v = views(target)[0]
        image_strip = target.reshape(4, NODES, NODES * NODES, LANES)
        image_flat = target.reshape(4, NODES**3, LANES)

        def faces(t, carry):
            i0 = 7 * (t // 2)
            j0 = 7 * lax.rem(t, 2)
            nodes = range(NODES)
            values = [face_v[t, i, j0] for i in nodes]
            weight = [flux_v[0][t, i, j0] for i in nodes]
            result = stiff(values, weight)
            result = [r + w * v for r, w, v in zip(result, weight, values)]
            result_y = stiff([face_v[t, i0, j] for j in nodes], [flux_v[0][t, i0, j] for j in nodes])
            strips = [(t, i0, pl.ds(k, 8, stride=8)) for k in nodes]
            result_z = stiff(read(face_strip, strips), [flux_zv[0][t, i0, k] for k in nodes])
            columns = [(t, pl.ds(j0 * 8 + k, 8, stride=64)) for k in nodes]
            values = [jnp.where(node == i0, 0.0, v) for v in read(face_flat, columns)]
            result_c = stiff(values, read(flux_flat, columns))
            for at, r in zip(strips, result_z):
                image_strip[at] = image_strip[at] + r
            for at, r in zip(columns, result_c):
                image_flat[at] = image_flat[at] + r
            for i, r in zip(nodes, result):
                image_v[t, i, j0] = image_v[t, i, j0] + r
            for j, r in zip(nodes, result_y):
                image_v[t, i0, j] = image_v[t, i0, j] + r
            ends_x = [jnp.where(j0 == j, 0.0, face_v[t, i0, j]) for j in nodes]
            ends_y = [jnp.where(i0 == i, 0.0, face_v[t, i, j0]) for i in nodes]
            for i in nodes:
                for j in nodes:
                    more = coef_xv[t, i, j] * ends_x[j] + coef_yv[t, i, j] * ends_y[i]
                    image_v[t, i, j] = image_v[t, i, j] + more
            return carry

        lax.fori_loop(0, 4, faces, 0)
        assemble_inside(target)
        send(IMAGE + s)
        return carry

    lax.fori_loop(0, SOURCES, correct, 0)

    twice_z = ((node == 0) & (lane > 0)) | ((node == 7) & (lane < LANES - 1))
    share_z = jnp.where(twice_z, jnp.float32(0.5), jnp.float32(1.0))

    def share(g, carry):
        for line in lines_y(g):
            write(weighted_v[1], line, [v * share_z for v in read(inverse_v[1], line)])
        return carry

    lax.fori_loop(0, 8, share, 0)

    def part_of(there):
        return 0.5 if there is None else jnp.where(there, 0.5, 1.0).astype(jnp.float32)

    for there, ex, i in [(has_down, 0, 0), (None, 0, 7), (None, 1, 0), (has_up, 1, 7)]:
        for ey in range(2):
            weighted[ex, ey, i] = weighted[ex, ey, i] * part_of(there)
    for there, ey, j in [(has_left, 0, 0), (None, 0, 7), (None, 1, 0), (has_right, 1, 7)]:
        for ex in range(2):
            weighted[ex, ey, :, j] = weighted[ex, ey, :, j] * part_of(there)

    zero = jnp.zeros((8, LANES), jnp.float32)

    def settle(s, carry):
        collect(IMAGE + s)
        right_v = views(fields.at[s])[1]
        image_v = views(fields.at[IMAGE + s])[1]

        def products(g, carry):
            terms = [[], [], []]
            for line in lines_y(g):
                for at in line:
                    r, v, w = right_v[at], image_v[at], weighted_v[1][at]
                    rw = r * w
                    terms[0].append(r * rw)
                    terms[1].append(v * rw)
                    terms[2].append(v * (v * w))
            return tuple(c + tree_sum(t) for c, t in zip(carry, terms))

        totals = lax.fori_loop(0, 8, products, (zero, zero, zero))
        for n, total in enumerate(totals):
            sums[pl.ds(n * SOURCES + s, 1), :] = jnp.sum(total, axis=0, keepdims=True)
        return carry

    lax.fori_loop(0, SOURCES, settle, 0)

    def gather(stage, slots, mine, count, at, target):
        slots[at] = mine[...]
        copies = [
            pltpu.make_async_remote_copy(
                mine,
                slots.at[at],
                sum_send.at[stage],
                sum_recv.at[stage],
                device_id=target(lax.rem(at + step, count)),
                device_id_type=MESH,
            )
            for step in range(1, count)
        ]
        for copy in copies:
            copy.start()
        others = slots.at[pl.ds(0, count - 1)]
        pltpu.make_async_copy(others, others, sum_recv.at[stage]).wait()
        pltpu.make_async_copy(others, others, sum_send.at[stage]).wait()
        total = slots[0]
        for n in range(1, count):
            total = total + slots[n]
        return total

    total = jnp.sum(sums[...], axis=1, keepdims=True)
    node16 = lax.broadcasted_iota(jnp.int32, (16, LANES), 0)
    lane16 = lax.broadcasted_iota(jnp.int32, (16, LANES), 1)
    packed = jnp.where(node16 == lane16, jnp.broadcast_to(total, (16, LANES)), 0.0)
    part[0:1, :] = jnp.sum(packed, axis=0, keepdims=True)
    part[1:2, :] = gather(0, gather_row, part.at[0:1], N_ROW, row, lambda r: (r, col))
    total = gather(1, gather_col, part.at[1:2], N_COL, col, lambda c: (row, c))
    total = jnp.broadcast_to(total, (16, LANES))
    total = jnp.sum(jnp.where(node16 == lane16, total, 0.0), axis=1, keepdims=True)
    rz_first, curvature, square = total[0:4], total[4:8], total[8:12]
    alpha = rz_first / curvature
    rz_second = alpha * alpha * square - rz_first
    beta = rz_second / rz_first
    scalars[0:4, :] = jnp.broadcast_to(alpha, (4, LANES))
    scalars[4:8, :] = jnp.broadcast_to(beta, (4, LANES))


SLOTS = 8


def update_kernel(fields, inverse, scalars, first, second, third, staging, sem):
    outputs = (first, second, third)

    def copies(n):
        return [
            pltpu.make_async_copy(
                staging.at[n % SLOTS, q], outputs[q].at[n // NODES, n % NODES], sem.at[n % SLOTS]
            )
            for q in range(3)
        ]

    def await_slot(slot):
        pltpu.make_async_copy(staging.at[slot], staging.at[slot], sem.at[slot]).wait()

    def step(n, carry):
        s, i, slot = n // NODES, n % NODES, n % SLOTS

        @pl.when(n >= SLOTS)
        def _():
            await_slot(slot)

        alpha = jnp.broadcast_to(scalars[pl.ds(s, 1), :], (8, LANES))
        beta = jnp.broadcast_to(scalars[pl.ds(s + 4, 1), :], (8, LANES))
        for ex in range(2):
            for ey in range(2):
                lanes = pl.ds((ex * 2 + ey) * LANES, LANES)
                for j in range(NODES):
                    right = fields[s, ex, ey, i, j]
                    inv = inverse[ex, ey, i, j]
                    rest = right - alpha * fields[IMAGE + s, ex, ey, i, j]
                    staging[slot, 0, j, :, lanes] = alpha * (right * inv)
                    staging[slot, 1, j, :, lanes] = rest
                    staging[slot, 2, j, :, lanes] = (rest + beta * right) * inv
        for copy in copies(n):
            copy.start()
        return carry

    steps = SOURCES * NODES
    lax.fori_loop(0, steps, step, 0)
    for n in range(steps - SLOTS, steps):
        await_slot(n % SLOTS)


def per_device(loads, conduct):
    f32 = jnp.float32
    vmem = pltpu.VMEM
    whole = pl.BlockSpec(memory_space=vmem)
    results = pl.pallas_call(
        solve_kernel,
        out_shape=[vmem((FIELDS,) + FIELD, f32), vmem(FIELD, f32), vmem((8, LANES), f32)],
        in_specs=[pl.BlockSpec(memory_space=pl.ANY)] * 2,
        out_specs=[whole] * 3,
        scratch_shapes=[vmem(FIELD, f32)] * 8
        + [
            vmem((FIELDS, 2, 2, NODES, NODES, LANES), f32),
            vmem((FIELDS, 2, 2, NODES, NODES, LANES), f32),
            vmem((FIELDS, 4, NODES, LANES), f32),
            vmem((16, LANES), f32),
            vmem((8, LANES), f32),
            vmem((N_ROW, 1, LANES), f32),
            vmem((N_COL, 1, LANES), f32),
            pltpu.SemaphoreType.DMA((SOURCES + 1,)),
            pltpu.SemaphoreType.DMA((FIELDS,)),
            pltpu.SemaphoreType.DMA((FIELDS,)),
            pltpu.SemaphoreType.DMA((2,)),
            pltpu.SemaphoreType.DMA((2,)),
        ],
        compiler_params=pltpu.CompilerParams(
            collective_id=0, has_side_effects=True, vmem_limit_bytes=40 * 1024 * 1024
        ),
    )(*[pltpu.with_memory_space_constraint(x, pltpu.HBM) for x in (loads, conduct)])
    shape = (SOURCES, NODES, NODES, NODES, 4 * LANES)
    return pl.pallas_call(
        update_kernel,
        out_shape=[jax.ShapeDtypeStruct(shape, f32)] * 3,
        in_specs=[whole] * 3,
        out_specs=[pl.BlockSpec(memory_space=pl.ANY)] * 3,
        scratch_shapes=[
            vmem((SLOTS, 3, NODES, NODES, 4 * LANES), f32),
            pltpu.SemaphoreType.DMA((SLOTS,)),
        ],
        compiler_params=pltpu.CompilerParams(vmem_limit_bytes=16 * 1024 * 1024),
    )(*[pltpu.with_memory_space_constraint(x, vmem) for x in results])


def solution(mesh):
    in_specs = (P(None, None, None, None, ("row", "col")), P(None, None, None, ("row", "col")))
    out = P(None, None, None, None, ("row", "col"))
    return jax.shard_map(
        per_device, mesh=mesh, in_specs=in_specs, out_specs=(out, out, out), check_vma=False
    )
```

```python
import functools

import jax
import jax.numpy as jnp
import numpy as np
from jax import lax
from jax.experimental import pallas as pl
from jax.experimental.pallas import tpu as pltpu
from jax.sharding import PartitionSpec as P

NODES = 8
SOURCES = 4
LANES = 128
N_ROW = 8
N_COL = 16
SCREENING = 0.5
GLL_INNER = [
    -0.8717401485096066,
    -0.5917001814331423,
    -0.2092992179024789,
    0.2092992179024789,
    0.5917001814331423,
    0.8717401485096066,
]
MESH = pl.DeviceIdType.MESH
FIELD = (2, 2, NODES, NODES, NODES, LANES)


def gll_tables():
    degree = NODES - 1
    points = np.array([-1.0] + GLL_INNER + [1.0])
    previous = points * 0.0 + 1.0
    current = points * 1.0
    for order in range(1, degree):
        following = ((2 * order + 1) * points * current - order * previous) / (order + 1)
        previous = current
        current = following
    weights = 2.0 / (degree * (degree + 1) * current**2)
    spread = points[:, None] - points[None, :]
    index_ids = np.arange(NODES)
    same = index_ids[:, None] == index_ids[None, :]
    safe_spread = np.where(same, 1.0, spread)
    deriv = np.where(same, 0.0, current[:, None] / (current[None, :] * safe_spread))
    corner = degree * (degree + 1) / 4.0
    ends = np.where(index_ids == 0, -corner, np.where(index_ids == degree, corner, 0.0))
    deriv = deriv + np.where(same, ends[None, :], 0.0)
    return deriv, weights


DERIV, WEIGHTS = gll_tables()
SQUARE = DERIV * DERIV
HALF = NODES // 2


def halves(table):
    mirrored = table[:HALF, ::-1][:, :HALF]
    direct = table[:HALF, :HALF]
    plus = (direct + mirrored) / 2.0
    minus = (direct - mirrored) / 2.0
    return plus.tolist(), minus.tolist()


SLOPE = DERIV * np.sqrt(2.0)
D_PLUS, D_MINUS = halves(SLOPE)
Q_PLUS, Q_MINUS = halves(SQUARE * 2.0)


def fold(values):
    plus = [values[i] + values[7 - i] for i in range(HALF)]
    minus = [values[i] - values[7 - i] for i in range(HALF)]
    return plus, minus


def combine(table, values, transposed):
    out = []
    for a in range(HALF):
        total = None
        for i in range(HALF):
            factor = table[i][a] if transposed else table[a][i]
            term = values[i] * factor
            total = term if total is None else total + term
        out.append(total)
    return out


def unfold(base, turn):
    low = [base[a] + turn[a] for a in range(HALF)]
    high = [base[a] - turn[a] for a in range(HALF)]
    return low + high[::-1]


def derive(values):
    plus, minus = fold(values)
    return unfold(combine(D_MINUS, minus, False), combine(D_PLUS, plus, False))


def derive_back(values):
    plus, minus = fold(values)
    return unfold(combine(D_PLUS, minus, True), combine(D_MINUS, plus, True))


def square_back(values):
    plus, minus = fold(values)
    return unfold(combine(Q_PLUS, plus, True), combine(Q_MINUS, minus, True))


def tree_sum(terms):
    while len(terms) > 1:
        terms = [a + b for a, b in zip(terms[::2], terms[1::2])]
    return terms[0]


def lines_x(t):
    return [[(t, i, j) for i in range(NODES)] for j in range(NODES)]


def lines_y(g):
    return [[(g, u, j) for j in range(NODES)] for u in range(4)]


def lines_z(g):
    return [[(g, u, pl.ds(k, 8, stride=8)) for k in range(NODES)] for u in range(4)]


def views(ref):
    along_x = ref.reshape(4, NODES, NODES, NODES, LANES)
    along_y = ref.reshape(8, 4, NODES, NODES, LANES)
    along_z = ref.reshape(8, 4, NODES * NODES, LANES)
    return along_x, along_y, along_z


def read(ref, line):
    return [ref[at] for at in line]


def write(ref, line, values):
    for at, value in zip(line, values):
        ref[at] = value


def sum_z(first, last):
    lane = lax.broadcasted_iota(jnp.int32, (8, LANES), 1)
    after = jnp.where(lane < LANES - 1, pltpu.roll(first, LANES - 1, 1), 0.0)
    before = jnp.where(lane > 0, pltpu.roll(last, 1, 1), 0.0)
    return first + before, last + after


def assemble_inside(ref):
    for ey in range(2):
        for j in range(NODES):
            both = ref[0, ey, 7, j] + ref[1, ey, 0, j]
            ref[0, ey, 7, j] = both
            ref[1, ey, 0, j] = both
    for ex in range(2):
        for i in range(NODES):
            both = ref[ex, 0, i, 7] + ref[ex, 1, i, 0]
            ref[ex, 0, i, 7] = both
            ref[ex, 1, i, 0] = both
    strips = views(ref)[2]

    def along_z(g, carry):
        lines = [line for u in range(4) for line in lines_z(g * 4 + u)]
        ends = [(strips[line[0]], strips[line[7]]) for line in lines]
        ends = [sum_z(first, last) for first, last in ends]
        for line, (first, last) in zip(lines, ends):
            strips[line[0]] = first
            strips[line[7]] = last
        return carry

    lax.fori_loop(0, 2, along_z, 0)


DIAG = SOURCES
IMAGE = SOURCES + 1
FIELDS = 2 * SOURCES + 1


def solve_kernel(
    loads,
    conduct,
    fields,
    inverse,
    scalars,
    flux,
    flux_z,
    part_z,
    z0,
    z_face,
    coef_x,
    coef_y,
    weighted,
    from_x,
    from_y,
    from_edge,
    sums,
    part,
    gathered,
    in_sem,
    send_sem,
    recv_sem,
    sum_send,
    sum_recv,
    ready,
):
    row = lax.axis_index("row")
    col = lax.axis_index("col")
    for ex in range(2):
        for ey in range(2):
            lanes = pl.ds((ex * 2 + ey) * LANES, LANES)
            pltpu.make_async_copy(
                conduct.at[:, :, :, lanes], flux.at[ex, ey], in_sem.at[SOURCES]
            ).start()
    for s in range(SOURCES):
        for ex in range(2):
            for ey in range(2):
                lanes = pl.ds((ex * 2 + ey) * LANES, LANES)
                pltpu.make_async_copy(
                    loads.at[s, :, :, :, lanes], fields.at[s, ex, ey], in_sem.at[s]
                ).start()

    has_up, has_down = row < N_ROW - 1, row > 0
    has_right, has_left = col < N_COL - 1, col > 0
    ways = [
        (1, 0, has_up),
        (-1, 0, has_down),
        (0, 1, has_right),
        (0, -1, has_left),
        (1, 1, has_up & has_right),
        (1, -1, has_up & has_left),
        (-1, 1, has_down & has_right),
        (-1, -1, has_down & has_left),
    ]
    sides_x = has_up.astype(jnp.int32) + has_down.astype(jnp.int32)
    sides_y = has_right.astype(jnp.int32) + has_left.astype(jnp.int32)
    barrier = pltpu.get_barrier_semaphore()
    corners = 0
    for dr, dc, there in ways[4:]:

        @pl.when(there)
        def _():
            pl.semaphore_signal(barrier, 1, device_id=(row + dr, col + dc), device_id_type=MESH)

        corners = corners + there.astype(jnp.int32)
    for step in range(1, N_COL):
        pl.semaphore_signal(
            barrier, 1, device_id=(row, lax.rem(col + step, N_COL)), device_id_type=MESH
        )
    for step in range(1, N_ROW):
        pl.semaphore_signal(
            barrier, 1, device_id=(lax.rem(row + step, N_ROW), col), device_id_type=MESH
        )

    def transfers(q):
        ref = fields.at[q]
        rest = pl.ds(1, NODES - 1)
        pieces = [
            (2, ref.at[0, 1, :, 7], from_y.at[q, 0, 0]),
            (2, ref.at[1, 1, rest, 7], from_y.at[q, 0, 1, rest]),
            (3, ref.at[0, 0, :, 0], from_y.at[q, 1, 0]),
            (3, ref.at[1, 0, rest, 0], from_y.at[q, 1, 1, rest]),
            (4, ref.at[1, 1, 7, 7], from_edge.at[q, 0]),
            (5, ref.at[1, 0, 7, 0], from_edge.at[q, 1]),
            (6, ref.at[0, 1, 0, 7], from_edge.at[q, 2]),
            (7, ref.at[0, 0, 0, 0], from_edge.at[q, 3]),
            (0, ref.at[1, :, 7], from_x.at[q, 0]),
            (1, ref.at[0, :, 0], from_x.at[q, 1]),
        ]
        return [
            (
                way,
                pltpu.make_async_remote_copy(
                    src,
                    dst,
                    send_sem.at[q],
                    recv_sem.at[q],
                    device_id=(row + ways[way][0], col + ways[way][1]),
                    device_id_type=MESH,
                ),
            )
            for way, src, dst in pieces
        ]

    def send(q):
        for way, copy in transfers(q):
            pl.when(ways[way][2])(copy.start)

    def collect(q):
        ref = fields.at[q]
        tiles = ref.reshape(4 * NODES * NODES, NODES, LANES)
        for across in (1, 2):
            for along in (1, 2):

                @pl.when((sides_x == across) & (sides_y == along))
                def _():
                    size = tiles.at[pl.ds(0, 16 * across + 15 * along + across * along)]
                    pltpu.make_async_copy(size, size, send_sem.at[q]).wait()
                    pltpu.make_async_copy(size, size, recv_sem.at[q]).wait()

        for ey in range(2):
            for j in range(NODES):
                ref[0, ey, 0, j] = ref[0, ey, 0, j] + from_x[q, 0, ey, j]
                ref[1, ey, 7, j] = ref[1, ey, 7, j] + from_x[q, 1, ey, j]
        for ex in range(2):
            for i in range(NODES):
                at = (0, 7) if (ex, i) == (1, 0) else (ex, i)
                ref[ex, 0, i, 0] = ref[ex, 0, i, 0] + from_y[(q, 0) + at]
                ref[ex, 1, i, 7] = ref[ex, 1, i, 7] + from_y[(q, 1) + at]
        for corner in range(4):
            ex, ey = corner // 2, corner % 2
            at = (ex, ey, 7 * ex, 7 * ey)
            ref[at] = ref[at] + from_edge[q, corner]

    def clear(ref, there, pick):
        @pl.when(jnp.logical_not(there))
        def _():
            def body(q, carry):
                target = pick(ref, q)
                target[...] = jnp.zeros_like(target)
                return carry

            lax.fori_loop(0, FIELDS, body, 0)

    clear(from_x, has_down, lambda ref, q: ref.at[q, 0])
    clear(from_x, has_up, lambda ref, q: ref.at[q, 1])
    clear(from_y, has_left, lambda ref, q: ref.at[q, 0])
    clear(from_y, has_right, lambda ref, q: ref.at[q, 1])
    clear(from_edge, has_down & has_left, lambda ref, q: ref.at[q, 0])
    clear(from_edge, has_down & has_right, lambda ref, q: ref.at[q, 1])
    clear(from_edge, has_up & has_left, lambda ref, q: ref.at[q, 2])
    clear(from_edge, has_up & has_right, lambda ref, q: ref.at[q, 3])
    sums[...] = jnp.zeros_like(sums)

    flux_v = views(flux)
    flux_zv = views(flux_z)
    part_v = views(part_z)
    z0_v = views(z0)
    weighted_v = views(weighted)
    inverse_v = views(inverse)
    diag_v = views(fields.at[DIAG])

    pltpu.make_async_copy(flux, flux, in_sem.at[SOURCES]).wait()
    node = lax.broadcasted_iota(jnp.int32, (8, LANES), 0)
    lane = lax.broadcasted_iota(jnp.int32, (8, LANES), 1)
    weight_z = jnp.full((8, LANES), WEIGHTS[3], jnp.float32)
    for k in (0, 1, 2):
        ends = (node == k) | (node == 7 - k)
        weight_z = jnp.where(ends, jnp.float32(WEIGHTS[k]), weight_z)

    def diag_x(t, carry):
        for j, line in enumerate(lines_x(t)):
            values = [
                v * (weight_z * float(SCREENING * WEIGHTS[i] * WEIGHTS[j]))
                for i, v in enumerate(read(flux_v[0], line))
            ]
            write(flux_v[0], line, values)
            write(diag_v[0], line, [r + v for r, v in zip(square_back(values), values)])
        return carry

    def diag_yz(g, carry):
        for line, strip in zip(lines_y(g), lines_z(g)):
            before = read(diag_v[1], line)
            result_y = square_back(read(flux_v[1], line))
            values = read(flux_v[2], strip)
            write(flux_zv[1], line, values)
            write(part_v[2], strip, square_back(values))
            write(diag_v[1], line, [b + r for b, r in zip(before, result_y)])
        return carry

    def diag_sum(g, carry):
        for line in lines_y(g):
            both = zip(read(diag_v[1], line), read(part_v[1], line))
            write(diag_v[1], line, [b + r for b, r in both])
        return carry

    lax.fori_loop(0, 4, diag_x, 0)
    lax.fori_loop(0, 8, diag_yz, 0)
    lax.fori_loop(0, 8, diag_sum, 0)

    def prepare(n, carry):
        q = lax.rem(n + DIAG, DIAG + 1)

        @pl.when(n > 0)
        def _():
            pltpu.make_async_copy(fields.at[q], fields.at[q], in_sem.at[q]).wait()

        assemble_inside(fields.at[q])
        return carry

    lax.fori_loop(0, DIAG + 1, prepare, 0)

    def invert(g, carry):
        for line in lines_y(g):
            write(inverse_v[1], line, [1.0 / v for v in read(diag_v[1], line)])
        return carry

    z0_strip = z0.reshape(4, NODES, NODES * NODES, LANES)
    part_strip = part_z.reshape(4, NODES, NODES * NODES, LANES)

    def stiff(values, weight):
        return derive_back([g * w for g, w in zip(derive(values), weight)])

    def own_part(s):
        right_v = views(fields.at[s])
        image_v = views(fields.at[IMAGE + s])

        def scale(g, carry):
            for line in lines_y(g):
                both = zip(read(right_v[1], line), read(inverse_v[1], line))
                write(z0_v[1], line, [v * d for v, d in both])
            return carry

        lax.fori_loop(0, 8, scale, 0)
        empty = jnp.zeros((8, LANES), jnp.float32)
        for ex in range(2):
            for ey in range(2):
                for n in range(NODES):
                    z0[ex, ey, 7 * ex, n] = empty
                    z0[ex, ey, n, 7 * ey] = empty

        def stiff_z(t, carry):
            planes = pl.ds(1 - t // 2, NODES - 1)
            values, weight = z0_strip.at[t, planes], flux_zv[0].at[t, planes]
            result = part_strip.at[t, planes]
            for u in range(NODES - 1):
                strips = [(u, pl.ds(k, 8, stride=8)) for k in range(NODES)]
                out = stiff(read(values, strips), [weight[u, k] for k in range(NODES)])
                write(result, strips, out)
            return carry

        def stiff_x(t, carry):
            end = lax.rem(t, 2)
            lines = pl.ds(1 - end, NODES - 1)
            values, weight = z0_v[0].at[t, :, lines], flux_v[0].at[t, :, lines]
            result = image_v[0].at[t, :, lines]
            for n in range(NODES - 1):
                line = [(i, n) for i in range(NODES)]
                v, w = read(values, line), read(weight, line)
                out = stiff(v, w)
                write(result, line, [r + b * a for r, b, a in zip(out, w, v)])
            for i in range(NODES):
                image_v[0][t, i, 7 * end] = empty
            return carry

        def stiff_y(t, carry):
            planes = pl.ds(1 - t // 2, NODES - 1)
            values, weight = z0_v[0].at[t, planes], flux_v[0].at[t, planes]
            result, other = image_v[0].at[t, planes], part_v[0].at[t, planes]
            for u in range(NODES - 1):
                line = [(u, j) for j in range(NODES)]
                out = stiff(read(values, line), read(weight, line))
                before = zip(read(result, line), read(other, line), out)
                write(result, line, [a + b + r for a, b, r in before])
            return carry

        lax.fori_loop(0, 4, stiff_z, 0)
        lax.fori_loop(0, 4, stiff_x, 0)
        lax.fori_loop(0, 4, stiff_y, 0)

    def send_first(n, carry):
        send(lax.rem(n + DIAG, DIAG + 1))
        return carry

    pl.semaphore_wait(barrier, N_ROW - 1 + N_COL - 1 + corners)
    lax.fori_loop(0, DIAG + 1, send_first, 0)

    def tell(step, carry):
        pl.semaphore_signal(
            ready, 1, device_id=(row, lax.rem(col + step, N_COL)), device_id_type=MESH
        )
        return carry

    lax.fori_loop(1, N_COL, tell, 0)
    lax.fori_loop(0, 8, invert, 0)

    def begin(s, carry):
        own_part(s)
        return carry

    lax.fori_loop(0, SOURCES, begin, 0)

    for side in range(2):
        end = 7 * side

        def lean(other, carry):
            for n in range(NODES):
                weight = [flux[side, other, a, n] for a in range(NODES)]
                result = derive_back([w * float(SLOPE[a, end]) for a, w in enumerate(weight)])
                result[end] = result[end] + weight[end]
                for i in range(NODES):
                    coef_x[side, other, i, n] = result[i]
                weight = [flux[other, side, n, b] for b in range(NODES)]
                result = derive_back([w * float(SLOPE[b, end]) for b, w in enumerate(weight)])
                for j in range(NODES):
                    coef_y[other, side, n, j] = result[j]
            return carry

        lax.fori_loop(0, 2, lean, 0)

    collect(DIAG)
    for ex in range(2):
        for ey in range(2):
            for n in range(NODES):
                for at in ((ex, ey, 7 * ex, n), (ex, ey, n, 7 * ey)):
                    inverse[at] = 1.0 / fields[(DIAG,) + at]

    face_v = views(z_face)[0]
    face_strip = z_face.reshape(4, NODES, NODES * NODES, LANES)
    face_flat = z_face.reshape(4, NODES**3, LANES)
    flux_flat = flux.reshape(4, NODES**3, LANES)
    coef_xv = views(coef_x)[0]
    coef_yv = views(coef_y)[0]

    def correct(s, carry):
        collect(s)
        for ex in range(2):
            for ey in range(2):
                for n in range(NODES):
                    for at in ((ex, ey, 7 * ex, n), (ex, ey, n, 7 * ey)):
                        z_face[at] = fields[(s,) + at] * inverse[at]
        target = fields.at[IMAGE + s]
        image_v = views(target)[0]
        image_strip = target.reshape(4, NODES, NODES * NODES, LANES)
        image_flat = target.reshape(4, NODES**3, LANES)

        def faces(t, carry):
            i0 = 7 * (t // 2)
            j0 = 7 * lax.rem(t, 2)
            nodes = range(NODES)
            values = [face_v[t, i, j0] for i in nodes]
            weight = [flux_v[0][t, i, j0] for i in nodes]
            result = stiff(values, weight)
            result = [r + w * v for r, w, v in zip(result, weight, values)]
            result_y = stiff([face_v[t, i0, j] for j in nodes], [flux_v[0][t, i0, j] for j in nodes])
            strips = [(t, i0, pl.ds(k, 8, stride=8)) for k in nodes]
            result_z = stiff(read(face_strip, strips), [flux_zv[0][t, i0, k] for k in nodes])
            columns = [(t, pl.ds(j0 * 8 + k, 8, stride=64)) for k in nodes]
            values = [jnp.where(node == i0, 0.0, v) for v in read(face_flat, columns)]
            result_c = stiff(values, read(flux_flat, columns))
            for at, r in zip(strips, result_z):
                image_strip[at] = image_strip[at] + r
            for at, r in zip(columns, result_c):
                image_flat[at] = image_flat[at] + r
            for i, r in zip(nodes, result):
                image_v[t, i, j0] = image_v[t, i, j0] + r
            for j, r in zip(nodes, result_y):
                image_v[t, i0, j] = image_v[t, i0, j] + r
            ends_x = [jnp.where(j0 == j, 0.0, face_v[t, i0, j]) for j in nodes]
            ends_y = [jnp.where(i0 == i, 0.0, face_v[t, i, j0]) for i in nodes]
            for i in nodes:
                for j in nodes:
                    more = coef_xv[t, i, j] * ends_x[j] + coef_yv[t, i, j] * ends_y[i]
                    image_v[t, i, j] = image_v[t, i, j] + more
            return carry

        lax.fori_loop(0, 4, faces, 0)
        assemble_inside(target)
        send(IMAGE + s)
        return carry

    lax.fori_loop(0, SOURCES, correct, 0)

    twice_z = ((node == 0) & (lane > 0)) | ((node == 7) & (lane < LANES - 1))
    share_z = jnp.where(twice_z, jnp.float32(0.5), jnp.float32(1.0))

    def share(g, carry):
        for line in lines_y(g):
            write(weighted_v[1], line, [v * share_z for v in read(inverse_v[1], line)])
        return carry

    lax.fori_loop(0, 8, share, 0)

    def part_of(there):
        return 0.5 if there is None else jnp.where(there, 0.5, 1.0).astype(jnp.float32)

    for there, ex, i in [(has_down, 0, 0), (None, 0, 7), (None, 1, 0), (has_up, 1, 7)]:
        for ey in range(2):
            weighted[ex, ey, i] = weighted[ex, ey, i] * part_of(there)
    for there, ey, j in [(has_left, 0, 0), (None, 0, 7), (None, 1, 0), (has_right, 1, 7)]:
        for ex in range(2):
            weighted[ex, ey, :, j] = weighted[ex, ey, :, j] * part_of(there)

    zero = jnp.zeros((8, LANES), jnp.float32)

    def settle(s, carry):
        collect(IMAGE + s)
        right_v = views(fields.at[s])[1]
        image_v = views(fields.at[IMAGE + s])[1]

        def products(g, carry):
            terms = [[], [], []]
            for line in lines_y(g):
                for at in line:
                    r, v, w = right_v[at], image_v[at], weighted_v[1][at]
                    rw = r * w
                    terms[0].append(r * rw)
                    terms[1].append(v * rw)
                    terms[2].append(v * (v * w))
            return tuple(c + tree_sum(t) for c, t in zip(carry, terms))

        totals = lax.fori_loop(0, 8, products, (zero, zero, zero))
        for n, total in enumerate(totals):
            sums[pl.ds(n * SOURCES + s, 1), :] = jnp.sum(total, axis=0, keepdims=True)
        return carry

    lax.fori_loop(0, SOURCES, settle, 0)

    total = jnp.sum(sums[...], axis=1, keepdims=True)
    node16 = lax.broadcasted_iota(jnp.int32, (16, LANES), 0)
    lane16 = lax.broadcasted_iota(jnp.int32, (16, LANES), 1)
    packed = jnp.where(node16 == lane16, jnp.broadcast_to(total, (16, LANES)), 0.0)
    packed = jnp.sum(packed, axis=0, keepdims=True)
    part[0:1, :] = packed
    mine = pl.ds(row * N_COL + col, 1)
    gathered[mine, :] = packed
    pl.semaphore_wait(ready, N_COL - 1)

    def spread(step, carry):
        there = (lax.rem(row + step // N_COL, N_ROW), lax.rem(col + lax.rem(step, N_COL), N_COL))
        pltpu.make_async_remote_copy(
            part.at[0:1],
            gathered.at[mine],
            sum_send.at[0],
            sum_recv.at[0],
            device_id=there,
            device_id_type=MESH,
        ).start()
        return carry

    lax.fori_loop(1, N_ROW * N_COL, spread, 0)
    others = gathered.at[pl.ds(0, N_ROW * N_COL - 1)]
    pltpu.make_async_copy(others, others, sum_recv.at[0]).wait()
    pltpu.make_async_copy(others, others, sum_send.at[0]).wait()
    total = tree_sum([gathered[pl.ds(8 * n, 8), :] for n in range(N_ROW * N_COL // 8)])
    total = jnp.sum(total, axis=0, keepdims=True)
    total = jnp.broadcast_to(total, (16, LANES))
    total = jnp.sum(jnp.where(node16 == lane16, total, 0.0), axis=1, keepdims=True)
    rz_first, curvature, square = total[0:4], total[4:8], total[8:12]
    alpha = rz_first / curvature
    rz_second = alpha * alpha * square - rz_first
    beta = rz_second / rz_first
    scalars[0:4, :] = jnp.broadcast_to(alpha, (4, LANES))
    scalars[4:8, :] = jnp.broadcast_to(beta, (4, LANES))


SLOTS = 8


def update_kernel(fields, inverse, scalars, first, second, third, staging, sem):
    outputs = (first, second, third)

    def copies(n):
        return [
            pltpu.make_async_copy(
                staging.at[n % SLOTS, q], outputs[q].at[n // NODES, n % NODES], sem.at[n % SLOTS]
            )
            for q in range(3)
        ]

    def await_slot(slot):
        pltpu.make_async_copy(staging.at[slot], staging.at[slot], sem.at[slot]).wait()

    def step(n, carry):
        s, i, slot = n // NODES, n % NODES, n % SLOTS

        @pl.when(n >= SLOTS)
        def _():
            await_slot(slot)

        alpha = jnp.broadcast_to(scalars[pl.ds(s, 1), :], (8, LANES))
        beta = jnp.broadcast_to(scalars[pl.ds(s + 4, 1), :], (8, LANES))
        for ex in range(2):
            for ey in range(2):
                lanes = pl.ds((ex * 2 + ey) * LANES, LANES)
                for j in range(NODES):
                    right = fields[s, ex, ey, i, j]
                    inv = inverse[ex, ey, i, j]
                    rest = right - alpha * fields[IMAGE + s, ex, ey, i, j]
                    staging[slot, 0, j, :, lanes] = alpha * (right * inv)
                    staging[slot, 1, j, :, lanes] = rest
                    staging[slot, 2, j, :, lanes] = (rest + beta * right) * inv
        for copy in copies(n):
            copy.start()
        return carry

    steps = SOURCES * NODES
    lax.fori_loop(0, steps, step, 0)
    for n in range(steps - SLOTS, steps):
        await_slot(n % SLOTS)


def per_device(loads, conduct):
    f32 = jnp.float32
    vmem = pltpu.VMEM
    whole = pl.BlockSpec(memory_space=vmem)
    results = pl.pallas_call(
        solve_kernel,
        out_shape=[vmem((FIELDS,) + FIELD, f32), vmem(FIELD, f32), vmem((8, LANES), f32)],
        in_specs=[pl.BlockSpec(memory_space=pl.ANY)] * 2,
        out_specs=[whole] * 3,
        scratch_shapes=[vmem(FIELD, f32)] * 8
        + [
            vmem((FIELDS, 2, 2, NODES, NODES, LANES), f32),
            vmem((FIELDS, 2, 2, NODES, NODES, LANES), f32),
            vmem((FIELDS, 4, NODES, LANES), f32),
            vmem((16, LANES), f32),
            vmem((8, LANES), f32),
            vmem((N_ROW * N_COL, LANES), f32),
            pltpu.SemaphoreType.DMA((SOURCES + 1,)),
            pltpu.SemaphoreType.DMA((FIELDS,)),
            pltpu.SemaphoreType.DMA((FIELDS,)),
            pltpu.SemaphoreType.DMA((1,)),
            pltpu.SemaphoreType.DMA((1,)),
            pltpu.SemaphoreType.REGULAR,
        ],
        compiler_params=pltpu.CompilerParams(
            collective_id=0, has_side_effects=True, vmem_limit_bytes=40 * 1024 * 1024
        ),
    )(*[pltpu.with_memory_space_constraint(x, pltpu.HBM) for x in (loads, conduct)])
    shape = (SOURCES, NODES, NODES, NODES, 4 * LANES)
    return pl.pallas_call(
        update_kernel,
        out_shape=[jax.ShapeDtypeStruct(shape, f32)] * 3,
        in_specs=[whole] * 3,
        out_specs=[pl.BlockSpec(memory_space=pl.ANY)] * 3,
        scratch_shapes=[
            vmem((SLOTS, 3, NODES, NODES, 4 * LANES), f32),
            pltpu.SemaphoreType.DMA((SLOTS,)),
        ],
        compiler_params=pltpu.CompilerParams(vmem_limit_bytes=16 * 1024 * 1024),
    )(*[pltpu.with_memory_space_constraint(x, vmem) for x in results])


def solution(mesh):
    in_specs = (P(None, None, None, None, ("row", "col")), P(None, None, None, ("row", "col")))
    out = P(None, None, None, None, ("row", "col"))
    return jax.shard_map(
        per_device, mesh=mesh, in_specs=in_specs, out_specs=(out, out, out), check_vma=False
    )
```

```python
import functools

import jax
import jax.numpy as jnp
import numpy as np
from jax import lax
from jax.experimental import pallas as pl
from jax.experimental.pallas import tpu as pltpu
from jax.sharding import PartitionSpec as P

NODES = 8
SOURCES = 4
LANES = 128
N_ROW = 8
N_COL = 16
SCREENING = 0.5
GLL_INNER = [
    -0.8717401485096066,
    -0.5917001814331423,
    -0.2092992179024789,
    0.2092992179024789,
    0.5917001814331423,
    0.8717401485096066,
]
MESH = pl.DeviceIdType.MESH
FIELD = (2, 2, NODES, NODES, NODES, LANES)


def gll_tables():
    degree = NODES - 1
    points = np.array([-1.0] + GLL_INNER + [1.0])
    previous = points * 0.0 + 1.0
    current = points * 1.0
    for order in range(1, degree):
        following = ((2 * order + 1) * points * current - order * previous) / (order + 1)
        previous = current
        current = following
    weights = 2.0 / (degree * (degree + 1) * current**2)
    spread = points[:, None] - points[None, :]
    index_ids = np.arange(NODES)
    same = index_ids[:, None] == index_ids[None, :]
    safe_spread = np.where(same, 1.0, spread)
    deriv = np.where(same, 0.0, current[:, None] / (current[None, :] * safe_spread))
    corner = degree * (degree + 1) / 4.0
    ends = np.where(index_ids == 0, -corner, np.where(index_ids == degree, corner, 0.0))
    deriv = deriv + np.where(same, ends[None, :], 0.0)
    return deriv, weights


DERIV, WEIGHTS = gll_tables()
SQUARE = DERIV * DERIV
HALF = NODES // 2


def halves(table):
    mirrored = table[:HALF, ::-1][:, :HALF]
    direct = table[:HALF, :HALF]
    plus = (direct + mirrored) / 2.0
    minus = (direct - mirrored) / 2.0
    return plus.tolist(), minus.tolist()


SLOPE = DERIV * np.sqrt(2.0)
D_PLUS, D_MINUS = halves(SLOPE)
Q_PLUS, Q_MINUS = halves(SQUARE * 2.0)


def fold(values):
    plus = [values[i] + values[7 - i] for i in range(HALF)]
    minus = [values[i] - values[7 - i] for i in range(HALF)]
    return plus, minus


def combine(table, values, transposed):
    out = []
    for a in range(HALF):
        total = None
        for i in range(HALF):
            factor = table[i][a] if transposed else table[a][i]
            term = values[i] * factor
            total = term if total is None else total + term
        out.append(total)
    return out


def unfold(base, turn):
    low = [base[a] + turn[a] for a in range(HALF)]
    high = [base[a] - turn[a] for a in range(HALF)]
    return low + high[::-1]


def derive(values):
    plus, minus = fold(values)
    return unfold(combine(D_MINUS, minus, False), combine(D_PLUS, plus, False))


def derive_back(values):
    plus, minus = fold(values)
    return unfold(combine(D_PLUS, minus, True), combine(D_MINUS, plus, True))


def square_back(values):
    plus, minus = fold(values)
    return unfold(combine(Q_PLUS, plus, True), combine(Q_MINUS, minus, True))


def tree_sum(terms):
    while len(terms) > 1:
        terms = [a + b for a, b in zip(terms[::2], terms[1::2])]
    return terms[0]


def lines_x(t):
    return [[(t, i, j) for i in range(NODES)] for j in range(NODES)]


def lines_y(g):
    return [[(g, u, j) for j in range(NODES)] for u in range(4)]


def lines_z(g):
    return [[(g, u, pl.ds(k, 8, stride=8)) for k in range(NODES)] for u in range(4)]


def views(ref):
    along_x = ref.reshape(4, NODES, NODES, NODES, LANES)
    along_y = ref.reshape(8, 4, NODES, NODES, LANES)
    along_z = ref.reshape(8, 4, NODES * NODES, LANES)
    return along_x, along_y, along_z


def read(ref, line):
    return [ref[at] for at in line]


def write(ref, line, values):
    for at, value in zip(line, values):
        ref[at] = value


def sum_z(first, last, rows=True):
    lane = lax.broadcasted_iota(jnp.int32, (8, LANES), 1)
    after = jnp.where((lane < LANES - 1) & rows, pltpu.roll(first, LANES - 1, 1), 0.0)
    before = jnp.where((lane > 0) & rows, pltpu.roll(last, 1, 1), 0.0)
    return first + before, last + after


def assemble_inside(ref):
    for ey in range(2):
        for j in range(NODES):
            both = ref[0, ey, 7, j] + ref[1, ey, 0, j]
            ref[0, ey, 7, j] = both
            ref[1, ey, 0, j] = both
    for ex in range(2):
        for i in range(NODES):
            both = ref[ex, 0, i, 7] + ref[ex, 1, i, 0]
            ref[ex, 0, i, 7] = both
            ref[ex, 1, i, 0] = both
    strips = views(ref)[2]

    def along_z(g, carry):
        lines = [line for u in range(4) for line in lines_z(g * 4 + u)]
        ends = [(strips[line[0]], strips[line[7]]) for line in lines]
        ends = [sum_z(first, last) for first, last in ends]
        for line, (first, last) in zip(lines, ends):
            strips[line[0]] = first
            strips[line[7]] = last
        return carry

    lax.fori_loop(0, 2, along_z, 0)


DIAG = SOURCES
IMAGE = SOURCES + 1
FIELDS = 2 * SOURCES + 1


def solve_kernel(
    loads,
    conduct,
    fields,
    inverse,
    scalars,
    flux,
    flux_z,
    part_z,
    z0,
    z_face,
    coef_x,
    coef_y,
    weighted,
    from_x,
    from_y,
    from_edge,
    sums,
    part,
    gather_row,
    gather_col,
    in_sem,
    send_sem,
    recv_sem,
    sum_send,
    sum_recv,
):
    row = lax.axis_index("row")
    col = lax.axis_index("col")
    for ex in range(2):
        for ey in range(2):
            lanes = pl.ds((ex * 2 + ey) * LANES, LANES)
            pltpu.make_async_copy(
                conduct.at[:, :, :, lanes], flux.at[ex, ey], in_sem.at[SOURCES]
            ).start()
    for s in range(SOURCES):
        for ex in range(2):
            for ey in range(2):
                lanes = pl.ds((ex * 2 + ey) * LANES, LANES)
                pltpu.make_async_copy(
                    loads.at[s, :, :, :, lanes], fields.at[s, ex, ey], in_sem.at[s]
                ).start()

    has_up, has_down = row < N_ROW - 1, row > 0
    has_right, has_left = col < N_COL - 1, col > 0
    ways = [
        (1, 0, has_up),
        (-1, 0, has_down),
        (0, 1, has_right),
        (0, -1, has_left),
        (1, 1, has_up & has_right),
        (1, -1, has_up & has_left),
        (-1, 1, has_down & has_right),
        (-1, -1, has_down & has_left),
    ]
    sides_x = has_up.astype(jnp.int32) + has_down.astype(jnp.int32)
    sides_y = has_right.astype(jnp.int32) + has_left.astype(jnp.int32)
    barrier = pltpu.get_barrier_semaphore()
    corners = 0
    for dr, dc, there in ways[4:]:

        @pl.when(there)
        def _():
            pl.semaphore_signal(barrier, 1, device_id=(row + dr, col + dc), device_id_type=MESH)

        corners = corners + there.astype(jnp.int32)
    for step in range(1, N_COL):
        pl.semaphore_signal(
            barrier, 1, device_id=(row, lax.rem(col + step, N_COL)), device_id_type=MESH
        )
    for step in range(1, N_ROW):
        pl.semaphore_signal(
            barrier, 1, device_id=(lax.rem(row + step, N_ROW), col), device_id_type=MESH
        )

    def transfers(q):
        ref = fields.at[q]
        rest = pl.ds(1, NODES - 1)
        pieces = [
            (2, ref.at[0, 1, :, 7], from_y.at[q, 0, 0]),
            (2, ref.at[1, 1, rest, 7], from_y.at[q, 0, 1, rest]),
            (3, ref.at[0, 0, :, 0], from_y.at[q, 1, 0]),
            (3, ref.at[1, 0, rest, 0], from_y.at[q, 1, 1, rest]),
            (4, ref.at[1, 1, 7, 7], from_edge.at[q, 0]),
            (5, ref.at[1, 0, 7, 0], from_edge.at[q, 1]),
            (6, ref.at[0, 1, 0, 7], from_edge.at[q, 2]),
            (7, ref.at[0, 0, 0, 0], from_edge.at[q, 3]),
            (0, ref.at[1, :, 7], from_x.at[q, 0]),
            (1, ref.at[0, :, 0], from_x.at[q, 1]),
        ]
        return [
            (
                way,
                pltpu.make_async_remote_copy(
                    src,
                    dst,
                    send_sem.at[q],
                    recv_sem.at[q],
                    device_id=(row + ways[way][0], col + ways[way][1]),
                    device_id_type=MESH,
                ),
            )
            for way, src, dst in pieces
        ]

    def send(q):
        for way, copy in transfers(q):
            pl.when(ways[way][2])(copy.start)

    def await_all(q, sem):
        tiles = fields.at[q].reshape(4 * NODES * NODES, NODES, LANES)
        for across in (1, 2):
            for along in (1, 2):

                @pl.when((sides_x == across) & (sides_y == along))
                def _():
                    size = tiles.at[pl.ds(0, 16 * across + 15 * along + across * along)]
                    pltpu.make_async_copy(size, size, sem).wait()

    def collect(q):
        await_all(q, recv_sem.at[q])
        ref = fields.at[q]
        for ey in range(2):
            for j in range(NODES):
                ref[0, ey, 0, j] = ref[0, ey, 0, j] + from_x[q, 0, ey, j]
                ref[1, ey, 7, j] = ref[1, ey, 7, j] + from_x[q, 1, ey, j]
        for ex in range(2):
            for i in range(NODES):
                at = (0, 7) if (ex, i) == (1, 0) else (ex, i)
                ref[ex, 0, i, 0] = ref[ex, 0, i, 0] + from_y[(q, 0) + at]
                ref[ex, 1, i, 7] = ref[ex, 1, i, 7] + from_y[(q, 1) + at]
        for corner in range(4):
            ex, ey = corner // 2, corner % 2
            at = (ex, ey, 7 * ex, 7 * ey)
            ref[at] = ref[at] + from_edge[q, corner]

    def clear(ref, there, pick):
        @pl.when(jnp.logical_not(there))
        def _():
            def body(q, carry):
                target = pick(ref, q)
                target[...] = jnp.zeros_like(target)
                return carry

            lax.fori_loop(0, FIELDS, body, 0)

    clear(from_x, has_down, lambda ref, q: ref.at[q, 0])
    clear(from_x, has_up, lambda ref, q: ref.at[q, 1])
    clear(from_y, has_left, lambda ref, q: ref.at[q, 0])
    clear(from_y, has_right, lambda ref, q: ref.at[q, 1])
    clear(from_edge, has_down & has_left, lambda ref, q: ref.at[q, 0])
    clear(from_edge, has_down & has_right, lambda ref, q: ref.at[q, 1])
    clear(from_edge, has_up & has_left, lambda ref, q: ref.at[q, 2])
    clear(from_edge, has_up & has_right, lambda ref, q: ref.at[q, 3])
    sums[...] = jnp.zeros_like(sums)

    flux_v = views(flux)
    flux_zv = views(flux_z)
    part_v = views(part_z)
    z0_v = views(z0)
    weighted_v = views(weighted)
    inverse_v = views(inverse)
    diag_v = views(fields.at[DIAG])

    pltpu.make_async_copy(flux, flux, in_sem.at[SOURCES]).wait()
    node = lax.broadcasted_iota(jnp.int32, (8, LANES), 0)
    lane = lax.broadcasted_iota(jnp.int32, (8, LANES), 1)
    weight_z = jnp.full((8, LANES), WEIGHTS[3], jnp.float32)
    for k in (0, 1, 2):
        ends = (node == k) | (node == 7 - k)
        weight_z = jnp.where(ends, jnp.float32(WEIGHTS[k]), weight_z)

    def diag_x(t, carry):
        for j, line in enumerate(lines_x(t)):
            values = [
                v * (weight_z * float(SCREENING * WEIGHTS[i] * WEIGHTS[j]))
                for i, v in enumerate(read(flux_v[0], line))
            ]
            write(flux_v[0], line, values)
            write(diag_v[0], line, [r + v for r, v in zip(square_back(values), values)])
        return carry

    def diag_yz(g, carry):
        for line, strip in zip(lines_y(g), lines_z(g)):
            before = read(diag_v[1], line)
            result_y = square_back(read(flux_v[1], line))
            values = read(flux_v[2], strip)
            write(flux_zv[1], line, values)
            write(part_v[2], strip, square_back(values))
            write(diag_v[1], line, [b + r for b, r in zip(before, result_y)])
        return carry

    def diag_sum(g, carry):
        for line in lines_y(g):
            both = zip(read(diag_v[1], line), read(part_v[1], line))
            write(diag_v[1], line, [b + r for b, r in both])
        return carry

    lax.fori_loop(0, 4, diag_x, 0)
    lax.fori_loop(0, 8, diag_yz, 0)
    lax.fori_loop(0, 8, diag_sum, 0)

    def prepare(n, carry):
        q = lax.rem(n + DIAG, DIAG + 1)

        @pl.when(n > 0)
        def _():
            pltpu.make_async_copy(fields.at[q], fields.at[q], in_sem.at[q]).wait()

        assemble_inside(fields.at[q])
        return carry

    lax.fori_loop(0, DIAG + 1, prepare, 0)

    def invert(g, carry):
        for line in lines_y(g):
            write(inverse_v[1], line, [1.0 / v for v in read(diag_v[1], line)])
        return carry

    z0_strip = z0.reshape(4, NODES, NODES * NODES, LANES)

    def stiff(values, weight):
        return derive_back([g * w for g, w in zip(derive(values), weight)])

    empty = jnp.zeros((8, LANES), jnp.float32)

    def inside_part(s):
        right_v = views(fields.at[s])

        def scale(g, carry):
            for line in lines_y(g):
                both = zip(read(right_v[1], line), read(inverse_v[1], line))
                write(z0_v[1], line, [v * d for v, d in both])
            return carry

        lax.fori_loop(0, 8, scale, 0)
        for ex in range(2):
            for ey in range(2):
                for n in range(NODES):
                    z0[ex, ey, 7 * ex, n] = empty
                    z0[ex, ey, n, 7 * ey] = empty

    def begin(s, carry):
        inside_part(s)
        image_v = views(fields.at[IMAGE + s])

        def stiff_x(t, carry):
            end = lax.rem(t, 2)
            lines = pl.ds(1 - end, NODES - 1)
            values, weight = z0_v[0].at[t, :, lines], flux_v[0].at[t, :, lines]
            result = image_v[0].at[t, :, lines]
            for n in range(NODES - 1):
                line = [(i, n) for i in range(NODES)]
                v, w = read(values, line), read(weight, line)
                out = stiff(v, w)
                write(result, line, [r + b * a for r, b, a in zip(out, w, v)])
            for i in range(NODES):
                image_v[0][t, i, 7 * end] = empty
            return carry

        def stiff_y(t, carry):
            planes = pl.ds(1 - t // 2, NODES - 1)
            values, weight = z0_v[0].at[t, planes], flux_v[0].at[t, planes]
            result = image_v[0].at[t, planes]
            for u in range(NODES - 1):
                line = [(u, j) for j in range(NODES)]
                out = stiff(read(values, line), read(weight, line))
                write(result, line, [a + r for a, r in zip(read(result, line), out)])
            return carry

        lax.fori_loop(0, 4, stiff_x, 0)
        lax.fori_loop(0, 4, stiff_y, 0)
        return carry

    def finish_z(s):
        inside_part(s)
        target = fields.at[IMAGE + s]
        strip = target.reshape(4, NODES, NODES * NODES, LANES)

        def stiff_z(t, carry):
            planes = pl.ds(1 - t // 2, NODES - 1)
            values, weight = z0_strip.at[t, planes], flux_zv[0].at[t, planes]
            result = strip.at[t, planes]
            off_face = node != 7 * lax.rem(t, 2)
            for u in range(NODES - 1):
                strips = [(u, pl.ds(k, 8, stride=8)) for k in range(NODES)]
                out = stiff(read(values, strips), [weight[u, k] for k in range(NODES)])
                out = [a + r for a, r in zip(read(result, strips), out)]
                out[0], out[7] = sum_z(out[0], out[7], off_face)
                write(result, strips, out)
            return carry

        lax.fori_loop(0, 4, stiff_z, 0)
        for ey in range(2):
            for j in range(1 - ey, NODES - ey):
                both = target[0, ey, 7, j] + target[1, ey, 0, j]
                target[0, ey, 7, j] = both
                target[1, ey, 0, j] = both
        for ex in range(2):
            for i in range(1 - ex, NODES - ex):
                both = target[ex, 0, i, 7] + target[ex, 1, i, 0]
                target[ex, 0, i, 7] = both
                target[ex, 1, i, 0] = both

    def send_first(n, carry):
        send(lax.rem(n + DIAG, DIAG + 1))
        return carry

    pl.semaphore_wait(barrier, N_ROW - 1 + N_COL - 1 + corners)
    lax.fori_loop(0, DIAG + 1, send_first, 0)
    lax.fori_loop(0, 8, invert, 0)

    lax.fori_loop(0, SOURCES, begin, 0)

    for side in range(2):
        end = 7 * side

        def lean(other, carry):
            for n in range(NODES):
                weight = [flux[side, other, a, n] for a in range(NODES)]
                result = derive_back([w * float(SLOPE[a, end]) for a, w in enumerate(weight)])
                result[end] = result[end] + weight[end]
                for i in range(NODES):
                    coef_x[side, other, i, n] = result[i]
                weight = [flux[other, side, n, b] for b in range(NODES)]
                result = derive_back([w * float(SLOPE[b, end]) for b, w in enumerate(weight)])
                for j in range(NODES):
                    coef_y[other, side, n, j] = result[j]
            return carry

        lax.fori_loop(0, 2, lean, 0)

    await_all(DIAG, send_sem.at[DIAG])
    collect(DIAG)
    for ex in range(2):
        for ey in range(2):
            for n in range(NODES):
                for at in ((ex, ey, 7 * ex, n), (ex, ey, n, 7 * ey)):
                    inverse[at] = 1.0 / fields[(DIAG,) + at]

    face_v = views(z_face)[0]
    face_strip = z_face.reshape(4, NODES, NODES * NODES, LANES)
    face_flat = z_face.reshape(4, NODES**3, LANES)
    flux_flat = flux.reshape(4, NODES**3, LANES)
    coef_xv = views(coef_x)[0]
    coef_yv = views(coef_y)[0]

    def correct(s, carry):
        await_all(s, send_sem.at[s])
        collect(s)
        for ex in range(2):
            for ey in range(2):
                for n in range(NODES):
                    for at in ((ex, ey, 7 * ex, n), (ex, ey, n, 7 * ey)):
                        z_face[at] = fields[(s,) + at] * inverse[at]
        target = fields.at[IMAGE + s]
        image_v = views(target)[0]
        image_strip = target.reshape(4, NODES, NODES * NODES, LANES)
        image_flat = target.reshape(4, NODES**3, LANES)

        def faces(t, carry):
            i0 = 7 * (t // 2)
            j0 = 7 * lax.rem(t, 2)
            nodes = range(NODES)
            values = [face_v[t, i, j0] for i in nodes]
            weight = [flux_v[0][t, i, j0] for i in nodes]
            result = stiff(values, weight)
            result = [r + w * v for r, w, v in zip(result, weight, values)]
            result_y = stiff([face_v[t, i0, j] for j in nodes], [flux_v[0][t, i0, j] for j in nodes])
            strips = [(t, i0, pl.ds(k, 8, stride=8)) for k in nodes]
            result_z = stiff(read(face_strip, strips), [flux_zv[0][t, i0, k] for k in nodes])
            columns = [(t, pl.ds(j0 * 8 + k, 8, stride=64)) for k in nodes]
            values = [jnp.where(node == i0, 0.0, v) for v in read(face_flat, columns)]
            result_c = stiff(values, read(flux_flat, columns))
            for at, r in zip(strips, result_z):
                image_strip[at] = image_strip[at] + r
            for at, r in zip(columns, result_c):
                image_flat[at] = image_flat[at] + r
            for i, r in zip(nodes, result):
                image_v[t, i, j0] = image_v[t, i, j0] + r
            for j, r in zip(nodes, result_y):
                image_v[t, i0, j] = image_v[t, i0, j] + r
            ends_x = [jnp.where(j0 == j, 0.0, face_v[t, i0, j]) for j in nodes]
            ends_y = [jnp.where(i0 == i, 0.0, face_v[t, i, j0]) for i in nodes]
            for i in nodes:
                for j in nodes:
                    more = coef_xv[t, i, j] * ends_x[j] + coef_yv[t, i, j] * ends_y[i]
                    image_v[t, i, j] = image_v[t, i, j] + more
            return carry

        lax.fori_loop(0, 4, faces, 0)
        for ey in range(2):
            both = target[0, ey, 7, 7 * ey] + target[1, ey, 0, 7 * ey]
            target[0, ey, 7, 7 * ey] = both
            target[1, ey, 0, 7 * ey] = both
        for ex in range(2):
            both = target[ex, 0, 7 * ex, 7] + target[ex, 1, 7 * ex, 0]
            target[ex, 0, 7 * ex, 7] = both
            target[ex, 1, 7 * ex, 0] = both
        ends = []
        for t in range(4):
            i0, j0 = 7 * (t // 2), 7 * (t % 2)
            strips = [(t, i0, pl.ds(k, 8, stride=8)) for k in (0, 7)]
            columns = [(t, pl.ds(j0 * 8 + k, 8, stride=64)) for k in (0, 7)]
            ends.append((image_strip, strips, read(image_strip, strips)))
            ends.append((image_flat, columns, read(image_flat, columns)))
        for ref, at, (first, last) in ends:
            write(ref, at, sum_z(first, last))
        send(IMAGE + s)
        return carry

    lax.fori_loop(0, SOURCES, correct, 0)

    twice_z = ((node == 0) & (lane > 0)) | ((node == 7) & (lane < LANES - 1))
    share_z = jnp.where(twice_z, jnp.float32(0.5), jnp.float32(1.0))

    def share(g, carry):
        for line in lines_y(g):
            write(weighted_v[1], line, [v * share_z for v in read(inverse_v[1], line)])
        return carry

    lax.fori_loop(0, 8, share, 0)

    def part_of(there):
        return 0.5 if there is None else jnp.where(there, 0.5, 1.0).astype(jnp.float32)

    for there, ex, i in [(has_down, 0, 0), (None, 0, 7), (None, 1, 0), (has_up, 1, 7)]:
        for ey in range(2):
            weighted[ex, ey, i] = weighted[ex, ey, i] * part_of(there)
    for there, ey, j in [(has_left, 0, 0), (None, 0, 7), (None, 1, 0), (has_right, 1, 7)]:
        for ex in range(2):
            weighted[ex, ey, :, j] = weighted[ex, ey, :, j] * part_of(there)

    zero = jnp.zeros((8, LANES), jnp.float32)

    def settle(s, carry):
        await_all(IMAGE + s, send_sem.at[IMAGE + s])
        finish_z(s)
        collect(IMAGE + s)
        right_v = views(fields.at[s])[1]
        image_v = views(fields.at[IMAGE + s])[1]

        def products(g, carry):
            terms = [[], [], []]
            for line in lines_y(g):
                for at in line:
                    r, v, w = right_v[at], image_v[at], weighted_v[1][at]
                    rw = r * w
                    terms[0].append(r * rw)
                    terms[1].append(v * rw)
                    terms[2].append(v * (v * w))
            return tuple(c + tree_sum(t) for c, t in zip(carry, terms))

        totals = lax.fori_loop(0, 8, products, (zero, zero, zero))
        for n, total in enumerate(totals):
            sums[pl.ds(n * SOURCES + s, 1), :] = jnp.sum(total, axis=0, keepdims=True)
        return carry

    lax.fori_loop(0, SOURCES, settle, 0)

    def gather(stage, slots, mine, count, at, target):
        slots[at] = mine[...]
        copies = [
            pltpu.make_async_remote_copy(
                mine,
                slots.at[at],
                sum_send.at[stage],
                sum_recv.at[stage],
                device_id=target(lax.rem(at + step, count)),
                device_id_type=MESH,
            )
            for step in range(1, count)
        ]
        for copy in copies:
            copy.start()
        others = slots.at[pl.ds(0, count - 1)]
        pltpu.make_async_copy(others, others, sum_recv.at[stage]).wait()
        pltpu.make_async_copy(others, others, sum_send.at[stage]).wait()
        total = slots[0]
        for n in range(1, count):
            total = total + slots[n]
        return total

    total = jnp.sum(sums[...], axis=1, keepdims=True)
    node16 = lax.broadcasted_iota(jnp.int32, (16, LANES), 0)
    lane16 = lax.broadcasted_iota(jnp.int32, (16, LANES), 1)
    packed = jnp.where(node16 == lane16, jnp.broadcast_to(total, (16, LANES)), 0.0)
    part[0:1, :] = jnp.sum(packed, axis=0, keepdims=True)
    part[1:2, :] = gather(0, gather_row, part.at[0:1], N_ROW, row, lambda r: (r, col))
    total = gather(1, gather_col, part.at[1:2], N_COL, col, lambda c: (row, c))
    total = jnp.broadcast_to(total, (16, LANES))
    total = jnp.sum(jnp.where(node16 == lane16, total, 0.0), axis=1, keepdims=True)
    rz_first, curvature, square = total[0:4], total[4:8], total[8:12]
    alpha = rz_first / curvature
    rz_second = alpha * alpha * square - rz_first
    beta = rz_second / rz_first
    scalars[0:4, :] = jnp.broadcast_to(alpha, (4, LANES))
    scalars[4:8, :] = jnp.broadcast_to(beta, (4, LANES))


SLOTS = 8


def update_kernel(fields, inverse, scalars, first, second, third, staging, sem):
    outputs = (first, second, third)

    def copies(n):
        return [
            pltpu.make_async_copy(
                staging.at[n % SLOTS, q], outputs[q].at[n // NODES, n % NODES], sem.at[n % SLOTS]
            )
            for q in range(3)
        ]

    def await_slot(slot):
        pltpu.make_async_copy(staging.at[slot], staging.at[slot], sem.at[slot]).wait()

    def step(n, carry):
        s, i, slot = n // NODES, n % NODES, n % SLOTS

        @pl.when(n >= SLOTS)
        def _():
            await_slot(slot)

        alpha = jnp.broadcast_to(scalars[pl.ds(s, 1), :], (8, LANES))
        beta = jnp.broadcast_to(scalars[pl.ds(s + 4, 1), :], (8, LANES))
        for ex in range(2):
            for ey in range(2):
                lanes = pl.ds((ex * 2 + ey) * LANES, LANES)
                for j in range(NODES):
                    right = fields[s, ex, ey, i, j]
                    inv = inverse[ex, ey, i, j]
                    rest = right - alpha * fields[IMAGE + s, ex, ey, i, j]
                    staging[slot, 0, j, :, lanes] = alpha * (right * inv)
                    staging[slot, 1, j, :, lanes] = rest
                    staging[slot, 2, j, :, lanes] = (rest + beta * right) * inv
        for copy in copies(n):
            copy.start()
        return carry

    steps = SOURCES * NODES
    lax.fori_loop(0, steps, step, 0)
    for n in range(steps - SLOTS, steps):
        await_slot(n % SLOTS)


def per_device(loads, conduct):
    f32 = jnp.float32
    vmem = pltpu.VMEM
    whole = pl.BlockSpec(memory_space=vmem)
    results = pl.pallas_call(
        solve_kernel,
        out_shape=[vmem((FIELDS,) + FIELD, f32), vmem(FIELD, f32), vmem((8, LANES), f32)],
        in_specs=[pl.BlockSpec(memory_space=pl.ANY)] * 2,
        out_specs=[whole] * 3,
        scratch_shapes=[vmem(FIELD, f32)] * 8
        + [
            vmem((FIELDS, 2, 2, NODES, NODES, LANES), f32),
            vmem((FIELDS, 2, 2, NODES, NODES, LANES), f32),
            vmem((FIELDS, 4, NODES, LANES), f32),
            vmem((16, LANES), f32),
            vmem((8, LANES), f32),
            vmem((N_ROW, 1, LANES), f32),
            vmem((N_COL, 1, LANES), f32),
            pltpu.SemaphoreType.DMA((SOURCES + 1,)),
            pltpu.SemaphoreType.DMA((FIELDS,)),
            pltpu.SemaphoreType.DMA((FIELDS,)),
            pltpu.SemaphoreType.DMA((2,)),
            pltpu.SemaphoreType.DMA((2,)),
        ],
        compiler_params=pltpu.CompilerParams(
            collective_id=0, has_side_effects=True, vmem_limit_bytes=40 * 1024 * 1024
        ),
    )(*[pltpu.with_memory_space_constraint(x, pltpu.HBM) for x in (loads, conduct)])
    shape = (SOURCES, NODES, NODES, NODES, 4 * LANES)
    return pl.pallas_call(
        update_kernel,
        out_shape=[jax.ShapeDtypeStruct(shape, f32)] * 3,
        in_specs=[whole] * 3,
        out_specs=[pl.BlockSpec(memory_space=pl.ANY)] * 3,
        scratch_shapes=[
            vmem((SLOTS, 3, NODES, NODES, 4 * LANES), f32),
            pltpu.SemaphoreType.DMA((SLOTS,)),
        ],
        compiler_params=pltpu.CompilerParams(vmem_limit_bytes=16 * 1024 * 1024),
    )(*[pltpu.with_memory_space_constraint(x, vmem) for x in results])


def solution(mesh):
    in_specs = (P(None, None, None, None, ("row", "col")), P(None, None, None, ("row", "col")))
    out = P(None, None, None, None, ("row", "col"))
    return jax.shard_map(
        per_device, mesh=mesh, in_specs=in_specs, out_specs=(out, out, out), check_vma=False
    )
```

```python
import functools

import jax
import jax.numpy as jnp
import numpy as np
from jax import lax
from jax.experimental import pallas as pl
from jax.experimental.pallas import tpu as pltpu
from jax.sharding import PartitionSpec as P

NODES = 8
SOURCES = 4
LANES = 128
N_ROW = 8
N_COL = 16
SCREENING = 0.5
GLL_INNER = [
    -0.8717401485096066,
    -0.5917001814331423,
    -0.2092992179024789,
    0.2092992179024789,
    0.5917001814331423,
    0.8717401485096066,
]
MESH = pl.DeviceIdType.MESH
FIELD = (2, 2, NODES, NODES, NODES, LANES)


def gll_tables():
    degree = NODES - 1
    points = np.array([-1.0] + GLL_INNER + [1.0])
    previous = points * 0.0 + 1.0
    current = points * 1.0
    for order in range(1, degree):
        following = ((2 * order + 1) * points * current - order * previous) / (order + 1)
        previous = current
        current = following
    weights = 2.0 / (degree * (degree + 1) * current**2)
    spread = points[:, None] - points[None, :]
    index_ids = np.arange(NODES)
    same = index_ids[:, None] == index_ids[None, :]
    safe_spread = np.where(same, 1.0, spread)
    deriv = np.where(same, 0.0, current[:, None] / (current[None, :] * safe_spread))
    corner = degree * (degree + 1) / 4.0
    ends = np.where(index_ids == 0, -corner, np.where(index_ids == degree, corner, 0.0))
    deriv = deriv + np.where(same, ends[None, :], 0.0)
    return deriv, weights


DERIV, WEIGHTS = gll_tables()
SQUARE = DERIV * DERIV
HALF = NODES // 2


def halves(table):
    mirrored = table[:HALF, ::-1][:, :HALF]
    direct = table[:HALF, :HALF]
    plus = (direct + mirrored) / 2.0
    minus = (direct - mirrored) / 2.0
    return plus.tolist(), minus.tolist()


SLOPE = DERIV * np.sqrt(2.0)
D_PLUS, D_MINUS = halves(SLOPE)
Q_PLUS, Q_MINUS = halves(SQUARE * 2.0)


def fold(values):
    plus = [values[i] + values[7 - i] for i in range(HALF)]
    minus = [values[i] - values[7 - i] for i in range(HALF)]
    return plus, minus


def combine(table, values, transposed):
    out = []
    for a in range(HALF):
        total = None
        for i in range(HALF):
            factor = table[i][a] if transposed else table[a][i]
            term = values[i] * factor
            total = term if total is None else total + term
        out.append(total)
    return out


def unfold(base, turn):
    low = [base[a] + turn[a] for a in range(HALF)]
    high = [base[a] - turn[a] for a in range(HALF)]
    return low + high[::-1]


def derive(values):
    plus, minus = fold(values)
    return unfold(combine(D_MINUS, minus, False), combine(D_PLUS, plus, False))


def derive_back(values):
    plus, minus = fold(values)
    return unfold(combine(D_PLUS, minus, True), combine(D_MINUS, plus, True))


def square_back(values):
    plus, minus = fold(values)
    return unfold(combine(Q_PLUS, plus, True), combine(Q_MINUS, minus, True))


def tree_sum(terms):
    while len(terms) > 1:
        terms = [a + b for a, b in zip(terms[::2], terms[1::2])]
    return terms[0]


def lines_x(t):
    return [[(t, i, j) for i in range(NODES)] for j in range(NODES)]


def lines_y(g):
    return [[(g, u, j) for j in range(NODES)] for u in range(4)]


def lines_z(g):
    return [[(g, u, pl.ds(k, 8, stride=8)) for k in range(NODES)] for u in range(4)]


def views(ref):
    along_x = ref.reshape(4, NODES, NODES, NODES, LANES)
    along_y = ref.reshape(8, 4, NODES, NODES, LANES)
    along_z = ref.reshape(8, 4, NODES * NODES, LANES)
    return along_x, along_y, along_z


def read(ref, line):
    return [ref[at] for at in line]


def write(ref, line, values):
    for at, value in zip(line, values):
        ref[at] = value


def sum_z(first, last, rows=True):
    lane = lax.broadcasted_iota(jnp.int32, (8, LANES), 1)
    after = jnp.where((lane < LANES - 1) & rows, pltpu.roll(first, LANES - 1, 1), 0.0)
    before = jnp.where((lane > 0) & rows, pltpu.roll(last, 1, 1), 0.0)
    return first + before, last + after


def assemble_inside(ref):
    for ey in range(2):
        for j in range(NODES):
            both = ref[0, ey, 7, j] + ref[1, ey, 0, j]
            ref[0, ey, 7, j] = both
            ref[1, ey, 0, j] = both
    for ex in range(2):
        for i in range(NODES):
            both = ref[ex, 0, i, 7] + ref[ex, 1, i, 0]
            ref[ex, 0, i, 7] = both
            ref[ex, 1, i, 0] = both
    strips = views(ref)[2]

    def along_z(g, carry):
        lines = [line for u in range(4) for line in lines_z(g * 4 + u)]
        ends = [(strips[line[0]], strips[line[7]]) for line in lines]
        ends = [sum_z(first, last) for first, last in ends]
        for line, (first, last) in zip(lines, ends):
            strips[line[0]] = first
            strips[line[7]] = last
        return carry

    lax.fori_loop(0, 2, along_z, 0)


DIAG = SOURCES
IMAGE = SOURCES + 1
FIELDS = 2 * SOURCES + 1


def solve_kernel(
    loads,
    conduct,
    fields,
    inverse,
    scalars,
    flux,
    flux_z,
    part_z,
    z0,
    z_face,
    coef_x,
    coef_y,
    weighted,
    from_x,
    from_y,
    from_edge,
    sums,
    part,
    gather_row,
    gather_col,
    in_sem,
    send_sem,
    recv_sem,
    sum_send,
    sum_recv,
):
    row = lax.axis_index("row")
    col = lax.axis_index("col")
    for ex in range(2):
        for ey in range(2):
            lanes = pl.ds((ex * 2 + ey) * LANES, LANES)
            pltpu.make_async_copy(
                conduct.at[:, :, :, lanes], flux.at[ex, ey], in_sem.at[SOURCES]
            ).start()
    for s in range(SOURCES):
        for ex in range(2):
            for ey in range(2):
                lanes = pl.ds((ex * 2 + ey) * LANES, LANES)
                pltpu.make_async_copy(
                    loads.at[s, :, :, :, lanes], fields.at[s, ex, ey], in_sem.at[s]
                ).start()

    has_up, has_down = row < N_ROW - 1, row > 0
    has_right, has_left = col < N_COL - 1, col > 0
    ways = [
        (1, 0, has_up),
        (-1, 0, has_down),
        (0, 1, has_right),
        (0, -1, has_left),
        (1, 1, has_up & has_right),
        (1, -1, has_up & has_left),
        (-1, 1, has_down & has_right),
        (-1, -1, has_down & has_left),
    ]
    sides_x = has_up.astype(jnp.int32) + has_down.astype(jnp.int32)
    sides_y = has_right.astype(jnp.int32) + has_left.astype(jnp.int32)
    barrier = pltpu.get_barrier_semaphore()
    corners = 0
    for dr, dc, there in ways[4:]:

        @pl.when(there)
        def _():
            pl.semaphore_signal(barrier, 1, device_id=(row + dr, col + dc), device_id_type=MESH)

        corners = corners + there.astype(jnp.int32)
    for step in range(1, N_COL):
        pl.semaphore_signal(
            barrier, 1, device_id=(row, lax.rem(col + step, N_COL)), device_id_type=MESH
        )
    for step in range(1, N_ROW):
        pl.semaphore_signal(
            barrier, 1, device_id=(lax.rem(row + step, N_ROW), col), device_id_type=MESH
        )

    def transfers(q):
        ref = fields.at[q]
        rest = pl.ds(1, NODES - 1)
        pieces = [
            (2, ref.at[0, 1, :, 7], from_y.at[q, 0, 0]),
            (2, ref.at[1, 1, rest, 7], from_y.at[q, 0, 1, rest]),
            (3, ref.at[0, 0, :, 0], from_y.at[q, 1, 0]),
            (3, ref.at[1, 0, rest, 0], from_y.at[q, 1, 1, rest]),
            (4, ref.at[1, 1, 7, 7], from_edge.at[q, 0]),
            (5, ref.at[1, 0, 7, 0], from_edge.at[q, 1]),
            (6, ref.at[0, 1, 0, 7], from_edge.at[q, 2]),
            (7, ref.at[0, 0, 0, 0], from_edge.at[q, 3]),
            (0, ref.at[1, :, 7], from_x.at[q, 0]),
            (1, ref.at[0, :, 0], from_x.at[q, 1]),
        ]
        return [
            (
                way,
                pltpu.make_async_remote_copy(
                    src,
                    dst,
                    send_sem.at[q],
                    recv_sem.at[q],
                    device_id=(row + ways[way][0], col + ways[way][1]),
                    device_id_type=MESH,
                ),
            )
            for way, src, dst in pieces
        ]

    def send(q):
        for way, copy in transfers(q):
            pl.when(ways[way][2])(copy.start)

    def await_all(q, sem):
        tiles = fields.at[q].reshape(4 * NODES * NODES, NODES, LANES)
        for across in (1, 2):
            for along in (1, 2):

                @pl.when((sides_x == across) & (sides_y == along))
                def _():
                    size = tiles.at[pl.ds(0, 16 * across + 15 * along + across * along)]
                    pltpu.make_async_copy(size, size, sem).wait()

    def collect(q):
        await_all(q, recv_sem.at[q])
        ref = fields.at[q]
        for ey in range(2):
            for j in range(NODES):
                ref[0, ey, 0, j] = ref[0, ey, 0, j] + from_x[q, 0, ey, j]
                ref[1, ey, 7, j] = ref[1, ey, 7, j] + from_x[q, 1, ey, j]
        for ex in range(2):
            for i in range(NODES):
                at = (0, 7) if (ex, i) == (1, 0) else (ex, i)
                ref[ex, 0, i, 0] = ref[ex, 0, i, 0] + from_y[(q, 0) + at]
                ref[ex, 1, i, 7] = ref[ex, 1, i, 7] + from_y[(q, 1) + at]
        for corner in range(4):
            ex, ey = corner // 2, corner % 2
            at = (ex, ey, 7 * ex, 7 * ey)
            ref[at] = ref[at] + from_edge[q, corner]

    def clear(ref, there, pick):
        @pl.when(jnp.logical_not(there))
        def _():
            def body(q, carry):
                target = pick(ref, q)
                target[...] = jnp.zeros_like(target)
                return carry

            lax.fori_loop(0, FIELDS, body, 0)

    clear(from_x, has_down, lambda ref, q: ref.at[q, 0])
    clear(from_x, has_up, lambda ref, q: ref.at[q, 1])
    clear(from_y, has_left, lambda ref, q: ref.at[q, 0])
    clear(from_y, has_right, lambda ref, q: ref.at[q, 1])
    clear(from_edge, has_down & has_left, lambda ref, q: ref.at[q, 0])
    clear(from_edge, has_down & has_right, lambda ref, q: ref.at[q, 1])
    clear(from_edge, has_up & has_left, lambda ref, q: ref.at[q, 2])
    clear(from_edge, has_up & has_right, lambda ref, q: ref.at[q, 3])
    sums[...] = jnp.zeros_like(sums)

    flux_v = views(flux)
    flux_zv = views(flux_z)
    part_v = views(part_z)
    weighted_v = views(weighted)
    inverse_v = views(inverse)
    diag_v = views(fields.at[DIAG])

    pltpu.make_async_copy(flux, flux, in_sem.at[SOURCES]).wait()
    node = lax.broadcasted_iota(jnp.int32, (8, LANES), 0)
    lane = lax.broadcasted_iota(jnp.int32, (8, LANES), 1)
    weight_z = jnp.full((8, LANES), WEIGHTS[3], jnp.float32)
    for k in (0, 1, 2):
        ends = (node == k) | (node == 7 - k)
        weight_z = jnp.where(ends, jnp.float32(WEIGHTS[k]), weight_z)

    def diag_x(t, carry):
        for j, line in enumerate(lines_x(t)):
            values = [
                v * (weight_z * float(SCREENING * WEIGHTS[i] * WEIGHTS[j]))
                for i, v in enumerate(read(flux_v[0], line))
            ]
            write(flux_v[0], line, values)
            write(diag_v[0], line, [r + v for r, v in zip(square_back(values), values)])
        return carry

    def diag_yz(g, carry):
        for line, strip in zip(lines_y(g), lines_z(g)):
            before = read(diag_v[1], line)
            result_y = square_back(read(flux_v[1], line))
            values = read(flux_v[2], strip)
            write(flux_zv[1], line, values)
            write(part_v[2], strip, square_back(values))
            write(diag_v[1], line, [b + r for b, r in zip(before, result_y)])
        return carry

    def diag_sum(g, carry):
        for line in lines_y(g):
            both = zip(read(diag_v[1], line), read(part_v[1], line))
            write(diag_v[1], line, [b + r for b, r in both])
        return carry

    lax.fori_loop(0, 4, diag_x, 0)
    lax.fori_loop(0, 8, diag_yz, 0)
    lax.fori_loop(0, 8, diag_sum, 0)

    def prepare(n, carry):
        q = lax.rem(n + DIAG, DIAG + 1)

        @pl.when(n > 0)
        def _():
            pltpu.make_async_copy(fields.at[q], fields.at[q], in_sem.at[q]).wait()

        assemble_inside(fields.at[q])

        @pl.when(n == 0)
        def _():
            pl.semaphore_wait(barrier, N_ROW - 1 + N_COL - 1 + corners)

        send(q)
        return carry

    lax.fori_loop(0, DIAG + 1, prepare, 0)

    def invert(g, carry):
        for line in lines_y(g):
            write(inverse_v[1], line, [1.0 / v for v in read(diag_v[1], line)])
        return carry


    def stiff(values, weight):
        return derive_back([g * w for g, w in zip(derive(values), weight)])

    empty = jnp.zeros((8, LANES), jnp.float32)

    def inside_part(s):
        right_v = views(fields.at[s])
        z0_v = views(z0.at[s])

        def scale(g, carry):
            for line in lines_y(g):
                both = zip(read(right_v[1], line), read(inverse_v[1], line))
                write(z0_v[1], line, [v * d for v, d in both])
            return carry

        lax.fori_loop(0, 8, scale, 0)
        for ex in range(2):
            for ey in range(2):
                for n in range(NODES):
                    z0[s, ex, ey, 7 * ex, n] = empty
                    z0[s, ex, ey, n, 7 * ey] = empty

    def begin(s, carry):
        inside_part(s)
        z0_v = views(z0.at[s])
        image_v = views(fields.at[IMAGE + s])

        def stiff_x(t, carry):
            end = lax.rem(t, 2)
            lines = pl.ds(1 - end, NODES - 1)
            values, weight = z0_v[0].at[t, :, lines], flux_v[0].at[t, :, lines]
            result = image_v[0].at[t, :, lines]
            for n in range(NODES - 1):
                line = [(i, n) for i in range(NODES)]
                v, w = read(values, line), read(weight, line)
                out = stiff(v, w)
                write(result, line, [r + b * a for r, b, a in zip(out, w, v)])
            for i in range(NODES):
                image_v[0][t, i, 7 * end] = empty
            return carry

        def stiff_y(t, carry):
            planes = pl.ds(1 - t // 2, NODES - 1)
            values, weight = z0_v[0].at[t, planes], flux_v[0].at[t, planes]
            result = image_v[0].at[t, planes]
            for u in range(NODES - 1):
                line = [(u, j) for j in range(NODES)]
                out = stiff(read(values, line), read(weight, line))
                write(result, line, [a + r for a, r in zip(read(result, line), out)])
            return carry

        lax.fori_loop(0, 4, stiff_x, 0)
        lax.fori_loop(0, 4, stiff_y, 0)
        return carry

    def finish_z(s):
        z0_strip = z0.at[s].reshape(4, NODES, NODES * NODES, LANES)
        target = fields.at[IMAGE + s]
        strip = target.reshape(4, NODES, NODES * NODES, LANES)

        def stiff_z(t, carry):
            planes = pl.ds(1 - t // 2, NODES - 1)
            values, weight = z0_strip.at[t, planes], flux_zv[0].at[t, planes]
            result = strip.at[t, planes]
            off_face = node != 7 * lax.rem(t, 2)
            for u in range(NODES - 1):
                strips = [(u, pl.ds(k, 8, stride=8)) for k in range(NODES)]
                out = stiff(read(values, strips), [weight[u, k] for k in range(NODES)])
                out = [a + r for a, r in zip(read(result, strips), out)]
                out[0], out[7] = sum_z(out[0], out[7], off_face)
                write(result, strips, out)
            return carry

        lax.fori_loop(0, 4, stiff_z, 0)
        for ey in range(2):
            for j in range(1 - ey, NODES - ey):
                both = target[0, ey, 7, j] + target[1, ey, 0, j]
                target[0, ey, 7, j] = both
                target[1, ey, 0, j] = both
        for ex in range(2):
            for i in range(1 - ex, NODES - ex):
                both = target[ex, 0, i, 7] + target[ex, 1, i, 0]
                target[ex, 0, i, 7] = both
                target[ex, 1, i, 0] = both

    lax.fori_loop(0, 8, invert, 0)

    lax.fori_loop(0, SOURCES, begin, 0)

    for side in range(2):
        end = 7 * side

        def lean(other, carry):
            for n in range(NODES):
                weight = [flux[side, other, a, n] for a in range(NODES)]
                result = derive_back([w * float(SLOPE[a, end]) for a, w in enumerate(weight)])
                result[end] = result[end] + weight[end]
                for i in range(NODES):
                    coef_x[side, other, i, n] = result[i]
                weight = [flux[other, side, n, b] for b in range(NODES)]
                result = derive_back([w * float(SLOPE[b, end]) for b, w in enumerate(weight)])
                for j in range(NODES):
                    coef_y[other, side, n, j] = result[j]
            return carry

        lax.fori_loop(0, 2, lean, 0)

    await_all(DIAG, send_sem.at[DIAG])
    collect(DIAG)
    for ex in range(2):
        for ey in range(2):
            for n in range(NODES):
                for at in ((ex, ey, 7 * ex, n), (ex, ey, n, 7 * ey)):
                    inverse[at] = 1.0 / fields[(DIAG,) + at]

    face_v = views(z_face)[0]
    face_strip = z_face.reshape(4, NODES, NODES * NODES, LANES)
    face_flat = z_face.reshape(4, NODES**3, LANES)
    flux_flat = flux.reshape(4, NODES**3, LANES)
    coef_xv = views(coef_x)[0]
    coef_yv = views(coef_y)[0]

    def correct(s, carry):
        await_all(s, send_sem.at[s])
        collect(s)
        for ex in range(2):
            for ey in range(2):
                for n in range(NODES):
                    for at in ((ex, ey, 7 * ex, n), (ex, ey, n, 7 * ey)):
                        z_face[at] = fields[(s,) + at] * inverse[at]
        target = fields.at[IMAGE + s]
        image_v = views(target)[0]
        image_strip = target.reshape(4, NODES, NODES * NODES, LANES)
        image_flat = target.reshape(4, NODES**3, LANES)

        def faces(t, carry):
            i0 = 7 * (t // 2)
            j0 = 7 * lax.rem(t, 2)
            nodes = range(NODES)
            values = [face_v[t, i, j0] for i in nodes]
            weight = [flux_v[0][t, i, j0] for i in nodes]
            result = stiff(values, weight)
            result = [r + w * v for r, w, v in zip(result, weight, values)]
            result_y = stiff([face_v[t, i0, j] for j in nodes], [flux_v[0][t, i0, j] for j in nodes])
            strips = [(t, i0, pl.ds(k, 8, stride=8)) for k in nodes]
            result_z = stiff(read(face_strip, strips), [flux_zv[0][t, i0, k] for k in nodes])
            columns = [(t, pl.ds(j0 * 8 + k, 8, stride=64)) for k in nodes]
            values = [jnp.where(node == i0, 0.0, v) for v in read(face_flat, columns)]
            result_c = stiff(values, read(flux_flat, columns))
            for at, r in zip(strips, result_z):
                image_strip[at] = image_strip[at] + r
            for at, r in zip(columns, result_c):
                image_flat[at] = image_flat[at] + r
            for i, r in zip(nodes, result):
                image_v[t, i, j0] = image_v[t, i, j0] + r
            for j, r in zip(nodes, result_y):
                image_v[t, i0, j] = image_v[t, i0, j] + r
            ends_x = [jnp.where(j0 == j, 0.0, face_v[t, i0, j]) for j in nodes]
            ends_y = [jnp.where(i0 == i, 0.0, face_v[t, i, j0]) for i in nodes]
            for i in nodes:
                for j in nodes:
                    more = coef_xv[t, i, j] * ends_x[j] + coef_yv[t, i, j] * ends_y[i]
                    image_v[t, i, j] = image_v[t, i, j] + more
            return carry

        lax.fori_loop(0, 4, faces, 0)
        for ey in range(2):
            both = target[0, ey, 7, 7 * ey] + target[1, ey, 0, 7 * ey]
            target[0, ey, 7, 7 * ey] = both
            target[1, ey, 0, 7 * ey] = both
        for ex in range(2):
            both = target[ex, 0, 7 * ex, 7] + target[ex, 1, 7 * ex, 0]
            target[ex, 0, 7 * ex, 7] = both
            target[ex, 1, 7 * ex, 0] = both
        ends = []
        for t in range(4):
            i0, j0 = 7 * (t // 2), 7 * (t % 2)
            strips = [(t, i0, pl.ds(k, 8, stride=8)) for k in (0, 7)]
            columns = [(t, pl.ds(j0 * 8 + k, 8, stride=64)) for k in (0, 7)]
            ends.append((image_strip, strips, read(image_strip, strips)))
            ends.append((image_flat, columns, read(image_flat, columns)))
        for ref, at, (first, last) in ends:
            write(ref, at, sum_z(first, last))
        send(IMAGE + s)
        return carry

    lax.fori_loop(0, SOURCES, correct, 0)

    twice_z = ((node == 0) & (lane > 0)) | ((node == 7) & (lane < LANES - 1))
    share_z = jnp.where(twice_z, jnp.float32(0.5), jnp.float32(1.0))

    def share(g, carry):
        for line in lines_y(g):
            write(weighted_v[1], line, [v * share_z for v in read(inverse_v[1], line)])
        return carry

    lax.fori_loop(0, 8, share, 0)

    def part_of(there):
        return 0.5 if there is None else jnp.where(there, 0.5, 1.0).astype(jnp.float32)

    for there, ex, i in [(has_down, 0, 0), (None, 0, 7), (None, 1, 0), (has_up, 1, 7)]:
        for ey in range(2):
            weighted[ex, ey, i] = weighted[ex, ey, i] * part_of(there)
    for there, ey, j in [(has_left, 0, 0), (None, 0, 7), (None, 1, 0), (has_right, 1, 7)]:
        for ex in range(2):
            weighted[ex, ey, :, j] = weighted[ex, ey, :, j] * part_of(there)

    zero = jnp.zeros((8, LANES), jnp.float32)

    def settle(s, carry):
        await_all(IMAGE + s, send_sem.at[IMAGE + s])
        finish_z(s)
        collect(IMAGE + s)
        right_v = views(fields.at[s])[1]
        image_v = views(fields.at[IMAGE + s])[1]

        def products(g, carry):
            terms = [[], [], []]
            for line in lines_y(g):
                for at in line:
                    r, v, w = right_v[at], image_v[at], weighted_v[1][at]
                    rw = r * w
                    terms[0].append(r * rw)
                    terms[1].append(v * rw)
                    terms[2].append(v * (v * w))
            return tuple(c + tree_sum(t) for c, t in zip(carry, terms))

        totals = lax.fori_loop(0, 8, products, (zero, zero, zero))
        for n, total in enumerate(totals):
            sums[pl.ds(n * SOURCES + s, 1), :] = jnp.sum(total, axis=0, keepdims=True)
        return carry

    lax.fori_loop(0, SOURCES, settle, 0)

    def gather(stage, slots, mine, count, at, target):
        slots[at] = mine[...]
        copies = [
            pltpu.make_async_remote_copy(
                mine,
                slots.at[at],
                sum_send.at[stage],
                sum_recv.at[stage],
                device_id=target(lax.rem(at + step, count)),
                device_id_type=MESH,
            )
            for step in range(1, count)
        ]
        for copy in copies:
            copy.start()
        others = slots.at[pl.ds(0, count - 1)]
        pltpu.make_async_copy(others, others, sum_recv.at[stage]).wait()
        return tree_sum([slots[n] for n in range(count)]), others

    total = jnp.sum(sums[...], axis=1, keepdims=True)
    node16 = lax.broadcasted_iota(jnp.int32, (16, LANES), 0)
    lane16 = lax.broadcasted_iota(jnp.int32, (16, LANES), 1)
    packed = jnp.where(node16 == lane16, jnp.broadcast_to(total, (16, LANES)), 0.0)
    part[0:1, :] = jnp.sum(packed, axis=0, keepdims=True)
    total, sent = gather(0, gather_row, part.at[0:1], N_ROW, row, lambda r: (r, col))
    part[1:2, :] = total
    total, sent_too = gather(1, gather_col, part.at[1:2], N_COL, col, lambda c: (row, c))
    pltpu.make_async_copy(sent, sent, sum_send.at[0]).wait()
    pltpu.make_async_copy(sent_too, sent_too, sum_send.at[1]).wait()
    total = jnp.broadcast_to(total, (16, LANES))
    total = jnp.sum(jnp.where(node16 == lane16, total, 0.0), axis=1, keepdims=True)
    rz_first, curvature, square = total[0:4], total[4:8], total[8:12]
    alpha = rz_first / curvature
    rz_second = alpha * alpha * square - rz_first
    beta = rz_second / rz_first
    scalars[0:4, :] = jnp.broadcast_to(alpha, (4, LANES))
    scalars[4:8, :] = jnp.broadcast_to(beta, (4, LANES))


SLOTS = 8


def update_kernel(fields, inverse, scalars, first, second, third, staging, sem):
    outputs = (first, second, third)

    def copies(n):
        return [
            pltpu.make_async_copy(
                staging.at[n % SLOTS, q], outputs[q].at[n // NODES, n % NODES], sem.at[n % SLOTS]
            )
            for q in range(3)
        ]

    def await_slot(slot):
        pltpu.make_async_copy(staging.at[slot], staging.at[slot], sem.at[slot]).wait()

    def step(n, carry):
        s, i, slot = n // NODES, n % NODES, n % SLOTS

        @pl.when(n >= SLOTS)
        def _():
            await_slot(slot)

        alpha = jnp.broadcast_to(scalars[pl.ds(s, 1), :], (8, LANES))
        beta = jnp.broadcast_to(scalars[pl.ds(s + 4, 1), :], (8, LANES))
        for ex in range(2):
            for ey in range(2):
                lanes = pl.ds((ex * 2 + ey) * LANES, LANES)
                for j in range(NODES):
                    right = fields[s, ex, ey, i, j]
                    inv = inverse[ex, ey, i, j]
                    rest = right - alpha * fields[IMAGE + s, ex, ey, i, j]
                    staging[slot, 0, j, :, lanes] = alpha * (right * inv)
                    staging[slot, 1, j, :, lanes] = rest
                    staging[slot, 2, j, :, lanes] = (rest + beta * right) * inv
        for copy in copies(n):
            copy.start()
        return carry

    steps = SOURCES * NODES
    lax.fori_loop(0, steps, step, 0)
    for n in range(steps - SLOTS, steps):
        await_slot(n % SLOTS)


def per_device(loads, conduct):
    f32 = jnp.float32
    vmem = pltpu.VMEM
    whole = pl.BlockSpec(memory_space=vmem)
    results = pl.pallas_call(
        solve_kernel,
        out_shape=[vmem((FIELDS,) + FIELD, f32), vmem(FIELD, f32), vmem((8, LANES), f32)],
        in_specs=[pl.BlockSpec(memory_space=pl.ANY)] * 2,
        out_specs=[whole] * 3,
        scratch_shapes=[vmem(FIELD, f32)] * 3
        + [vmem((SOURCES,) + FIELD, f32)]
        + [vmem(FIELD, f32)] * 4
        + [
            vmem((FIELDS, 2, 2, NODES, NODES, LANES), f32),
            vmem((FIELDS, 2, 2, NODES, NODES, LANES), f32),
            vmem((FIELDS, 4, NODES, LANES), f32),
            vmem((16, LANES), f32),
            vmem((8, LANES), f32),
            vmem((N_ROW, 1, LANES), f32),
            vmem((N_COL, 1, LANES), f32),
            pltpu.SemaphoreType.DMA((SOURCES + 1,)),
            pltpu.SemaphoreType.DMA((FIELDS,)),
            pltpu.SemaphoreType.DMA((FIELDS,)),
            pltpu.SemaphoreType.DMA((2,)),
            pltpu.SemaphoreType.DMA((2,)),
        ],
        compiler_params=pltpu.CompilerParams(
            collective_id=0, has_side_effects=True, vmem_limit_bytes=40 * 1024 * 1024
        ),
    )(*[pltpu.with_memory_space_constraint(x, pltpu.HBM) for x in (loads, conduct)])
    shape = (SOURCES, NODES, NODES, NODES, 4 * LANES)
    return pl.pallas_call(
        update_kernel,
        out_shape=[jax.ShapeDtypeStruct(shape, f32)] * 3,
        in_specs=[whole] * 3,
        out_specs=[pl.BlockSpec(memory_space=pl.ANY)] * 3,
        scratch_shapes=[
            vmem((SLOTS, 3, NODES, NODES, 4 * LANES), f32),
            pltpu.SemaphoreType.DMA((SLOTS,)),
        ],
        compiler_params=pltpu.CompilerParams(vmem_limit_bytes=16 * 1024 * 1024),
    )(*[pltpu.with_memory_space_constraint(x, vmem) for x in results])


def solution(mesh):
    in_specs = (P(None, None, None, None, ("row", "col")), P(None, None, None, ("row", "col")))
    out = P(None, None, None, None, ("row", "col"))
    return jax.shard_map(
        per_device, mesh=mesh, in_specs=in_specs, out_specs=(out, out, out), check_vma=False
    )
```

```python
import functools

import jax
import jax.numpy as jnp
import numpy as np
from jax import lax
from jax.experimental import pallas as pl
from jax.experimental.pallas import tpu as pltpu
from jax.sharding import PartitionSpec as P

NODES = 8
SOURCES = 4
LANES = 128
N_ROW = 8
N_COL = 16
SCREENING = 0.5
GLL_INNER = [
    -0.8717401485096066,
    -0.5917001814331423,
    -0.2092992179024789,
    0.2092992179024789,
    0.5917001814331423,
    0.8717401485096066,
]
MESH = pl.DeviceIdType.MESH
FIELD = (2, 2, NODES, NODES, NODES, LANES)


def gll_tables():
    degree = NODES - 1
    points = np.array([-1.0] + GLL_INNER + [1.0])
    previous = points * 0.0 + 1.0
    current = points * 1.0
    for order in range(1, degree):
        following = ((2 * order + 1) * points * current - order * previous) / (order + 1)
        previous = current
        current = following
    weights = 2.0 / (degree * (degree + 1) * current**2)
    spread = points[:, None] - points[None, :]
    index_ids = np.arange(NODES)
    same = index_ids[:, None] == index_ids[None, :]
    safe_spread = np.where(same, 1.0, spread)
    deriv = np.where(same, 0.0, current[:, None] / (current[None, :] * safe_spread))
    corner = degree * (degree + 1) / 4.0
    ends = np.where(index_ids == 0, -corner, np.where(index_ids == degree, corner, 0.0))
    deriv = deriv + np.where(same, ends[None, :], 0.0)
    return deriv, weights


DERIV, WEIGHTS = gll_tables()
SQUARE = DERIV * DERIV
HALF = NODES // 2


def halves(table):
    mirrored = table[:HALF, ::-1][:, :HALF]
    direct = table[:HALF, :HALF]
    plus = (direct + mirrored) / 2.0
    minus = (direct - mirrored) / 2.0
    return plus.tolist(), minus.tolist()


SLOPE = DERIV * np.sqrt(2.0)
D_PLUS, D_MINUS = halves(SLOPE)
Q_PLUS, Q_MINUS = halves(SQUARE * 2.0)


def fold(values):
    plus = [values[i] + values[7 - i] for i in range(HALF)]
    minus = [values[i] - values[7 - i] for i in range(HALF)]
    return plus, minus


def combine(table, values, transposed):
    out = []
    for a in range(HALF):
        total = None
        for i in range(HALF):
            factor = table[i][a] if transposed else table[a][i]
            term = values[i] * factor
            total = term if total is None else total + term
        out.append(total)
    return out


def unfold(base, turn):
    low = [base[a] + turn[a] for a in range(HALF)]
    high = [base[a] - turn[a] for a in range(HALF)]
    return low + high[::-1]


def derive(values):
    plus, minus = fold(values)
    return unfold(combine(D_MINUS, minus, False), combine(D_PLUS, plus, False))


def derive_back(values):
    plus, minus = fold(values)
    return unfold(combine(D_PLUS, minus, True), combine(D_MINUS, plus, True))


def square_back(values):
    plus, minus = fold(values)
    return unfold(combine(Q_PLUS, plus, True), combine(Q_MINUS, minus, True))


def tree_sum(terms):
    while len(terms) > 1:
        terms = [a + b for a, b in zip(terms[::2], terms[1::2])]
    return terms[0]


def lines_x(t):
    return [[(t, i, j) for i in range(NODES)] for j in range(NODES)]


def lines_y(g):
    return [[(g, u, j) for j in range(NODES)] for u in range(4)]


def lines_z(g):
    return [[(g, u, pl.ds(k, 8, stride=8)) for k in range(NODES)] for u in range(4)]


def views(ref):
    along_x = ref.reshape(4, NODES, NODES, NODES, LANES)
    along_y = ref.reshape(8, 4, NODES, NODES, LANES)
    along_z = ref.reshape(8, 4, NODES * NODES, LANES)
    return along_x, along_y, along_z


def read(ref, line):
    return [ref[at] for at in line]


def write(ref, line, values):
    for at, value in zip(line, values):
        ref[at] = value


def sum_z(first, last, rows=True):
    lane = lax.broadcasted_iota(jnp.int32, (8, LANES), 1)
    after = jnp.where((lane < LANES - 1) & rows, pltpu.roll(first, LANES - 1, 1), 0.0)
    before = jnp.where((lane > 0) & rows, pltpu.roll(last, 1, 1), 0.0)
    return first + before, last + after


def assemble_inside(ref):
    for ey in range(2):
        for j in range(NODES):
            both = ref[0, ey, 7, j] + ref[1, ey, 0, j]
            ref[0, ey, 7, j] = both
            ref[1, ey, 0, j] = both
    for ex in range(2):
        for i in range(NODES):
            both = ref[ex, 0, i, 7] + ref[ex, 1, i, 0]
            ref[ex, 0, i, 7] = both
            ref[ex, 1, i, 0] = both
    strips = views(ref)[2]

    def along_z(g, carry):
        lines = [line for u in range(4) for line in lines_z(g * 4 + u)]
        ends = [(strips[line[0]], strips[line[7]]) for line in lines]
        ends = [sum_z(first, last) for first, last in ends]
        for line, (first, last) in zip(lines, ends):
            strips[line[0]] = first
            strips[line[7]] = last
        return carry

    lax.fori_loop(0, 2, along_z, 0)


DIAG = SOURCES
IMAGE = SOURCES + 1
FIELDS = 2 * SOURCES + 1


def solve_kernel(
    loads,
    conduct,
    fields,
    inverse,
    scalars,
    flux,
    flux_z,
    part_z,
    z0,
    z_face,
    coef_x,
    coef_y,
    weighted,
    from_x,
    from_y,
    from_edge,
    sums,
    part,
    gather_row,
    gather_col,
    in_sem,
    send_sem,
    recv_sem,
    sum_send,
    sum_recv,
):
    row = lax.axis_index("row")
    col = lax.axis_index("col")
    for ex in range(2):
        for ey in range(2):
            lanes = pl.ds((ex * 2 + ey) * LANES, LANES)
            pltpu.make_async_copy(
                conduct.at[:, :, :, lanes], flux.at[ex, ey], in_sem.at[SOURCES]
            ).start()
    for s in range(SOURCES):
        for ex in range(2):
            for ey in range(2):
                lanes = pl.ds((ex * 2 + ey) * LANES, LANES)
                pltpu.make_async_copy(
                    loads.at[s, :, :, :, lanes], fields.at[s, ex, ey], in_sem.at[s]
                ).start()

    has_up, has_down = row < N_ROW - 1, row > 0
    has_right, has_left = col < N_COL - 1, col > 0
    ways = [
        (1, 0, has_up),
        (-1, 0, has_down),
        (0, 1, has_right),
        (0, -1, has_left),
        (1, 1, has_up & has_right),
        (1, -1, has_up & has_left),
        (-1, 1, has_down & has_right),
        (-1, -1, has_down & has_left),
    ]
    sides_x = has_up.astype(jnp.int32) + has_down.astype(jnp.int32)
    sides_y = has_right.astype(jnp.int32) + has_left.astype(jnp.int32)
    barrier = pltpu.get_barrier_semaphore()
    corners = 0
    for dr, dc, there in ways[4:]:

        @pl.when(there)
        def _():
            pl.semaphore_signal(barrier, 1, device_id=(row + dr, col + dc), device_id_type=MESH)

        corners = corners + there.astype(jnp.int32)
    for step in range(1, N_COL):
        pl.semaphore_signal(
            barrier, 1, device_id=(row, lax.rem(col + step, N_COL)), device_id_type=MESH
        )
    for step in range(1, N_ROW):
        pl.semaphore_signal(
            barrier, 1, device_id=(lax.rem(row + step, N_ROW), col), device_id_type=MESH
        )

    def transfers(q):
        ref = fields.at[q]
        rest = pl.ds(1, NODES - 1)
        pieces = [
            (2, ref.at[0, 1, :, 7], from_y.at[q, 0, 0]),
            (2, ref.at[1, 1, rest, 7], from_y.at[q, 0, 1, rest]),
            (3, ref.at[0, 0, :, 0], from_y.at[q, 1, 0]),
            (3, ref.at[1, 0, rest, 0], from_y.at[q, 1, 1, rest]),
            (4, ref.at[1, 1, 7, 7], from_edge.at[q, 0]),
            (5, ref.at[1, 0, 7, 0], from_edge.at[q, 1]),
            (6, ref.at[0, 1, 0, 7], from_edge.at[q, 2]),
            (7, ref.at[0, 0, 0, 0], from_edge.at[q, 3]),
            (0, ref.at[1, :, 7], from_x.at[q, 0]),
            (1, ref.at[0, :, 0], from_x.at[q, 1]),
        ]
        return [
            (
                way,
                pltpu.make_async_remote_copy(
                    src,
                    dst,
                    send_sem.at[q],
                    recv_sem.at[q],
                    device_id=(row + ways[way][0], col + ways[way][1]),
                    device_id_type=MESH,
                ),
            )
            for way, src, dst in pieces
        ]

    def send(q):
        for way, copy in transfers(q):
            pl.when(ways[way][2])(copy.start)

    def await_all(q, sem):
        tiles = fields.at[q].reshape(4 * NODES * NODES, NODES, LANES)
        for across in (1, 2):
            for along in (1, 2):

                @pl.when((sides_x == across) & (sides_y == along))
                def _():
                    size = tiles.at[pl.ds(0, 16 * across + 15 * along + across * along)]
                    pltpu.make_async_copy(size, size, sem).wait()

    def collect(q):
        await_all(q, recv_sem.at[q])
        ref = fields.at[q]
        for ey in range(2):
            for j in range(NODES):
                ref[0, ey, 0, j] = ref[0, ey, 0, j] + from_x[q, 0, ey, j]
                ref[1, ey, 7, j] = ref[1, ey, 7, j] + from_x[q, 1, ey, j]
        for ex in range(2):
            for i in range(NODES):
                at = (0, 7) if (ex, i) == (1, 0) else (ex, i)
                ref[ex, 0, i, 0] = ref[ex, 0, i, 0] + from_y[(q, 0) + at]
                ref[ex, 1, i, 7] = ref[ex, 1, i, 7] + from_y[(q, 1) + at]
        for corner in range(4):
            ex, ey = corner // 2, corner % 2
            at = (ex, ey, 7 * ex, 7 * ey)
            ref[at] = ref[at] + from_edge[q, corner]

    def clear(ref, there, pick):
        @pl.when(jnp.logical_not(there))
        def _():
            def body(q, carry):
                target = pick(ref, q)
                target[...] = jnp.zeros_like(target)
                return carry

            lax.fori_loop(0, FIELDS, body, 0)

    clear(from_x, has_down, lambda ref, q: ref.at[q, 0])
    clear(from_x, has_up, lambda ref, q: ref.at[q, 1])
    clear(from_y, has_left, lambda ref, q: ref.at[q, 0])
    clear(from_y, has_right, lambda ref, q: ref.at[q, 1])
    clear(from_edge, has_down & has_left, lambda ref, q: ref.at[q, 0])
    clear(from_edge, has_down & has_right, lambda ref, q: ref.at[q, 1])
    clear(from_edge, has_up & has_left, lambda ref, q: ref.at[q, 2])
    clear(from_edge, has_up & has_right, lambda ref, q: ref.at[q, 3])
    sums[...] = jnp.zeros_like(sums)

    flux_v = views(flux)
    flux_zv = views(flux_z)
    part_v = views(part_z)
    weighted_v = views(weighted)
    inverse_v = views(inverse)
    diag_v = views(fields.at[DIAG])

    pltpu.make_async_copy(flux, flux, in_sem.at[SOURCES]).wait()
    node = lax.broadcasted_iota(jnp.int32, (8, LANES), 0)
    lane = lax.broadcasted_iota(jnp.int32, (8, LANES), 1)
    weight_z = jnp.full((8, LANES), WEIGHTS[3], jnp.float32)
    for k in (0, 1, 2):
        ends = (node == k) | (node == 7 - k)
        weight_z = jnp.where(ends, jnp.float32(WEIGHTS[k]), weight_z)

    def diag_x(t, carry):
        for j, line in enumerate(lines_x(t)):
            values = [
                v * (weight_z * float(SCREENING * WEIGHTS[i] * WEIGHTS[j]))
                for i, v in enumerate(read(flux_v[0], line))
            ]
            write(flux_v[0], line, values)
            write(diag_v[0], line, [r + v for r, v in zip(square_back(values), values)])
        return carry

    def diag_yz(g, carry):
        for line, strip in zip(lines_y(g), lines_z(g)):
            before = read(diag_v[1], line)
            result_y = square_back(read(flux_v[1], line))
            values = read(flux_v[2], strip)
            write(flux_zv[1], line, values)
            write(part_v[2], strip, square_back(values))
            write(diag_v[1], line, [b + r for b, r in zip(before, result_y)])
        return carry

    def diag_sum(g, carry):
        for line in lines_y(g):
            both = zip(read(diag_v[1], line), read(part_v[1], line))
            write(diag_v[1], line, [b + r for b, r in both])
        return carry

    lax.fori_loop(0, 4, diag_x, 0)
    lax.fori_loop(0, 8, diag_yz, 0)
    lax.fori_loop(0, 8, diag_sum, 0)

    for side in range(2):
        end = 7 * side

        def lean(other, carry):
            for n in range(NODES):
                weight = [flux[side, other, a, n] for a in range(NODES)]
                result = derive_back([w * float(SLOPE[a, end]) for a, w in enumerate(weight)])
                result[end] = result[end] + weight[end]
                for i in range(NODES):
                    coef_x[side, other, i, n] = result[i]
                weight = [flux[other, side, n, b] for b in range(NODES)]
                result = derive_back([w * float(SLOPE[b, end]) for b, w in enumerate(weight)])
                for j in range(NODES):
                    coef_y[other, side, n, j] = result[j]
            return carry

        lax.fori_loop(0, 2, lean, 0)

    def prepare(n, carry):
        q = lax.rem(n + DIAG, DIAG + 1)

        @pl.when(n > 0)
        def _():
            pltpu.make_async_copy(fields.at[q], fields.at[q], in_sem.at[q]).wait()

        assemble_inside(fields.at[q])

        @pl.when(n == 0)
        def _():
            pl.semaphore_wait(barrier, N_ROW - 1 + N_COL - 1 + corners)

        send(q)
        return carry

    lax.fori_loop(0, DIAG + 1, prepare, 0)

    def invert(g, carry):
        for line in lines_y(g):
            write(inverse_v[1], line, [1.0 / v for v in read(diag_v[1], line)])
        return carry


    def stiff(values, weight):
        return derive_back([g * w for g, w in zip(derive(values), weight)])

    empty = jnp.zeros((8, LANES), jnp.float32)

    def inside_part(s):
        right_v = views(fields.at[s])
        z0_v = views(z0.at[s])

        def scale(g, carry):
            for line in lines_y(g):
                both = zip(read(right_v[1], line), read(inverse_v[1], line))
                write(z0_v[1], line, [v * d for v, d in both])
            return carry

        lax.fori_loop(0, 8, scale, 0)
        for ex in range(2):
            for ey in range(2):
                for n in range(NODES):
                    z0[s, ex, ey, 7 * ex, n] = empty
                    z0[s, ex, ey, n, 7 * ey] = empty

    def begin(s, carry):
        inside_part(s)
        z0_v = views(z0.at[s])
        image_v = views(fields.at[IMAGE + s])

        def stiff_x(t, carry):
            end = lax.rem(t, 2)
            lines = pl.ds(1 - end, NODES - 1)
            values, weight = z0_v[0].at[t, :, lines], flux_v[0].at[t, :, lines]
            result = image_v[0].at[t, :, lines]
            for n in range(NODES - 1):
                line = [(i, n) for i in range(NODES)]
                v, w = read(values, line), read(weight, line)
                out = stiff(v, w)
                write(result, line, [r + b * a for r, b, a in zip(out, w, v)])
            for i in range(NODES):
                image_v[0][t, i, 7 * end] = empty
            return carry

        def stiff_y(t, carry):
            planes = pl.ds(1 - t // 2, NODES - 1)
            values, weight = z0_v[0].at[t, planes], flux_v[0].at[t, planes]
            result = image_v[0].at[t, planes]
            for u in range(NODES - 1):
                line = [(u, j) for j in range(NODES)]
                out = stiff(read(values, line), read(weight, line))
                write(result, line, [a + r for a, r in zip(read(result, line), out)])
            return carry

        lax.fori_loop(0, 4, stiff_x, 0)
        lax.fori_loop(0, 4, stiff_y, 0)
        return carry

    def finish_z(s):
        z0_strip = z0.at[s].reshape(4, NODES, NODES * NODES, LANES)
        target = fields.at[IMAGE + s]
        strip = target.reshape(4, NODES, NODES * NODES, LANES)

        def stiff_z(t, carry):
            planes = pl.ds(1 - t // 2, NODES - 1)
            values, weight = z0_strip.at[t, planes], flux_zv[0].at[t, planes]
            result = strip.at[t, planes]
            off_face = node != 7 * lax.rem(t, 2)
            for u in range(NODES - 1):
                strips = [(u, pl.ds(k, 8, stride=8)) for k in range(NODES)]
                out = stiff(read(values, strips), [weight[u, k] for k in range(NODES)])
                out = [a + r for a, r in zip(read(result, strips), out)]
                out[0], out[7] = sum_z(out[0], out[7], off_face)
                write(result, strips, out)
            return carry

        lax.fori_loop(0, 4, stiff_z, 0)
        for ey in range(2):
            for j in range(1 - ey, NODES - ey):
                both = target[0, ey, 7, j] + target[1, ey, 0, j]
                target[0, ey, 7, j] = both
                target[1, ey, 0, j] = both
        for ex in range(2):
            for i in range(1 - ex, NODES - ex):
                both = target[ex, 0, i, 7] + target[ex, 1, i, 0]
                target[ex, 0, i, 7] = both
                target[ex, 1, i, 0] = both

    lax.fori_loop(0, 8, invert, 0)

    lax.fori_loop(0, SOURCES, begin, 0)

    await_all(DIAG, send_sem.at[DIAG])
    collect(DIAG)
    for ex in range(2):
        for ey in range(2):
            for n in range(NODES):
                for at in ((ex, ey, 7 * ex, n), (ex, ey, n, 7 * ey)):
                    inverse[at] = 1.0 / fields[(DIAG,) + at]

    face_v = views(z_face)[0]
    face_strip = z_face.reshape(4, NODES, NODES * NODES, LANES)
    face_flat = z_face.reshape(4, NODES**3, LANES)
    flux_flat = flux.reshape(4, NODES**3, LANES)
    coef_xv = views(coef_x)[0]
    coef_yv = views(coef_y)[0]

    def correct(s, carry):
        await_all(s, send_sem.at[s])
        collect(s)
        for ex in range(2):
            for ey in range(2):
                for n in range(NODES):
                    for at in ((ex, ey, 7 * ex, n), (ex, ey, n, 7 * ey)):
                        z_face[at] = fields[(s,) + at] * inverse[at]
        target = fields.at[IMAGE + s]
        image_v = views(target)[0]
        image_strip = target.reshape(4, NODES, NODES * NODES, LANES)
        image_flat = target.reshape(4, NODES**3, LANES)

        def faces(t, carry):
            i0 = 7 * (t // 2)
            j0 = 7 * lax.rem(t, 2)
            nodes = range(NODES)
            values = [face_v[t, i, j0] for i in nodes]
            weight = [flux_v[0][t, i, j0] for i in nodes]
            result = stiff(values, weight)
            result = [r + w * v for r, w, v in zip(result, weight, values)]
            result_y = stiff([face_v[t, i0, j] for j in nodes], [flux_v[0][t, i0, j] for j in nodes])
            strips = [(t, i0, pl.ds(k, 8, stride=8)) for k in nodes]
            result_z = stiff(read(face_strip, strips), [flux_zv[0][t, i0, k] for k in nodes])
            columns = [(t, pl.ds(j0 * 8 + k, 8, stride=64)) for k in nodes]
            values = [jnp.where(node == i0, 0.0, v) for v in read(face_flat, columns)]
            result_c = stiff(values, read(flux_flat, columns))
            for at, r in zip(strips, result_z):
                image_strip[at] = image_strip[at] + r
            for at, r in zip(columns, result_c):
                image_flat[at] = image_flat[at] + r
            for i, r in zip(nodes, result):
                image_v[t, i, j0] = image_v[t, i, j0] + r
            for j, r in zip(nodes, result_y):
                image_v[t, i0, j] = image_v[t, i0, j] + r
            ends_x = [jnp.where(j0 == j, 0.0, face_v[t, i0, j]) for j in nodes]
            ends_y = [jnp.where(i0 == i, 0.0, face_v[t, i, j0]) for i in nodes]
            for i in nodes:
                for j in nodes:
                    more = coef_xv[t, i, j] * ends_x[j] + coef_yv[t, i, j] * ends_y[i]
                    image_v[t, i, j] = image_v[t, i, j] + more
            return carry

        lax.fori_loop(0, 4, faces, 0)
        for ey in range(2):
            both = target[0, ey, 7, 7 * ey] + target[1, ey, 0, 7 * ey]
            target[0, ey, 7, 7 * ey] = both
            target[1, ey, 0, 7 * ey] = both
        for ex in range(2):
            both = target[ex, 0, 7 * ex, 7] + target[ex, 1, 7 * ex, 0]
            target[ex, 0, 7 * ex, 7] = both
            target[ex, 1, 7 * ex, 0] = both
        ends = []
        for t in range(4):
            i0, j0 = 7 * (t // 2), 7 * (t % 2)
            strips = [(t, i0, pl.ds(k, 8, stride=8)) for k in (0, 7)]
            columns = [(t, pl.ds(j0 * 8 + k, 8, stride=64)) for k in (0, 7)]
            ends.append((image_strip, strips, read(image_strip, strips)))
            ends.append((image_flat, columns, read(image_flat, columns)))
        for ref, at, (first, last) in ends:
            write(ref, at, sum_z(first, last))
        send(IMAGE + s)
        return carry

    lax.fori_loop(0, SOURCES, correct, 0)

    twice_z = ((node == 0) & (lane > 0)) | ((node == 7) & (lane < LANES - 1))
    share_z = jnp.where(twice_z, jnp.float32(0.5), jnp.float32(1.0))

    def share(g, carry):
        for line in lines_y(g):
            write(weighted_v[1], line, [v * share_z for v in read(inverse_v[1], line)])
        return carry

    lax.fori_loop(0, 8, share, 0)

    def part_of(there):
        return 0.5 if there is None else jnp.where(there, 0.5, 1.0).astype(jnp.float32)

    for there, ex, i in [(has_down, 0, 0), (None, 0, 7), (None, 1, 0), (has_up, 1, 7)]:
        for ey in range(2):
            weighted[ex, ey, i] = weighted[ex, ey, i] * part_of(there)
    for there, ey, j in [(has_left, 0, 0), (None, 0, 7), (None, 1, 0), (has_right, 1, 7)]:
        for ex in range(2):
            weighted[ex, ey, :, j] = weighted[ex, ey, :, j] * part_of(there)

    zero = jnp.zeros((8, LANES), jnp.float32)

    def settle(s, carry):
        await_all(IMAGE + s, send_sem.at[IMAGE + s])
        finish_z(s)
        collect(IMAGE + s)
        right_v = views(fields.at[s])[1]
        image_v = views(fields.at[IMAGE + s])[1]

        def products(g, carry):
            terms = [[], [], []]
            for line in lines_y(g):
                for at in line:
                    r, v, w = right_v[at], image_v[at], weighted_v[1][at]
                    rw = r * w
                    terms[0].append(r * rw)
                    terms[1].append(v * rw)
                    terms[2].append(v * (v * w))
            return tuple(c + tree_sum(t) for c, t in zip(carry, terms))

        totals = lax.fori_loop(0, 8, products, (zero, zero, zero))
        for n, total in enumerate(totals):
            sums[pl.ds(n * SOURCES + s, 1), :] = jnp.sum(total, axis=0, keepdims=True)
        return carry

    lax.fori_loop(0, SOURCES, settle, 0)

    def gather(stage, slots, mine, count, at, target):
        slots[at] = mine[...]
        copies = [
            pltpu.make_async_remote_copy(
                mine,
                slots.at[at],
                sum_send.at[stage],
                sum_recv.at[stage],
                device_id=target(lax.rem(at + step, count)),
                device_id_type=MESH,
            )
            for step in range(1, count)
        ]
        for copy in copies:
            copy.start()
        others = slots.at[pl.ds(0, count - 1)]
        pltpu.make_async_copy(others, others, sum_recv.at[stage]).wait()
        return tree_sum([slots[n] for n in range(count)]), others

    total = jnp.sum(sums[...], axis=1, keepdims=True)
    node16 = lax.broadcasted_iota(jnp.int32, (16, LANES), 0)
    lane16 = lax.broadcasted_iota(jnp.int32, (16, LANES), 1)
    packed = jnp.where(node16 == lane16, jnp.broadcast_to(total, (16, LANES)), 0.0)
    part[0:1, :] = jnp.sum(packed, axis=0, keepdims=True)
    total, sent = gather(0, gather_row, part.at[0:1], N_ROW, row, lambda r: (r, col))
    part[1:2, :] = total
    total, sent_too = gather(1, gather_col, part.at[1:2], N_COL, col, lambda c: (row, c))
    pltpu.make_async_copy(sent, sent, sum_send.at[0]).wait()
    pltpu.make_async_copy(sent_too, sent_too, sum_send.at[1]).wait()
    total = jnp.broadcast_to(total, (16, LANES))
    total = jnp.sum(jnp.where(node16 == lane16, total, 0.0), axis=1, keepdims=True)
    rz_first, curvature, square = total[0:4], total[4:8], total[8:12]
    alpha = rz_first / curvature
    rz_second = alpha * alpha * square - rz_first
    beta = rz_second / rz_first
    scalars[0:4, :] = jnp.broadcast_to(alpha, (4, LANES))
    scalars[4:8, :] = jnp.broadcast_to(beta, (4, LANES))


SLOTS = 8


def update_kernel(fields, inverse, scalars, first, second, third, staging, sem):
    outputs = (first, second, third)

    def copies(n):
        return [
            pltpu.make_async_copy(
                staging.at[n % SLOTS, q], outputs[q].at[n // NODES, n % NODES], sem.at[n % SLOTS]
            )
            for q in range(3)
        ]

    def await_slot(slot):
        pltpu.make_async_copy(staging.at[slot], staging.at[slot], sem.at[slot]).wait()

    def step(n, carry):
        s, i, slot = n // NODES, n % NODES, n % SLOTS

        @pl.when(n >= SLOTS)
        def _():
            await_slot(slot)

        alpha = jnp.broadcast_to(scalars[pl.ds(s, 1), :], (8, LANES))
        beta = jnp.broadcast_to(scalars[pl.ds(s + 4, 1), :], (8, LANES))
        for ex in range(2):
            for ey in range(2):
                lanes = pl.ds((ex * 2 + ey) * LANES, LANES)
                for j in range(NODES):
                    right = fields[s, ex, ey, i, j]
                    inv = inverse[ex, ey, i, j]
                    rest = right - alpha * fields[IMAGE + s, ex, ey, i, j]
                    staging[slot, 0, j, :, lanes] = alpha * (right * inv)
                    staging[slot, 1, j, :, lanes] = rest
                    staging[slot, 2, j, :, lanes] = (rest + beta * right) * inv
        for copy in copies(n):
            copy.start()
        return carry

    steps = SOURCES * NODES
    lax.fori_loop(0, steps, step, 0)
    for n in range(steps - SLOTS, steps):
        await_slot(n % SLOTS)


def per_device(loads, conduct):
    f32 = jnp.float32
    vmem = pltpu.VMEM
    whole = pl.BlockSpec(memory_space=vmem)
    results = pl.pallas_call(
        solve_kernel,
        out_shape=[vmem((FIELDS,) + FIELD, f32), vmem(FIELD, f32), vmem((8, LANES), f32)],
        in_specs=[pl.BlockSpec(memory_space=pl.ANY)] * 2,
        out_specs=[whole] * 3,
        scratch_shapes=[vmem(FIELD, f32)] * 3
        + [vmem((SOURCES,) + FIELD, f32)]
        + [vmem(FIELD, f32)] * 4
        + [
            vmem((FIELDS, 2, 2, NODES, NODES, LANES), f32),
            vmem((FIELDS, 2, 2, NODES, NODES, LANES), f32),
            vmem((FIELDS, 4, NODES, LANES), f32),
            vmem((16, LANES), f32),
            vmem((8, LANES), f32),
            vmem((N_ROW, 1, LANES), f32),
            vmem((N_COL, 1, LANES), f32),
            pltpu.SemaphoreType.DMA((SOURCES + 1,)),
            pltpu.SemaphoreType.DMA((FIELDS,)),
            pltpu.SemaphoreType.DMA((FIELDS,)),
            pltpu.SemaphoreType.DMA((2,)),
            pltpu.SemaphoreType.DMA((2,)),
        ],
        compiler_params=pltpu.CompilerParams(
            collective_id=0, has_side_effects=True, vmem_limit_bytes=40 * 1024 * 1024
        ),
    )(*[pltpu.with_memory_space_constraint(x, pltpu.HBM) for x in (loads, conduct)])
    shape = (SOURCES, NODES, NODES, NODES, 4 * LANES)
    return pl.pallas_call(
        update_kernel,
        out_shape=[jax.ShapeDtypeStruct(shape, f32)] * 3,
        in_specs=[whole] * 3,
        out_specs=[pl.BlockSpec(memory_space=pl.ANY)] * 3,
        scratch_shapes=[
            vmem((SLOTS, 3, NODES, NODES, 4 * LANES), f32),
            pltpu.SemaphoreType.DMA((SLOTS,)),
        ],
        compiler_params=pltpu.CompilerParams(vmem_limit_bytes=16 * 1024 * 1024),
    )(*[pltpu.with_memory_space_constraint(x, vmem) for x in results])


def solution(mesh):
    in_specs = (P(None, None, None, None, ("row", "col")), P(None, None, None, ("row", "col")))
    out = P(None, None, None, None, ("row", "col"))
    return jax.shard_map(
        per_device, mesh=mesh, in_specs=in_specs, out_specs=(out, out, out), check_vma=False
    )
```

```python
import functools

import jax
import jax.numpy as jnp
import numpy as np
from jax import lax
from jax.experimental import pallas as pl
from jax.experimental.pallas import tpu as pltpu
from jax.sharding import PartitionSpec as P

NODES = 8
SOURCES = 4
LANES = 128
N_ROW = 8
N_COL = 16
SCREENING = 0.5
GLL_INNER = [
    -0.8717401485096066,
    -0.5917001814331423,
    -0.2092992179024789,
    0.2092992179024789,
    0.5917001814331423,
    0.8717401485096066,
]
MESH = pl.DeviceIdType.MESH
FIELD = (2, 2, NODES, NODES, NODES, LANES)


def gll_tables():
    degree = NODES - 1
    points = np.array([-1.0] + GLL_INNER + [1.0])
    previous = points * 0.0 + 1.0
    current = points * 1.0
    for order in range(1, degree):
        following = ((2 * order + 1) * points * current - order * previous) / (order + 1)
        previous = current
        current = following
    weights = 2.0 / (degree * (degree + 1) * current**2)
    spread = points[:, None] - points[None, :]
    index_ids = np.arange(NODES)
    same = index_ids[:, None] == index_ids[None, :]
    safe_spread = np.where(same, 1.0, spread)
    deriv = np.where(same, 0.0, current[:, None] / (current[None, :] * safe_spread))
    corner = degree * (degree + 1) / 4.0
    ends = np.where(index_ids == 0, -corner, np.where(index_ids == degree, corner, 0.0))
    deriv = deriv + np.where(same, ends[None, :], 0.0)
    return deriv, weights


DERIV, WEIGHTS = gll_tables()
SQUARE = DERIV * DERIV
HALF = NODES // 2


def halves(table):
    mirrored = table[:HALF, ::-1][:, :HALF]
    direct = table[:HALF, :HALF]
    plus = (direct + mirrored) / 2.0
    minus = (direct - mirrored) / 2.0
    return plus.tolist(), minus.tolist()


SLOPE = DERIV * np.sqrt(2.0)
D_PLUS, D_MINUS = halves(SLOPE)
Q_PLUS, Q_MINUS = halves(SQUARE * 2.0)


def fold(values):
    plus = [values[i] + values[7 - i] for i in range(HALF)]
    minus = [values[i] - values[7 - i] for i in range(HALF)]
    return plus, minus


def combine(table, values, transposed):
    out = []
    for a in range(HALF):
        total = None
        for i in range(HALF):
            factor = table[i][a] if transposed else table[a][i]
            term = values[i] * factor
            total = term if total is None else total + term
        out.append(total)
    return out


def unfold(base, turn):
    low = [base[a] + turn[a] for a in range(HALF)]
    high = [base[a] - turn[a] for a in range(HALF)]
    return low + high[::-1]


def derive(values):
    plus, minus = fold(values)
    return unfold(combine(D_MINUS, minus, False), combine(D_PLUS, plus, False))


def derive_back(values):
    plus, minus = fold(values)
    return unfold(combine(D_PLUS, minus, True), combine(D_MINUS, plus, True))


def square_back(values):
    plus, minus = fold(values)
    return unfold(combine(Q_PLUS, plus, True), combine(Q_MINUS, minus, True))


def tree_sum(terms):
    while len(terms) > 1:
        terms = [a + b for a, b in zip(terms[::2], terms[1::2])]
    return terms[0]


def lines_x(t):
    return [[(t, i, j) for i in range(NODES)] for j in range(NODES)]


def lines_y(g):
    return [[(g, u, j) for j in range(NODES)] for u in range(4)]


def lines_z(g):
    return [[(g, u, pl.ds(k, 8, stride=8)) for k in range(NODES)] for u in range(4)]


def views(ref):
    along_x = ref.reshape(4, NODES, NODES, NODES, LANES)
    along_y = ref.reshape(8, 4, NODES, NODES, LANES)
    along_z = ref.reshape(8, 4, NODES * NODES, LANES)
    return along_x, along_y, along_z


def read(ref, line):
    return [ref[at] for at in line]


def write(ref, line, values):
    for at, value in zip(line, values):
        ref[at] = value


def sum_z(first, last, rows=True):
    lane = lax.broadcasted_iota(jnp.int32, (8, LANES), 1)
    after = jnp.where((lane < LANES - 1) & rows, pltpu.roll(first, LANES - 1, 1), 0.0)
    before = jnp.where((lane > 0) & rows, pltpu.roll(last, 1, 1), 0.0)
    return first + before, last + after


def assemble_inside(ref):
    for ey in range(2):
        for j in range(NODES):
            both = ref[0, ey, 7, j] + ref[1, ey, 0, j]
            ref[0, ey, 7, j] = both
            ref[1, ey, 0, j] = both
    for ex in range(2):
        for i in range(NODES):
            both = ref[ex, 0, i, 7] + ref[ex, 1, i, 0]
            ref[ex, 0, i, 7] = both
            ref[ex, 1, i, 0] = both
    strips = views(ref)[2]

    def along_z(g, carry):
        lines = [line for u in range(4) for line in lines_z(g * 4 + u)]
        ends = [(strips[line[0]], strips[line[7]]) for line in lines]
        ends = [sum_z(first, last) for first, last in ends]
        for line, (first, last) in zip(lines, ends):
            strips[line[0]] = first
            strips[line[7]] = last
        return carry

    lax.fori_loop(0, 2, along_z, 0)


DIAG = SOURCES
IMAGE = SOURCES + 1
FIELDS = 2 * SOURCES + 1


def solve_kernel(
    loads,
    conduct,
    fields,
    inverse,
    scalars,
    flux,
    flux_z,
    part_z,
    z0,
    z_face,
    coef_x,
    coef_y,
    weighted,
    from_x,
    from_y,
    from_edge,
    sums,
    part,
    gather_row,
    gather_col,
    in_sem,
    send_sem,
    recv_sem,
    sum_send,
    sum_recv,
):
    row = lax.axis_index("row")
    col = lax.axis_index("col")
    for ex in range(2):
        for ey in range(2):
            lanes = pl.ds((ex * 2 + ey) * LANES, LANES)
            pltpu.make_async_copy(
                conduct.at[:, :, :, lanes], flux.at[ex, ey], in_sem.at[SOURCES]
            ).start()
    for s in range(SOURCES):
        for ex in range(2):
            for ey in range(2):
                lanes = pl.ds((ex * 2 + ey) * LANES, LANES)
                pltpu.make_async_copy(
                    loads.at[s, :, :, :, lanes], fields.at[s, ex, ey], in_sem.at[s]
                ).start()

    has_up, has_down = row < N_ROW - 1, row > 0
    has_right, has_left = col < N_COL - 1, col > 0
    ways = [
        (1, 0, has_up),
        (-1, 0, has_down),
        (0, 1, has_right),
        (0, -1, has_left),
        (1, 1, has_up & has_right),
        (1, -1, has_up & has_left),
        (-1, 1, has_down & has_right),
        (-1, -1, has_down & has_left),
    ]
    sides_x = has_up.astype(jnp.int32) + has_down.astype(jnp.int32)
    sides_y = has_right.astype(jnp.int32) + has_left.astype(jnp.int32)
    barrier = pltpu.get_barrier_semaphore()
    corners = 0
    for dr, dc, there in ways[4:]:

        @pl.when(there)
        def _():
            pl.semaphore_signal(barrier, 1, device_id=(row + dr, col + dc), device_id_type=MESH)

        corners = corners + there.astype(jnp.int32)
    for step in range(1, N_COL):
        pl.semaphore_signal(
            barrier, 1, device_id=(row, lax.rem(col + step, N_COL)), device_id_type=MESH
        )
    for step in range(1, N_ROW):
        pl.semaphore_signal(
            barrier, 1, device_id=(lax.rem(row + step, N_ROW), col), device_id_type=MESH
        )

    def transfers(q):
        ref = fields.at[q]
        rest = pl.ds(1, NODES - 1)
        pieces = [
            (2, ref.at[0, 1, :, 7], from_y.at[q, 0, 0]),
            (2, ref.at[1, 1, rest, 7], from_y.at[q, 0, 1, rest]),
            (3, ref.at[0, 0, :, 0], from_y.at[q, 1, 0]),
            (3, ref.at[1, 0, rest, 0], from_y.at[q, 1, 1, rest]),
            (4, ref.at[1, 1, 7, 7], from_edge.at[q, 0]),
            (5, ref.at[1, 0, 7, 0], from_edge.at[q, 1]),
            (6, ref.at[0, 1, 0, 7], from_edge.at[q, 2]),
            (7, ref.at[0, 0, 0, 0], from_edge.at[q, 3]),
            (0, ref.at[1, :, 7], from_x.at[q, 0]),
            (1, ref.at[0, :, 0], from_x.at[q, 1]),
        ]
        return [
            (
                way,
                pltpu.make_async_remote_copy(
                    src,
                    dst,
                    send_sem.at[q],
                    recv_sem.at[q],
                    device_id=(row + ways[way][0], col + ways[way][1]),
                    device_id_type=MESH,
                ),
            )
            for way, src, dst in pieces
        ]

    def send(q):
        for way, copy in transfers(q):
            pl.when(ways[way][2])(copy.start)

    def await_all(q, sem):
        tiles = fields.at[q].reshape(4 * NODES * NODES, NODES, LANES)
        for across in (1, 2):
            for along in (1, 2):

                @pl.when((sides_x == across) & (sides_y == along))
                def _():
                    size = tiles.at[pl.ds(0, 16 * across + 15 * along + across * along)]
                    pltpu.make_async_copy(size, size, sem).wait()

    def collect(q):
        await_all(q, recv_sem.at[q])
        ref = fields.at[q]
        for ey in range(2):
            for j in range(NODES):
                ref[0, ey, 0, j] = ref[0, ey, 0, j] + from_x[q, 0, ey, j]
                ref[1, ey, 7, j] = ref[1, ey, 7, j] + from_x[q, 1, ey, j]
        for ex in range(2):
            for i in range(NODES):
                at = (0, 7) if (ex, i) == (1, 0) else (ex, i)
                ref[ex, 0, i, 0] = ref[ex, 0, i, 0] + from_y[(q, 0) + at]
                ref[ex, 1, i, 7] = ref[ex, 1, i, 7] + from_y[(q, 1) + at]
        for corner in range(4):
            ex, ey = corner // 2, corner % 2
            at = (ex, ey, 7 * ex, 7 * ey)
            ref[at] = ref[at] + from_edge[q, corner]

    def clear(ref, there, pick):
        @pl.when(jnp.logical_not(there))
        def _():
            def body(q, carry):
                target = pick(ref, q)
                target[...] = jnp.zeros_like(target)
                return carry

            lax.fori_loop(0, FIELDS, body, 0)

    clear(from_x, has_down, lambda ref, q: ref.at[q, 0])
    clear(from_x, has_up, lambda ref, q: ref.at[q, 1])
    clear(from_y, has_left, lambda ref, q: ref.at[q, 0])
    clear(from_y, has_right, lambda ref, q: ref.at[q, 1])
    clear(from_edge, has_down & has_left, lambda ref, q: ref.at[q, 0])
    clear(from_edge, has_down & has_right, lambda ref, q: ref.at[q, 1])
    clear(from_edge, has_up & has_left, lambda ref, q: ref.at[q, 2])
    clear(from_edge, has_up & has_right, lambda ref, q: ref.at[q, 3])
    sums[...] = jnp.zeros_like(sums)

    flux_v = views(flux)
    flux_zv = views(flux_z)
    part_v = views(part_z)
    weighted_v = views(weighted)
    inverse_v = views(inverse)
    diag_v = views(fields.at[DIAG])

    pltpu.make_async_copy(flux, flux, in_sem.at[SOURCES]).wait()
    node = lax.broadcasted_iota(jnp.int32, (8, LANES), 0)
    lane = lax.broadcasted_iota(jnp.int32, (8, LANES), 1)
    weight_z = jnp.full((8, LANES), WEIGHTS[3], jnp.float32)
    for k in (0, 1, 2):
        ends = (node == k) | (node == 7 - k)
        weight_z = jnp.where(ends, jnp.float32(WEIGHTS[k]), weight_z)

    def diag_x(t, carry):
        for j, line in enumerate(lines_x(t)):
            values = [
                v * (weight_z * float(SCREENING * WEIGHTS[i] * WEIGHTS[j]))
                for i, v in enumerate(read(flux_v[0], line))
            ]
            write(flux_v[0], line, values)
            write(diag_v[0], line, [r + v for r, v in zip(square_back(values), values)])
        return carry

    def diag_yz(g, carry):
        for line, strip in zip(lines_y(g), lines_z(g)):
            before = read(diag_v[1], line)
            result_y = square_back(read(flux_v[1], line))
            values = read(flux_v[2], strip)
            write(flux_zv[1], line, values)
            write(part_v[2], strip, square_back(values))
            write(diag_v[1], line, [b + r for b, r in zip(before, result_y)])
        return carry

    def diag_sum(g, carry):
        for line in lines_y(g):
            both = zip(read(diag_v[1], line), read(part_v[1], line))
            write(diag_v[1], line, [b + r for b, r in both])
        return carry

    lax.fori_loop(0, 4, diag_x, 0)
    lax.fori_loop(0, 8, diag_yz, 0)
    lax.fori_loop(0, 8, diag_sum, 0)

    for side in range(2):
        end = 7 * side

        def lean(other, carry):
            for n in range(NODES):
                weight = [flux[side, other, a, n] for a in range(NODES)]
                result = derive_back([w * float(SLOPE[a, end]) for a, w in enumerate(weight)])
                result[end] = result[end] + weight[end]
                for i in range(NODES):
                    coef_x[side, other, i, n] = result[i]
                weight = [flux[other, side, n, b] for b in range(NODES)]
                result = derive_back([w * float(SLOPE[b, end]) for b, w in enumerate(weight)])
                for j in range(NODES):
                    coef_y[other, side, n, j] = result[j]
            return carry

        lax.fori_loop(0, 2, lean, 0)

    def prepare(n, carry):
        q = lax.rem(n + DIAG, DIAG + 1)

        @pl.when(n > 0)
        def _():
            pltpu.make_async_copy(fields.at[q], fields.at[q], in_sem.at[q]).wait()

        assemble_inside(fields.at[q])

        @pl.when(n == 0)
        def _():
            pl.semaphore_wait(barrier, N_ROW - 1 + N_COL - 1 + corners)

        send(q)
        return carry

    lax.fori_loop(0, DIAG + 1, prepare, 0)

    def invert(g, carry):
        for line in lines_y(g):
            write(inverse_v[1], line, [1.0 / v for v in read(diag_v[1], line)])
        return carry


    def stiff(values, weight):
        return derive_back([g * w for g, w in zip(derive(values), weight)])

    empty = jnp.zeros((8, LANES), jnp.float32)

    def inside_part(s):
        right_v = views(fields.at[s])
        z0_v = views(z0.at[s])

        def scale(g, carry):
            for line in lines_y(g):
                both = zip(read(right_v[1], line), read(inverse_v[1], line))
                write(z0_v[1], line, [v * d for v, d in both])
            return carry

        lax.fori_loop(0, 8, scale, 0)
        for ex in range(2):
            for ey in range(2):
                for n in range(NODES):
                    z0[s, ex, ey, 7 * ex, n] = empty
                    z0[s, ex, ey, n, 7 * ey] = empty

    def begin(s, carry):
        inside_part(s)
        z0_v = views(z0.at[s])
        image_v = views(fields.at[IMAGE + s])

        def stiff_x(t, carry):
            end = lax.rem(t, 2)
            lines = pl.ds(1 - end, NODES - 1)
            values, weight = z0_v[0].at[t, :, lines], flux_v[0].at[t, :, lines]
            result = image_v[0].at[t, :, lines]
            for n in range(NODES - 1):
                line = [(i, n) for i in range(NODES)]
                v, w = read(values, line), read(weight, line)
                out = stiff(v, w)
                write(result, line, [r + b * a for r, b, a in zip(out, w, v)])
            for i in range(NODES):
                image_v[0][t, i, 7 * end] = empty
            return carry

        def stiff_y(t, carry):
            planes = pl.ds(1 - t // 2, NODES - 1)
            values, weight = z0_v[0].at[t, planes], flux_v[0].at[t, planes]
            result = image_v[0].at[t, planes]
            for u in range(NODES - 1):
                line = [(u, j) for j in range(NODES)]
                out = stiff(read(values, line), read(weight, line))
                write(result, line, [a + r for a, r in zip(read(result, line), out)])
            return carry

        lax.fori_loop(0, 4, stiff_x, 0)
        lax.fori_loop(0, 4, stiff_y, 0)
        return carry

    def finish_z(s):
        z0_strip = z0.at[s].reshape(4, NODES, NODES * NODES, LANES)
        target = fields.at[IMAGE + s]
        strip = target.reshape(4, NODES, NODES * NODES, LANES)

        def stiff_z(t, carry):
            planes = pl.ds(1 - t // 2, NODES - 1)
            values, weight = z0_strip.at[t, planes], flux_zv[0].at[t, planes]
            result = strip.at[t, planes]
            off_face = node != 7 * lax.rem(t, 2)
            for u in range(NODES - 1):
                strips = [(u, pl.ds(k, 8, stride=8)) for k in range(NODES)]
                out = stiff(read(values, strips), [weight[u, k] for k in range(NODES)])
                out = [a + r for a, r in zip(read(result, strips), out)]
                out[0], out[7] = sum_z(out[0], out[7], off_face)
                write(result, strips, out)
            return carry

        lax.fori_loop(0, 4, stiff_z, 0)
        for ey in range(2):
            for j in range(1 - ey, NODES - ey):
                both = target[0, ey, 7, j] + target[1, ey, 0, j]
                target[0, ey, 7, j] = both
                target[1, ey, 0, j] = both
        for ex in range(2):
            for i in range(1 - ex, NODES - ex):
                both = target[ex, 0, i, 7] + target[ex, 1, i, 0]
                target[ex, 0, i, 7] = both
                target[ex, 1, i, 0] = both

    lax.fori_loop(0, 8, invert, 0)

    lax.fori_loop(0, SOURCES, begin, 0)

    await_all(DIAG, send_sem.at[DIAG])
    collect(DIAG)
    for ex in range(2):
        for ey in range(2):
            for n in range(NODES):
                for at in ((ex, ey, 7 * ex, n), (ex, ey, n, 7 * ey)):
                    inverse[at] = 1.0 / fields[(DIAG,) + at]

    face_v = views(z_face)[0]
    face_strip = z_face.reshape(4, NODES, NODES * NODES, LANES)
    face_flat = z_face.reshape(4, NODES**3, LANES)
    flux_flat = flux.reshape(4, NODES**3, LANES)
    coef_xv = views(coef_x)[0]
    coef_yv = views(coef_y)[0]

    def correct(s, carry):
        await_all(s, send_sem.at[s])
        collect(s)
        for ex in range(2):
            for ey in range(2):
                for n in range(NODES):
                    for at in ((ex, ey, 7 * ex, n), (ex, ey, n, 7 * ey)):
                        z_face[at] = fields[(s,) + at] * inverse[at]
        target = fields.at[IMAGE + s]
        image_v = views(target)[0]
        image_strip = target.reshape(4, NODES, NODES * NODES, LANES)
        image_flat = target.reshape(4, NODES**3, LANES)

        def faces(t, carry):
            i0 = 7 * (t // 2)
            j0 = 7 * lax.rem(t, 2)
            nodes = range(NODES)
            values = [face_v[t, i, j0] for i in nodes]
            weight = [flux_v[0][t, i, j0] for i in nodes]
            result = stiff(values, weight)
            result = [r + w * v for r, w, v in zip(result, weight, values)]
            result_y = stiff([face_v[t, i0, j] for j in nodes], [flux_v[0][t, i0, j] for j in nodes])
            strips = [(t, i0, pl.ds(k, 8, stride=8)) for k in nodes]
            result_z = stiff(read(face_strip, strips), [flux_zv[0][t, i0, k] for k in nodes])
            columns = [(t, pl.ds(j0 * 8 + k, 8, stride=64)) for k in nodes]
            values = [jnp.where(node == i0, 0.0, v) for v in read(face_flat, columns)]
            result_c = stiff(values, read(flux_flat, columns))
            for at, r in zip(strips, result_z):
                image_strip[at] = image_strip[at] + r
            for at, r in zip(columns, result_c):
                image_flat[at] = image_flat[at] + r
            for i, r in zip(nodes, result):
                image_v[t, i, j0] = image_v[t, i, j0] + r
            for j, r in zip(nodes, result_y):
                image_v[t, i0, j] = image_v[t, i0, j] + r
            ends_x = [jnp.where(j0 == j, 0.0, face_v[t, i0, j]) for j in nodes]
            ends_y = [jnp.where(i0 == i, 0.0, face_v[t, i, j0]) for i in nodes]
            for i in nodes:
                for j in nodes:
                    more = coef_xv[t, i, j] * ends_x[j] + coef_yv[t, i, j] * ends_y[i]
                    image_v[t, i, j] = image_v[t, i, j] + more
            return carry

        lax.fori_loop(0, 4, faces, 0)
        for ey in range(2):
            both = target[0, ey, 7, 7 * ey] + target[1, ey, 0, 7 * ey]
            target[0, ey, 7, 7 * ey] = both
            target[1, ey, 0, 7 * ey] = both
        for ex in range(2):
            both = target[ex, 0, 7 * ex, 7] + target[ex, 1, 7 * ex, 0]
            target[ex, 0, 7 * ex, 7] = both
            target[ex, 1, 7 * ex, 0] = both
        ends = []
        for t in range(4):
            i0, j0 = 7 * (t // 2), 7 * (t % 2)
            strips = [(t, i0, pl.ds(k, 8, stride=8)) for k in (0, 7)]
            columns = [(t, pl.ds(j0 * 8 + k, 8, stride=64)) for k in (0, 7)]
            ends.append((image_strip, strips, read(image_strip, strips)))
            ends.append((image_flat, columns, read(image_flat, columns)))
        for ref, at, (first, last) in ends:
            write(ref, at, sum_z(first, last))
        send(IMAGE + s)
        return carry

    lax.fori_loop(0, SOURCES, correct, 0)

    twice_z = ((node == 0) & (lane > 0)) | ((node == 7) & (lane < LANES - 1))
    share_z = jnp.where(twice_z, jnp.float32(0.5), jnp.float32(1.0))

    def share(g, carry):
        for line in lines_y(g):
            write(weighted_v[1], line, [v * share_z for v in read(inverse_v[1], line)])
        return carry

    lax.fori_loop(0, 8, share, 0)

    def part_of(there):
        return 0.5 if there is None else jnp.where(there, 0.5, 1.0).astype(jnp.float32)

    for there, ex, i in [(has_down, 0, 0), (None, 0, 7), (None, 1, 0), (has_up, 1, 7)]:
        for ey in range(2):
            weighted[ex, ey, i] = weighted[ex, ey, i] * part_of(there)
    for there, ey, j in [(has_left, 0, 0), (None, 0, 7), (None, 1, 0), (has_right, 1, 7)]:
        for ex in range(2):
            weighted[ex, ey, :, j] = weighted[ex, ey, :, j] * part_of(there)

    zero = jnp.zeros((8, LANES), jnp.float32)

    def complete(s, carry):
        await_all(IMAGE + s, send_sem.at[IMAGE + s])
        finish_z(s)
        return carry

    lax.fori_loop(0, SOURCES, complete, 0)

    def settle(s, carry):
        collect(IMAGE + s)
        right_v = views(fields.at[s])[1]
        image_v = views(fields.at[IMAGE + s])[1]

        def products(g, carry):
            terms = [[], [], []]
            for line in lines_y(g):
                for at in line:
                    r, v, w = right_v[at], image_v[at], weighted_v[1][at]
                    rw = r * w
                    terms[0].append(r * rw)
                    terms[1].append(v * rw)
                    terms[2].append(v * (v * w))
            return tuple(c + tree_sum(t) for c, t in zip(carry, terms))

        totals = lax.fori_loop(0, 8, products, (zero, zero, zero))
        for n, total in enumerate(totals):
            sums[pl.ds(n * SOURCES + s, 1), :] = jnp.sum(total, axis=0, keepdims=True)
        return carry

    lax.fori_loop(0, SOURCES, settle, 0)

    def gather(stage, slots, mine, count, at, target):
        slots[at] = mine[...]
        copies = [
            pltpu.make_async_remote_copy(
                mine,
                slots.at[at],
                sum_send.at[stage],
                sum_recv.at[stage],
                device_id=target(lax.rem(at + step, count)),
                device_id_type=MESH,
            )
            for step in range(1, count)
        ]
        for copy in copies:
            copy.start()
        others = slots.at[pl.ds(0, count - 1)]
        pltpu.make_async_copy(others, others, sum_recv.at[stage]).wait()
        return tree_sum([slots[n] for n in range(count)]), others

    total = jnp.sum(sums[...], axis=1, keepdims=True)
    node16 = lax.broadcasted_iota(jnp.int32, (16, LANES), 0)
    lane16 = lax.broadcasted_iota(jnp.int32, (16, LANES), 1)
    packed = jnp.where(node16 == lane16, jnp.broadcast_to(total, (16, LANES)), 0.0)
    part[0:1, :] = jnp.sum(packed, axis=0, keepdims=True)
    total, sent = gather(0, gather_row, part.at[0:1], N_ROW, row, lambda r: (r, col))
    part[1:2, :] = total
    total, sent_too = gather(1, gather_col, part.at[1:2], N_COL, col, lambda c: (row, c))
    pltpu.make_async_copy(sent, sent, sum_send.at[0]).wait()
    pltpu.make_async_copy(sent_too, sent_too, sum_send.at[1]).wait()
    total = jnp.broadcast_to(total, (16, LANES))
    total = jnp.sum(jnp.where(node16 == lane16, total, 0.0), axis=1, keepdims=True)
    rz_first, curvature, square = total[0:4], total[4:8], total[8:12]
    alpha = rz_first / curvature
    rz_second = alpha * alpha * square - rz_first
    beta = rz_second / rz_first
    scalars[0:4, :] = jnp.broadcast_to(alpha, (4, LANES))
    scalars[4:8, :] = jnp.broadcast_to(beta, (4, LANES))


SLOTS = 8


def update_kernel(fields, inverse, scalars, first, second, third, staging, sem):
    outputs = (first, second, third)

    def copies(n):
        return [
            pltpu.make_async_copy(
                staging.at[n % SLOTS, q], outputs[q].at[n // NODES, n % NODES], sem.at[n % SLOTS]
            )
            for q in range(3)
        ]

    def await_slot(slot):
        pltpu.make_async_copy(staging.at[slot], staging.at[slot], sem.at[slot]).wait()

    def step(n, carry):
        s, i, slot = n // NODES, n % NODES, n % SLOTS

        @pl.when(n >= SLOTS)
        def _():
            await_slot(slot)

        alpha = jnp.broadcast_to(scalars[pl.ds(s, 1), :], (8, LANES))
        beta = jnp.broadcast_to(scalars[pl.ds(s + 4, 1), :], (8, LANES))
        for ex in range(2):
            for ey in range(2):
                lanes = pl.ds((ex * 2 + ey) * LANES, LANES)
                for j in range(NODES):
                    right = fields[s, ex, ey, i, j]
                    inv = inverse[ex, ey, i, j]
                    rest = right - alpha * fields[IMAGE + s, ex, ey, i, j]
                    staging[slot, 0, j, :, lanes] = alpha * (right * inv)
                    staging[slot, 1, j, :, lanes] = rest
                    staging[slot, 2, j, :, lanes] = (rest + beta * right) * inv
        for copy in copies(n):
            copy.start()
        return carry

    steps = SOURCES * NODES
    lax.fori_loop(0, steps, step, 0)
    for n in range(steps - SLOTS, steps):
        await_slot(n % SLOTS)


def per_device(loads, conduct):
    f32 = jnp.float32
    vmem = pltpu.VMEM
    whole = pl.BlockSpec(memory_space=vmem)
    results = pl.pallas_call(
        solve_kernel,
        out_shape=[vmem((FIELDS,) + FIELD, f32), vmem(FIELD, f32), vmem((8, LANES), f32)],
        in_specs=[pl.BlockSpec(memory_space=pl.ANY)] * 2,
        out_specs=[whole] * 3,
        scratch_shapes=[vmem(FIELD, f32)] * 3
        + [vmem((SOURCES,) + FIELD, f32)]
        + [vmem(FIELD, f32)] * 4
        + [
            vmem((FIELDS, 2, 2, NODES, NODES, LANES), f32),
            vmem((FIELDS, 2, 2, NODES, NODES, LANES), f32),
            vmem((FIELDS, 4, NODES, LANES), f32),
            vmem((16, LANES), f32),
            vmem((8, LANES), f32),
            vmem((N_ROW, 1, LANES), f32),
            vmem((N_COL, 1, LANES), f32),
            pltpu.SemaphoreType.DMA((SOURCES + 1,)),
            pltpu.SemaphoreType.DMA((FIELDS,)),
            pltpu.SemaphoreType.DMA((FIELDS,)),
            pltpu.SemaphoreType.DMA((2,)),
            pltpu.SemaphoreType.DMA((2,)),
        ],
        compiler_params=pltpu.CompilerParams(
            collective_id=0, has_side_effects=True, vmem_limit_bytes=40 * 1024 * 1024
        ),
    )(*[pltpu.with_memory_space_constraint(x, pltpu.HBM) for x in (loads, conduct)])
    shape = (SOURCES, NODES, NODES, NODES, 4 * LANES)
    return pl.pallas_call(
        update_kernel,
        out_shape=[jax.ShapeDtypeStruct(shape, f32)] * 3,
        in_specs=[whole] * 3,
        out_specs=[pl.BlockSpec(memory_space=pl.ANY)] * 3,
        scratch_shapes=[
            vmem((SLOTS, 3, NODES, NODES, 4 * LANES), f32),
            pltpu.SemaphoreType.DMA((SLOTS,)),
        ],
        compiler_params=pltpu.CompilerParams(vmem_limit_bytes=16 * 1024 * 1024),
    )(*[pltpu.with_memory_space_constraint(x, vmem) for x in results])


def solution(mesh):
    in_specs = (P(None, None, None, None, ("row", "col")), P(None, None, None, ("row", "col")))
    out = P(None, None, None, None, ("row", "col"))
    return jax.shard_map(
        per_device, mesh=mesh, in_specs=in_specs, out_specs=(out, out, out), check_vma=False
    )
```
